32 devices in a mesh: section: 2 (over core), group: 4 (over z), member: 4 (over y, x).
Axes of the slice: x: 2, y: 2, z: 4, core: 2. Of those that a mesh axis runs over, the one named last changes fastest.
Arguments:
- tokens: bfloat16 [65536, 384], P(('group', 'member')), may hold values from -6 to 6
- segment: int32 [65536], P(('group', 'member')), may hold values from -1 to 5, as said below
- cotangent: bfloat16 [65536, 384], P(('group', 'member')), may hold values from -6 to 6
- attn_gain: float32 [2, 384], P('section'), may hold values from 0.1 to 1.9
- attn_shift: float32 [2, 384], P('section'), may hold values from -3 to 3
- qkv_weight: bfloat16 [2, 384, 1152], P('section'), may hold values from -0.3125 to 0.3125
- qv_bias: float32 [2, 768], P('section'), may hold values from -3 to 3
- proj_weight: bfloat16 [2, 384, 384], P('section'), may hold values from -2.5 to 2.5
- proj_bias: float32 [2, 384], P('section'), may hold values from -3 to 3
- mlp_gain: float32 [2, 384], P('section'), may hold values from 0.1 to 1.9
- mlp_shift: float32 [2, 384], P('section'), may hold values from -3 to 3
- fc1_weight: bfloat16 [2, 384, 1536], P('section'), may hold values from -0.3125 to 0.3125
- fc1_bias: float32 [2, 1536], P('section'), may hold values from -3 to 3
- fc2_weight: bfloat16 [2, 1536, 384], P('section'), may hold values from -0.15625 to 0.15625
- fc2_bias: float32 [2, 384], P('section'), may hold values from -3 to 3
Outputs:
- activations: bfloat16 [2, 65536, 384], P('section', ('group', 'member'))
- in_grads: float32 [2, 65536, 384], P('section', ('group', 'member'))
- grad_attn_gain: float32 [2, 384], P('section', 'member')
- grad_attn_shift: float32 [2, 384], P('section', 'member')
- grad_qkv_weight: float32 [2, 384, 1152], P('section', 'member')
- grad_qv_bias: float32 [2, 768], P('section', 'member')
- grad_proj_weight: float32 [2, 384, 384], P('section', 'member')
- grad_proj_bias: float32 [2, 384], P('section', 'member')
- grad_mlp_gain: float32 [2, 384], P('section', 'member')
- grad_mlp_shift: float32 [2, 384], P('section', 'member')
- grad_fc1_weight: float32 [2, 384, 1536], P('section', 'member')
- grad_fc1_bias: float32 [2, 1536], P('section', 'member')
- grad_fc2_weight: float32 [2, 1536, 384], P('section', 'member')
- grad_fc2_bias: float32 [2, 384], P('section', 'member')
The draws below stay inside these ranges and needn't reach their ends.
Inputs may be any that keep to these rules, and one draw needn't show every extreme that they name: Sequences are consecutive runs of 256 rows. Even-numbered sequences hold one global crop: segment 0 on their first 197 rows, -1 after. Odd-numbered ones hold 4 to 6 local crops of 37 rows each, numbered 0, 1, ... in order, then -1 on the remaining rows.
All inputs are finite; a program needn't handle non-finite values.
Results may differ from the reference program's by a relative error of at most 0.017.
Values may be sent and summed in bfloat16 or wider, within the bound.
A program may use at most 384 MiB of HBM per device.

```python
import jax
import jax.numpy as jnp
from jax import lax

D = 384
H = 6
HD = 64
FF = 1536
S = 256
GLOBAL_LEN = 197
LOCAL_LEN = 37
SEQ_MB = 2
TOKENS = 65536


def draw_segment(key, part):
    key = jax.random.fold_in(key, 7)
    sequences = TOKENS // S
    most_crops = S // LOCAL_LEN
    counts = jax.random.randint(key, (sequences,), 4, most_crops + 1)
    counts = counts.at[1].set(most_crops)
    slot_ids = jnp.arange(S)
    crop_index = slot_ids // LOCAL_LEN
    local_rows = jnp.where(crop_index[None, :] < counts[:, None], crop_index[None, :], -1)
    global_rows = jnp.where(slot_ids < GLOBAL_LEN, 0, -1)
    parity = jnp.arange(sequences) % 2
    segment_ids = jnp.where(parity[:, None] == 0, global_rows[None, :], local_rows)
    return segment_ids.reshape(-1).astype(jnp.int32)


def spiked(entries, stream_key, source, target, parts, factor):
    owner, partner = [(jnp.arange(entries.shape[position]) // (entries.shape[position] // parts)).reshape([-1 if axis == position else 1 for axis in range(entries.ndim)]) for position in (source, target)]
    chosen = jax.random.permutation(stream_key, parts)[partner]
    strong = (owner == chosen) | (owner == (partner + parts // 2) % parts)
    return jnp.where(strong, factor * entries, entries)


def steps_of(key, extent, pieces, low, top_value):
    level, own = 1.0, jax.random.fold_in(key, 6)
    for dim, shards_of in pieces:
        steps = jnp.exp(jax.random.uniform(jax.random.fold_in(own, dim), (shards_of,), jnp.float32, low / len(pieces), top_value / len(pieces)))
        level = level * jnp.repeat(steps, extent[dim] // shards_of).reshape([-1 if axis == dim else 1 for axis in range(len(extent))])
    return level


def bell_draw(own_key, extent, scale, limit, shards=(), held_as=jnp.bfloat16):
    drawn = jax.random.normal(own_key, extent, jnp.float32) * scale
    if len(shards) > 0:
        drawn = steps_of(own_key, extent, shards, -0.22, 0.18) * drawn
    return jnp.clip(drawn, min=-limit, max=limit).astype(held_as)


def noise_with(own_key, shape, scale, reach, shards, heavy, held_as=jnp.bfloat16):
    result = scale * jax.random.normal(own_key, shape, jnp.float32)
    if shards:
        result = result * steps_of(own_key, shape, shards, -0.22, 0.18)
    return jnp.clip(spiked(result, jax.random.fold_in(own_key, 3), *heavy), -reach, reach).astype(held_as)


def setup_inputs(seed: int = 0) -> dict:
    keys = jax.random.split(jax.random.key(seed), 16)
    tokens = bell_draw(keys[0], (TOKENS, D), 1.0, 6.0, ((0, 16),))
    segment = draw_segment(jax.random.fold_in(keys[15], 71), 0)
    cotangent = noise_with(keys[2], (TOKENS, D), 1.0, 6.0, ((0, 16),), (0, 1, 16, 2.0))
    attn_gain = jnp.clip(1.0 + 0.18 * jax.random.normal(keys[3], (2, D), jnp.float32), 0.1, 1.9)
    attn_shift = bell_draw(keys[4], (2, D), 0.5, 3.0, ((0, 2),), jnp.float32)
    qkv_weight = bell_draw(keys[5], (2, D, 3 * D), D ** -0.5, 0.3125, ((0, 2),))
    qv_bias = bell_draw(keys[6], (2, 2 * D), 0.5, 3.0, ((0, 2),), jnp.float32)
    proj_weight = bell_draw(keys[7], (2, D, D), (max(D // 64, 1)) ** -0.5, 2.5, ((0, 2),))
    proj_bias = bell_draw(keys[8], (2, D), 0.5, 3.0, ((0, 2),), jnp.float32)
    mlp_gain = jnp.clip(1.0 + 0.18 * jax.random.normal(keys[9], (2, D), jnp.float32), 0.1, 1.9)
    mlp_shift = bell_draw(keys[10], (2, D), 0.5, 3.0, ((0, 2),), jnp.float32)
    fc1_weight = bell_draw(keys[11], (2, D, FF), D ** -0.5, 0.3125, ((0, 2),))
    fc1_bias = bell_draw(keys[12], (2, FF), 0.5, 3.0, ((0, 2),), jnp.float32)
    fc2_weight = bell_draw(keys[13], (2, FF, D), FF ** -0.5, 0.15625, ((0, 2),))
    fc2_bias = bell_draw(keys[14], (2, D), 0.5, 3.0, ((0, 2),), jnp.float32)
    return dict(tokens=tokens, segment=segment, cotangent=cotangent, attn_gain=attn_gain, attn_shift=attn_shift, qkv_weight=qkv_weight, qv_bias=qv_bias, proj_weight=proj_weight, proj_bias=proj_bias, mlp_gain=mlp_gain, mlp_shift=mlp_shift, fc1_weight=fc1_weight, fc1_bias=fc1_bias, fc2_weight=fc2_weight, fc2_bias=fc2_bias)


norm_eps = 1e-06

@jax.custom_vjp
def low(v):
    return lax.optimization_barrier(v.astype(jnp.bfloat16)).astype(jnp.float32)

@jax.custom_vjp
def low_back(v):
    return v

def low_keep(v):
    return (low(v), None)

def low_pass(kept, grad):
    return (grad,)

def back_keep(v):
    return (v, None)

def back_low(kept, grad):
    return (low(grad),)
low.defvjp(low_keep, low_pass)
low_back.defvjp(back_keep, back_low)

def mat_prod(left, right):
    return jnp.dot(left, right, precision=lax.Precision.HIGHEST, preferred_element_type=jnp.float32)

def normalize(values, gain, shift):
    average = lax.optimization_barrier(jnp.mean(values, axis=-1, keepdims=True))
    centered = values - average
    spread_sq = lax.optimization_barrier(jnp.mean(centered * centered, axis=-1, keepdims=True))
    return centered * lax.rsqrt(spread_sq + norm_eps) * gain + shift

def attend_block(operands):
    queries, key_rows, value_rows, segment_ids = operands
    raw = low_back(jnp.einsum('bqhd,bkhd->bhqk', queries, key_rows, precision=lax.Precision.HIGHEST))
    same = segment_ids[:, :, None] == segment_ids[:, None, :]
    allowed = same & (segment_ids[:, None, :] >= 0) | jnp.eye(S, dtype=bool)[None]
    scores = jnp.where(allowed[:, None], raw * HD ** (-0.5), -1e+30)
    weights = low(jax.nn.softmax(scores, axis=-1))
    return jnp.einsum('bhqk,bkhd->bqhd', weights, value_rows, precision=lax.Precision.HIGHEST)

def vit_layer(hidden, params, segment):
    attn_gain, attn_shift, qkv_weight, qv_bias, proj_weight, proj_bias, mlp_gain, mlp_shift, fc1_weight, fc1_bias, fc2_weight, fc2_bias = params
    width = hidden.shape[1]
    per_block = SEQ_MB
    blocks = hidden.shape[0] // (per_block * S)
    normed = low(normalize(hidden, attn_gain, attn_shift))
    key_zeros = jnp.zeros((width,), hidden.dtype)
    bias_full = jnp.concatenate([qv_bias[:width], key_zeros, qv_bias[width:]])
    mixed = low_back(low(mat_prod(normed, qkv_weight) + bias_full))
    shaped = mixed.reshape(blocks, per_block, S, 3, H, HD)
    segment_ids = segment.reshape(blocks, per_block, S)
    attended = lax.map(jax.checkpoint(attend_block), (shaped[:, :, :, 0], shaped[:, :, :, 1], shaped[:, :, :, 2], segment_ids))
    context = low_back(low(attended.reshape(-1, width)))
    after = hidden + low_back(mat_prod(context, proj_weight) + proj_bias)
    normed_two = low(normalize(after, mlp_gain, mlp_shift))
    before = low_back(mat_prod(normed_two, fc1_weight) + fc1_bias)
    active = low(jax.nn.gelu(before, approximate=False))
    return after + low_back(mat_prod(active, fc2_weight) + fc2_bias)

def reference(tokens, segment, cotangent, attn_gain, attn_shift, qkv_weight, qv_bias, proj_weight, proj_bias, mlp_gain, mlp_shift, fc1_weight, fc1_bias, fc2_weight, fc2_bias):
    stacked = (attn_gain, attn_shift, qkv_weight, qv_bias, proj_weight, proj_bias, mlp_gain, mlp_shift, fc1_weight, fc1_bias, fc2_weight, fc2_bias)
    first_params = tuple((item[0].astype(jnp.float32) for item in stacked))
    second_params = tuple((item[1].astype(jnp.float32) for item in stacked))
    begin_rows = tokens.astype(jnp.float32)
    middle_nudge = jnp.zeros_like(begin_rows)

    def forward(begin, first_set, second_set, shift_in):
        first_out = low(vit_layer(begin, first_set, segment))
        middle = low_back(first_out + shift_in)
        return (vit_layer(middle, second_set, segment), first_out)
    result_top, pullback, first_out = jax.vjp(forward, begin_rows, first_params, second_params, middle_nudge, has_aux=True)
    grad_begin, grad_first, grad_second, grad_middle = pullback(cotangent.astype(jnp.float32))
    activations = jnp.stack([first_out.astype(jnp.bfloat16), result_top.astype(jnp.bfloat16)])
    in_grads = jnp.stack([grad_begin, grad_middle])
    merged = [jnp.stack([lower_grad, upper_grad]) for lower_grad, upper_grad in zip(grad_first, grad_second)]
    return (activations, in_grads, merged[0], merged[1], merged[2], merged[3], merged[4], merged[5], merged[6], merged[7], merged[8], merged[9], merged[10], merged[11])
```

```python
import jax
import jax.numpy as jnp
from jax import lax
from jax.experimental import pallas as pl
from jax.experimental.pallas import tpu as pltpu
from jax.sharding import PartitionSpec as P

HD = 64
S = 256
HALF = S // 2
GLOBAL_LEN = 197
LOCAL_LEN = 37
PAIR = 2 * HD
STEP = 2 * S
EPS = 1e-06
SCALE = HD ** (-0.5)
LOG2E = 1.4426950408889634
CHUNK = 512
F32 = jnp.float32
BF16 = jnp.bfloat16
MIB = 1 << 20

ATTN_GAIN, ATTN_SHIFT, Q_BIAS, V_BIAS, PROJ_BIAS, MLP_GAIN, MLP_SHIFT, FC2_BIAS, FC1_BIAS = range(9)
VECTORS = 16


def up16(value):
    return -(-value // 16) * 16


def key_windows(local):
    if not local:
        return ((0, up16(GLOBAL_LEN)),) * 2
    first_end = ((HALF - 1) // LOCAL_LEN + 1) * LOCAL_LEN
    second_start = HALF // LOCAL_LEN * LOCAL_LEN // 16 * 16
    return ((0, up16(first_end)), (second_start, up16(S // LOCAL_LEN * LOCAL_LEN)))


WINDOWS = tuple((local, key_windows(local)) for local in (False, True))
PROB_ROWS = sum(hi - lo for _, windows in WINDOWS for lo, hi in windows)


def prob_offset(pair, sequence, block):
    spans = [hi - lo for _, windows in WINDOWS for lo, hi in windows]
    return pair * PROB_ROWS + sum(spans[: 2 * sequence + block])


def nn(left, right):
    return jnp.dot(left, right, preferred_element_type=F32)


def nt(left, right):
    return lax.dot_general(left, right, (((1,), (1,)), ((), ())), preferred_element_type=F32)


def tn(left, right):
    return lax.dot_general(left, right, (((0,), (0,)), ((), ())), preferred_element_type=F32)


def column_sums(values):
    return jnp.sum(values.reshape(values.shape[0] // 8, 8, values.shape[1]), axis=0)


def normalized(values):
    centered = values - jnp.mean(values, axis=1, keepdims=True)
    inverse = lax.rsqrt(jnp.mean(centered * centered, axis=1, keepdims=True) + EPS)
    return centered * inverse, inverse


def norm_back(scaled, inverse, gain, grad):
    grad_scaled = grad * gain
    first = jnp.mean(grad_scaled, axis=1, keepdims=True)
    second = jnp.mean(grad_scaled * scaled, axis=1, keepdims=True)
    return inverse * (grad_scaled - first - scaled * second)


def crop_of(index):
    total = jnp.zeros_like(index)
    for crop in range(1, S // LOCAL_LEN + 1):
        total = total + (index >= crop * LOCAL_LEN).astype(jnp.int32)
    return total


def mask_bias(local, block, lo, hi):
    if not local:
        rows = lax.broadcasted_iota(jnp.int32, (hi - lo, HALF), 0) + lo
        return jnp.where(rows < GLOBAL_LEN, 0.0, -1e30)
    keys = crop_of(lax.broadcasted_iota(jnp.int32, (hi - lo, HALF), 0) + lo)
    queries = crop_of(lax.broadcasted_iota(jnp.int32, (hi - lo, HALF), 1) + block * HALF)
    return jnp.where(keys == queries, 0.0, -1e30)


def split_pair(rows):
    lane = lax.broadcasted_iota(jnp.int32, (1, PAIR), 1)
    first = (lane < HD).astype(rows.dtype)
    second = (lane >= HD).astype(rows.dtype)
    return jnp.concatenate([rows * first, rows * second], axis=0)


def padded(rows, lo, hi):
    parts = [rows]
    if lo:
        parts = [jnp.zeros((lo, rows.shape[1]), rows.dtype)] + parts
    if hi < S:
        parts = parts + [jnp.zeros((S - hi, rows.shape[1]), rows.dtype)]
    return jnp.concatenate(parts, axis=0) if len(parts) > 1 else rows


def diagonal(values):
    return jnp.concatenate([values[:HD, :HALF], values[HD:, HALF:]], axis=0)


def attend(seg, qkv, prob, ctx_t, width):
    for sequence, (local, windows) in enumerate(WINDOWS):
        base = sequence * S
        valid = seg[0:1, base : base + S] >= 0
        biases = [mask_bias(local, block, lo, hi) for block, (lo, hi) in enumerate(windows)]
        for pair in range(width // PAIR):
            left = pair * PAIR
            queries = qkv[base : base + S, left : left + PAIR]
            keys = qkv[base : base + S, width + left : width + left + PAIR]
            values_t = qkv[base : base + S, 2 * width + left : 2 * width + left + PAIR].T
            for block, (lo, hi) in enumerate(windows):
                at = block * HALF
                valid_here = valid[:, at : at + HALF]
                raw = nt(keys[lo:hi], split_pair(queries[at : at + HALF]))
                bias = biases[block]
                scores = raw * (SCALE * LOG2E) + jnp.concatenate([bias, bias], axis=1)
                exponent = jnp.exp2(scores - jnp.max(scores, axis=0, keepdims=True))
                total = jnp.sum(exponent, axis=0, keepdims=True)
                inverse = jnp.where(jnp.concatenate([valid_here, valid_here], axis=1), 1.0 / total, 0.0)
                probs = (exponent * inverse).astype(BF16)
                offset = prob_offset(pair, sequence, block)
                prob[offset : offset + hi - lo, :] = probs
                context = diagonal(nn(values_t, padded(probs, lo, hi)))
                own = values_t[:, at : at + HALF].astype(F32)
                ctx_t[left : left + PAIR, base + at : base + at + HALF] = jnp.where(
                    valid_here, context, own
                ).astype(BF16)


def attend_back(seg, qkv, prob, grad_context, grad_qkv, width):
    for sequence, (local, windows) in enumerate(WINDOWS):
        base = sequence * S
        valid = (seg[0:1, base : base + S] >= 0).astype(jnp.int32)
        count = jnp.sum(valid, axis=1, keepdims=True)
        padding = lax.broadcasted_iota(jnp.int32, (S, PAIR), 0) >= count
        for pair in range(width // PAIR):
            left = pair * PAIR
            queries = qkv[base : base + S, left : left + PAIR]
            keys = qkv[base : base + S, width + left : width + left + PAIR]
            values = qkv[base : base + S, 2 * width + left : 2 * width + left + PAIR]
            grads = grad_context[base : base + S, left : left + PAIR]
            keys_t = keys.T
            grad_values = jnp.where(padding, grads.astype(F32), 0.0)
            grad_keys = jnp.zeros((S, PAIR), F32)
            for block, (lo, hi) in enumerate(windows):
                at = block * HALF
                grads_here = split_pair(grads[at : at + HALF])
                offset = prob_offset(pair, sequence, block)
                probs_low = prob[offset : offset + hi - lo, :]
                probs = probs_low.astype(F32)
                product = probs * nt(values[lo:hi], grads_here)
                inner = jnp.sum(product, axis=0, keepdims=True)
                grad_raw = (product - probs * inner).astype(BF16)
                grad_values = grad_values + padded(nn(probs_low, grads_here), lo, hi)
                grad_keys = grad_keys + padded(
                    nn(grad_raw, split_pair(queries[at : at + HALF])), lo, hi
                )
                grad_queries = diagonal(nn(keys_t, padded(grad_raw, lo, hi))) * SCALE
                grad_qkv[base + at : base + at + HALF, left : left + PAIR] = grad_queries.astype(
                    BF16
                ).T
            grad_qkv[base : base + S, width + left : width + left + PAIR] = (
                grad_keys * SCALE
            ).astype(BF16)
            grad_qkv[base : base + S, 2 * width + left : 2 * width + left + PAIR] = (
                grad_values.astype(BF16)
            )


def vector(vec, row, count=1):
    parts = [vec[0, row + i : row + i + 1, :] for i in range(count)]
    return parts[0] if count == 1 else jnp.concatenate(parts, axis=1)


def forward(x, seg, weights, kept, y):
    vec, w_qkv, w_proj, w_fc1, w_fc2 = weights
    xhat1, r1, qkv, prob, ctx_t, xhat2, r2, act, dgelu = kept
    rows, width = x.shape
    hidden = w_fc1.shape[2]
    for top in range(0, rows, S):
        here = slice(top, top + S)
        scaled, inverse = normalized(x[here, :].astype(F32))
        xhat1[here, :] = scaled.astype(BF16)
        r1[here, :] = inverse
        normed = (scaled * vector(vec, ATTN_GAIN) + vector(vec, ATTN_SHIFT)).astype(BF16)
        for part, bias in ((0, Q_BIAS), (1, None), (2, V_BIAS)):
            mixed = nn(normed, w_qkv[0, :, part * width : (part + 1) * width])
            if bias is not None:
                mixed = mixed + vector(vec, bias)
            qkv[here, part * width : (part + 1) * width] = mixed.astype(BF16)
    attend(seg, qkv, prob, ctx_t, width)
    for top in range(0, rows, S):
        here = slice(top, top + S)
        after = (
            x[here, :].astype(F32) + tn(ctx_t[:, here], w_proj[0]) + vector(vec, PROJ_BIAS)
        )
        scaled, inverse = normalized(after)
        xhat2[here, :] = scaled.astype(BF16)
        r2[here, :] = inverse
        normed = (scaled * vector(vec, MLP_GAIN) + vector(vec, MLP_SHIFT)).astype(BF16)
        output = after + vector(vec, FC2_BIAS)
        for left in range(0, hidden, CHUNK):
            cols = slice(left, left + CHUNK)
            bias = jnp.concatenate(
                [vec[0, FC1_BIAS + i : FC1_BIAS + i + 1, :] for i in range(hidden // width)], axis=1
            )[:, cols]
            pre = nn(normed, w_fc1[0, :, cols]) + bias
            phi_sum = 0.5 + 0.5 * lax.erf(pre * (0.5**0.5))
            density = jnp.exp2(pre * pre * (-0.5 * LOG2E)) * (1.0 / (2.0 * jnp.pi) ** 0.5)
            active = (pre * phi_sum).astype(BF16)
            act[here, cols] = active
            dgelu[here, cols] = (phi_sum + pre * density).astype(BF16)
            output = output + nn(active, w_fc2[0, cols, :])
        y[here, :] = output.astype(BF16)


def backward(dout, seg, weights, kept, sums, grad_context, grad_qkv, write):
    vec, w_qkv, w_proj, w_fc1, w_fc2 = weights
    xhat1, r1, qkv, prob, ctx_t, xhat2, r2, act, dgelu = kept
    sum_qkv, sum_proj, sum_fc1, sum_fc2, sum_vec = sums
    rows, width = dout.shape
    hidden = w_fc1.shape[2]

    def add(row, values):
        for i in range(values.shape[1] // width):
            at = (row + i) * 8
            sum_vec[at : at + 8, :] += column_sums(values[:, i * width : (i + 1) * width])

    top_grad = dout[...]
    top_wide = top_grad.astype(F32)
    add(FC2_BIAS, top_wide)
    top_t = top_grad.T
    scaled = xhat2[...].astype(F32)
    normed_t = (scaled * vector(vec, MLP_GAIN) + vector(vec, MLP_SHIFT)).astype(BF16).T
    grad_normed = jnp.zeros((rows, width), F32)
    column_parts = []
    for left in range(0, hidden, CHUNK):
        cols = slice(left, left + CHUNK)
        grad_pre = nt(top_grad, w_fc2[0, cols, :]) * dgelu[:, cols].astype(F32)
        column_parts.append(column_sums(grad_pre))
        grad_pre = grad_pre.astype(BF16)
        grad_normed = grad_normed + nt(grad_pre, w_fc1[0, :, cols])
        sum_fc1[:, cols] += nn(normed_t, grad_pre)
        sum_fc2[:, cols] += nn(top_t, act[:, cols])
    columns = jnp.concatenate(column_parts, axis=1)
    for i in range(hidden // width):
        at = (FC1_BIAS + i) * 8
        sum_vec[at : at + 8, :] += columns[:, i * width : (i + 1) * width]
    add(MLP_GAIN, grad_normed * scaled)
    add(MLP_SHIFT, grad_normed)
    grad_after = top_wide + norm_back(scaled, r2[...], vector(vec, MLP_GAIN), grad_normed)
    add(PROJ_BIAS, grad_after)
    grad_branch = grad_after.astype(BF16)
    sum_proj[...] += nn(ctx_t[...], grad_branch)
    grad_context[...] = nt(grad_branch, w_proj[0]).astype(BF16)

    attend_back(seg, qkv, prob, grad_context, grad_qkv, width)

    scaled = xhat1[...].astype(F32)
    normed_t = (scaled * vector(vec, ATTN_GAIN) + vector(vec, ATTN_SHIFT)).astype(BF16).T
    grad_normed = jnp.zeros((rows, width), F32)
    for part, row in ((0, Q_BIAS), (1, None), (2, V_BIAS)):
        cols = slice(part * width, (part + 1) * width)
        piece = grad_qkv[:, cols]
        if row is not None:
            add(row, piece.astype(F32))
        sum_qkv[:, cols] += nn(normed_t, piece)
        grad_normed = grad_normed + nt(piece, w_qkv[0, :, cols])
    add(ATTN_GAIN, grad_normed * scaled)
    add(ATTN_SHIFT, grad_normed)
    write(grad_after + norm_back(scaled, r1[...], vector(vec, ATTN_GAIN), grad_normed))


def write_sums(sums, members, grad_mlp, grad_attn, grad_vec):
    sum_qkv, sum_proj, sum_fc1, sum_fc2, sum_vec = sums
    width, hidden = sum_fc1.shape
    share = width // members
    parts = hidden // width
    for member in range(members):
        rows = slice(member * share, (member + 1) * share)
        for part in range(parts):
            at = (member * parts + part) * share
            grad_mlp[0, at : at + share, :] = sum_fc1[rows, part * width : (part + 1) * width].astype(BF16)
        pieces = (
            (0, 0, sum_proj[rows, :]),
            (0, 1, sum_qkv[rows, :width]),
            (1, 0, sum_qkv[rows, width : 2 * width]),
            (1, 1, sum_qkv[rows, 2 * width :]),
        )
        for half, slot, piece in pieces:
            at = (member * 2 + slot) * share
            grad_attn[half, at : at + share, :] = piece.astype(BF16)
    for part in range(parts):
        cols = slice(part * width, (part + 1) * width)
        grad_mlp[1, cols, :] = sum_fc2[:, cols].astype(BF16).T
    grad_vec[...] = jnp.sum(sum_vec[...].reshape(VECTORS, 8, width), axis=1)


def clear(refs):
    for ref in refs:
        ref[...] = jnp.zeros_like(ref)


def kept_shapes(steps, width, hidden):
    return (
        ((steps * STEP, width), BF16, (STEP, width), 0),
        ((steps * STEP, 1), F32, (STEP, 1), 0),
        ((steps * STEP, 3 * width), BF16, (STEP, 3 * width), 0),
        ((steps * PROB_ROWS * (width // PAIR), S), BF16, (PROB_ROWS * (width // PAIR), S), 0),
        ((width, steps * STEP), BF16, (width, STEP), 1),
        ((steps * STEP, width), BF16, (STEP, width), 0),
        ((steps * STEP, 1), F32, (STEP, 1), 0),
        ((steps * STEP, hidden), BF16, (STEP, hidden), 0),
        ((steps * STEP, hidden), BF16, (STEP, hidden), 0),
    )


def spec(block, axis, first=None):
    if axis == 0:
        if first is None:
            return pl.BlockSpec(block, lambda i, s: (i, 0))
        return pl.BlockSpec(block, lambda i, s: (s[0] * first + i, 0))
    if first is None:
        return pl.BlockSpec(block, lambda i, s: (0, i))
    return pl.BlockSpec(block, lambda i, s: (0, s[0] * first + i))


def weight_specs(weights, layer):
    return [
        pl.BlockSpec((1,) + w.shape[1:], lambda i, s: (layer, 0, 0), pipeline_mode=pl.Buffered(1))
        for w in weights
    ]


def sum_scratch(width, hidden):
    return [
        pltpu.VMEM((width, 3 * width), F32),
        pltpu.VMEM((width, width), F32),
        pltpu.VMEM((width, hidden), F32),
        pltpu.VMEM((width, hidden), F32),
        pltpu.VMEM((8 * VECTORS, width), F32),
    ]


def grad_outs(width, hidden):
    shapes = [((2, hidden, width), BF16), ((2, 2 * width, width), BF16), ((VECTORS, width), F32)]
    outs = [jax.ShapeDtypeStruct(shape, dtype) for shape, dtype in shapes]
    specs = [
        pl.BlockSpec(shape, lambda i, s, n=len(shape): (0,) * n, pipeline_mode=pl.Buffered(1))
        for shape, _ in shapes
    ]
    return outs, specs


def kernel_call(body, steps, in_specs, out_specs, out_shape, scratch, name, flops):
    return pl.pallas_call(
        body,
        grid_spec=pltpu.PrefetchScalarGridSpec(
            num_scalar_prefetch=1,
            grid=(steps,),
            in_specs=in_specs,
            out_specs=out_specs,
            scratch_shapes=scratch,
        ),
        out_shape=out_shape,
        compiler_params=pltpu.CompilerParams(vmem_limit_bytes=60 * MIB),
        cost_estimate=pl.CostEstimate(flops=flops, bytes_accessed=30 * MIB, transcendentals=0),
        name=name,
    )


def first_forward(section, x, seg, weights, steps):
    width, hidden = x.shape[1], weights[3].shape[2]
    shapes = kept_shapes(steps, width, hidden)

    def body(s, x, seg, vec, w_qkv, w_proj, w_fc1, w_fc2, y, *kept):
        forward(x, seg, (vec, w_qkv, w_proj, w_fc1, w_fc2), kept, y)

    return kernel_call(
        body,
        steps,
        [spec((STEP, width), 0, steps), spec((1, STEP), 1, steps)] + weight_specs(weights, 0),
        [spec((STEP, width), 0)] + [spec(block, axis) for _, _, block, axis in shapes],
        [jax.ShapeDtypeStruct((steps * STEP, width), BF16)]
        + [jax.ShapeDtypeStruct(shape, dtype) for shape, dtype, _, _ in shapes],
        [],
        "forward_first",
        steps * STEP * 4000000,
    )(section, x, seg, *weights)


def second_layer(section, x, seg, cotangent, weights, steps, members):
    width, hidden = x.shape[1], weights[3].shape[2]
    shapes = kept_shapes(steps, width, hidden)
    outs, specs = grad_outs(width, hidden)

    def body(s, x, seg, cot, vec, w_qkv, w_proj, w_fc1, w_fc2, y, g, g_mlp, g_attn, g_vec, *scratch):
        sums, kept, (grad_context, grad_qkv) = scratch[:5], scratch[5:-2], scratch[-2:]
        weights = (vec, w_qkv, w_proj, w_fc1, w_fc2)
        step = pl.program_id(0)

        @pl.when(step == 0)
        def _():
            clear(sums)

        forward(x, seg, weights, kept, y)

        def write(values):
            g[...] = values.astype(BF16)

        backward(cot, seg, weights, kept, sums, grad_context, grad_qkv, write)

        @pl.when(step == steps - 1)
        def _():
            write_sums(sums, members, g_mlp, g_attn, g_vec)

    rows = jax.ShapeDtypeStruct((steps * STEP, width), BF16)
    return kernel_call(
        body,
        steps,
        [spec((STEP, width), 0), spec((1, STEP), 1, steps), spec((STEP, width), 0, steps)]
        + weight_specs(weights, 1),
        [spec((STEP, width), 0), spec((STEP, width), 0)] + specs,
        [rows, rows] + outs,
        sum_scratch(width, hidden)
        + [pltpu.VMEM(block, dtype) for _, dtype, block, _ in shapes]
        + [pltpu.VMEM((STEP, width), BF16), pltpu.VMEM((STEP, 3 * width), BF16)],
        "second_layer",
        steps * STEP * 12000000,
    )(section, x, seg, cotangent, *weights)


def first_backward(section, seg, dout, kept, weights, steps, members):
    width, hidden = dout.shape[1], weights[3].shape[2]
    shapes = kept_shapes(steps, width, hidden)
    outs, specs = grad_outs(width, hidden)

    def body(s, seg, dout, vec, w_qkv, w_proj, w_fc1, w_fc2, *refs):
        kept, (g, g_mlp, g_attn, g_vec) = refs[:9], refs[9:13]
        sums, (grad_context, grad_qkv) = refs[13:18], refs[18:]
        weights = (vec, w_qkv, w_proj, w_fc1, w_fc2)
        step = pl.program_id(0)

        @pl.when(step == 0)
        def _():
            clear(sums)

        def write(values):
            g[...] = values

        backward(dout, seg, weights, kept, sums, grad_context, grad_qkv, write)

        @pl.when(step == steps - 1)
        def _():
            write_sums(sums, members, g_mlp, g_attn, g_vec)

    return kernel_call(
        body,
        steps,
        [spec((1, STEP), 1, steps), spec((STEP, width), 0)]
        + weight_specs(weights, 0)
        + [spec(block, axis) for _, _, block, axis in shapes],
        [spec((STEP, width), 0)] + specs,
        [jax.ShapeDtypeStruct((steps * STEP, width), F32)] + outs,
        sum_scratch(width, hidden)
        + [pltpu.VMEM((STEP, width), BF16), pltpu.VMEM((STEP, 3 * width), BF16)],
        "backward_first",
        steps * STEP * 8000000,
    )(section, seg, dout, *weights, *kept)


def pack_vectors(vectors, width):
    flat = jnp.concatenate([v.reshape(-1, width) for v in vectors], axis=0)
    return jnp.pad(flat, ((0, VECTORS - flat.shape[0]), (0, 0)))[None]


def local_part(section, tokens, segment, cotangent, weights, steps, members):
    y0, *kept = first_forward(section, tokens, segment, weights, steps)
    y1, g1, *grads1 = second_layer(section, y0, segment, cotangent, weights, steps, members)
    g0, *grads0 = first_backward(section, segment, g1, kept, weights, steps, members)
    return y0, y1, g0, g1, grads0, grads1


def swap(value):
    return lax.ppermute(value, "section", [(0, 1), (1, 0)])


def gather_weights(own, here):
    other = [swap(w) for w in own]
    return [
        jnp.concatenate([jnp.where(here, mine, got), jnp.where(here, got, mine)], axis=0)
        for mine, got in zip(own, other)
    ]


def per_device(
    tokens,
    segment,
    cotangent,
    attn_gain,
    attn_shift,
    qkv_weight,
    qv_bias,
    proj_weight,
    proj_bias,
    mlp_gain,
    mlp_shift,
    fc1_weight,
    fc1_bias,
    fc2_weight,
    fc2_bias,
):
    section = lax.axis_index("section")
    here = section == 0
    members = lax.axis_size("member")
    rows, width = tokens.shape
    steps = rows // 2 // STEP
    vec = pack_vectors(
        (attn_gain, attn_shift, qv_bias, proj_bias, mlp_gain, mlp_shift, fc2_bias, fc1_bias), width
    )
    weights = gather_weights([vec, qkv_weight, proj_weight, fc1_weight, fc2_weight], here)
    y0, y1, g0, g1, grads0, grads1 = local_part(
        section.reshape(1).astype(jnp.int32), tokens, segment.reshape(1, rows), cotangent, weights, steps, members
    )

    def joined(mine, got):
        return jnp.where(here, jnp.concatenate([mine, got]), jnp.concatenate([got, mine]))[None]

    def paired(first, second):
        return joined(jnp.where(here, first, second), swap(jnp.where(here, second, first)))

    activations = paired(y0, y1)
    g0_low = g0.astype(BF16)
    in_grads = joined(
        jnp.where(here, g0, g1.astype(F32)), swap(jnp.where(here, g1, g0_low)).astype(F32)
    )

    def reduced(first, second):
        total = lax.psum_scatter(jnp.stack([first, second]), "section", scatter_dimension=0, tiled=True)
        total = total.reshape(2, members, -1, width)
        total = lax.psum_scatter(total, "member", scatter_dimension=1, tiled=True)
        return lax.psum(total, "group")[:, 0].astype(F32)

    mlp = reduced(grads0[0], grads1[0])
    attn = reduced(grads0[1], grads1[1])
    vectors = lax.psum(
        jnp.where(here, grads0[2] + swap(grads0[2]), grads1[2] + swap(grads1[2])), ("member", "group")
    )
    member = lax.axis_index("member")
    hidden = fc1_weight.shape[2]
    share = width // members
    fc1 = mlp[0].reshape(hidden // width, share, width).transpose(1, 0, 2).reshape(share, hidden)
    proj = attn[0, :share]
    qkv = jnp.concatenate([attn[0, share:], attn[1, :share], attn[1, share:]], axis=1)

    def piece(row, count=1):
        flat = vectors[row : row + count].reshape(-1)
        size = flat.shape[0] // members
        return lax.dynamic_slice(flat, (member * size,), (size,))[None]

    return (
        activations,
        in_grads,
        piece(ATTN_GAIN),
        piece(ATTN_SHIFT),
        qkv[None],
        piece(Q_BIAS, 2),
        proj[None],
        piece(PROJ_BIAS),
        piece(MLP_GAIN),
        piece(MLP_SHIFT),
        fc1[None],
        piece(FC1_BIAS, hidden // width),
        mlp[1][None],
        piece(FC2_BIAS),
    )


def solution(mesh):
    row = P("section", None)
    mat = P("section", None, None)
    tokens = P(("group", "member"), None)
    split = P("section", "member")
    split_mat = P("section", "member", None)
    stacked = P("section", ("group", "member"), None)
    return jax.shard_map(
        per_device,
        mesh=mesh,
        in_specs=(
            tokens, P(("group", "member")), tokens,
            row, row, mat, row, mat, row, row, row, mat, row, mat, row,
        ),
        out_specs=(
            stacked, stacked,
            split, split, split_mat, split, split_mat, split, split, split, split_mat, split, split_mat, split,
        ),
        check_vma=False,
    )
```

```python
import jax
import jax.numpy as jnp
from jax import lax
from jax.experimental import pallas as pl
from jax.experimental.pallas import tpu as pltpu
from jax.sharding import PartitionSpec as P

HD = 64
S = 256
HALF = S // 2
GLOBAL_LEN = 197
LOCAL_LEN = 37
PAIR = 2 * HD
STEP = 2 * S
EPS = 1e-06
SCALE = HD ** (-0.5)
LOG2E = 1.4426950408889634
CHUNK = 512
F32 = jnp.float32
BF16 = jnp.bfloat16
MIB = 1 << 20
MESH = pl.DeviceIdType.MESH

ATTN_GAIN, ATTN_SHIFT, Q_BIAS, V_BIAS, PROJ_BIAS, MLP_GAIN, MLP_SHIFT, FC2_BIAS, FC1_BIAS = range(9)
VECTORS = 16


def up16(value):
    return -(-value // 16) * 16


def key_windows(local):
    if not local:
        return ((0, up16(GLOBAL_LEN)),) * 2
    first_end = ((HALF - 1) // LOCAL_LEN + 1) * LOCAL_LEN
    second_start = HALF // LOCAL_LEN * LOCAL_LEN // 16 * 16
    return ((0, up16(first_end)), (second_start, up16(S // LOCAL_LEN * LOCAL_LEN)))


WINDOWS = tuple((local, key_windows(local)) for local in (False, True))
PROB_ROWS = sum(hi - lo for _, windows in WINDOWS for lo, hi in windows)


def prob_offset(pair, sequence, block):
    spans = [hi - lo for _, windows in WINDOWS for lo, hi in windows]
    return pair * PROB_ROWS + sum(spans[: 2 * sequence + block])


def nn(left, right):
    return jnp.dot(left, right, preferred_element_type=F32)


def nt(left, right):
    return lax.dot_general(left, right, (((1,), (1,)), ((), ())), preferred_element_type=F32)


def tn(left, right):
    return lax.dot_general(left, right, (((0,), (0,)), ((), ())), preferred_element_type=F32)


def column_sums(values):
    return jnp.sum(values.reshape(values.shape[0] // 8, 8, values.shape[1]), axis=0)


def normalized(values):
    centered = values - jnp.mean(values, axis=1, keepdims=True)
    inverse = lax.rsqrt(jnp.mean(centered * centered, axis=1, keepdims=True) + EPS)
    return centered * inverse, inverse


def norm_back(scaled, inverse, gain, grad):
    grad_scaled = grad * gain
    first = jnp.mean(grad_scaled, axis=1, keepdims=True)
    second = jnp.mean(grad_scaled * scaled, axis=1, keepdims=True)
    return inverse * (grad_scaled - first - scaled * second)


def crop_of(index):
    total = jnp.zeros_like(index)
    for crop in range(1, S // LOCAL_LEN + 1):
        total = total + (index >= crop * LOCAL_LEN).astype(jnp.int32)
    return total


def mask_bias(local, block, lo, hi):
    if not local:
        rows = lax.broadcasted_iota(jnp.int32, (hi - lo, HALF), 0) + lo
        return jnp.where(rows < GLOBAL_LEN, 0.0, -1e30)
    keys = crop_of(lax.broadcasted_iota(jnp.int32, (hi - lo, HALF), 0) + lo)
    queries = crop_of(lax.broadcasted_iota(jnp.int32, (hi - lo, HALF), 1) + block * HALF)
    return jnp.where(keys == queries, 0.0, -1e30)


def split_pair(rows):
    lane = lax.broadcasted_iota(jnp.int32, (1, PAIR), 1)
    first = (lane < HD).astype(rows.dtype)
    second = (lane >= HD).astype(rows.dtype)
    return jnp.concatenate([rows * first, rows * second], axis=0)


def padded(rows, lo, hi):
    parts = [rows]
    if lo:
        parts = [jnp.zeros((lo, rows.shape[1]), rows.dtype)] + parts
    if hi < S:
        parts = parts + [jnp.zeros((S - hi, rows.shape[1]), rows.dtype)]
    return jnp.concatenate(parts, axis=0) if len(parts) > 1 else rows


def diagonal(values):
    return jnp.concatenate([values[:HD, :HALF], values[HD:, HALF:]], axis=0)


def attend(seg, qkv, prob, ctx_t, width):
    for sequence, (local, windows) in enumerate(WINDOWS):
        base = sequence * S
        valid = seg[0:1, base : base + S] >= 0
        biases = [mask_bias(local, block, lo, hi) for block, (lo, hi) in enumerate(windows)]
        for pair in range(width // PAIR):
            left = pair * PAIR
            queries = qkv[base : base + S, left : left + PAIR]
            keys = qkv[base : base + S, width + left : width + left + PAIR]
            values_t = qkv[base : base + S, 2 * width + left : 2 * width + left + PAIR].T
            for block, (lo, hi) in enumerate(windows):
                at = block * HALF
                valid_here = valid[:, at : at + HALF]
                raw = nt(keys[lo:hi], split_pair(queries[at : at + HALF]))
                bias = biases[block]
                scores = raw * (SCALE * LOG2E) + jnp.concatenate([bias, bias], axis=1)
                exponent = jnp.exp2(scores - jnp.max(scores, axis=0, keepdims=True))
                total = jnp.sum(exponent, axis=0, keepdims=True)
                inverse = jnp.where(jnp.concatenate([valid_here, valid_here], axis=1), 1.0 / total, 0.0)
                probs = (exponent * inverse).astype(BF16)
                offset = prob_offset(pair, sequence, block)
                prob[offset : offset + hi - lo, :] = probs
                context = diagonal(nn(values_t, padded(probs, lo, hi)))
                own = values_t[:, at : at + HALF].astype(F32)
                ctx_t[left : left + PAIR, base + at : base + at + HALF] = jnp.where(
                    valid_here, context, own
                ).astype(BF16)


def attend_back(seg, qkv, prob, grad_context, grad_qkv, width):
    for sequence, (local, windows) in enumerate(WINDOWS):
        base = sequence * S
        valid = (seg[0:1, base : base + S] >= 0).astype(jnp.int32)
        count = jnp.sum(valid, axis=1, keepdims=True)
        padding = lax.broadcasted_iota(jnp.int32, (S, PAIR), 0) >= count
        for pair in range(width // PAIR):
            left = pair * PAIR
            queries = qkv[base : base + S, left : left + PAIR]
            keys = qkv[base : base + S, width + left : width + left + PAIR]
            values = qkv[base : base + S, 2 * width + left : 2 * width + left + PAIR]
            grads = grad_context[base : base + S, left : left + PAIR]
            keys_t = keys.T
            grad_values = jnp.where(padding, grads.astype(F32), 0.0)
            grad_keys = jnp.zeros((S, PAIR), F32)
            for block, (lo, hi) in enumerate(windows):
                at = block * HALF
                grads_here = split_pair(grads[at : at + HALF])
                offset = prob_offset(pair, sequence, block)
                probs_low = prob[offset : offset + hi - lo, :]
                probs = probs_low.astype(F32)
                product = probs * nt(values[lo:hi], grads_here)
                inner = jnp.sum(product, axis=0, keepdims=True)
                grad_raw = (product - probs * inner).astype(BF16)
                grad_values = grad_values + padded(nn(probs_low, grads_here), lo, hi)
                grad_keys = grad_keys + padded(
                    nn(grad_raw, split_pair(queries[at : at + HALF])), lo, hi
                )
                grad_queries = diagonal(nn(keys_t, padded(grad_raw, lo, hi))) * SCALE
                grad_qkv[base + at : base + at + HALF, left : left + PAIR] = grad_queries.astype(
                    BF16
                ).T
            grad_qkv[base : base + S, width + left : width + left + PAIR] = (
                grad_keys * SCALE
            ).astype(BF16)
            grad_qkv[base : base + S, 2 * width + left : 2 * width + left + PAIR] = (
                grad_values.astype(BF16)
            )


def vector(vec, row, count=1):
    parts = [vec[0, row + i : row + i + 1, :] for i in range(count)]
    return parts[0] if count == 1 else jnp.concatenate(parts, axis=1)


def forward(x, seg, weights, kept, y):
    vec, w_qkv, w_proj, w_fc1, w_fc2 = weights
    xhat1, r1, qkv, prob, ctx_t, xhat2, r2, act, dgelu = kept
    rows, width = x.shape
    hidden = w_fc1.shape[2]
    for top in range(0, rows, S):
        here = slice(top, top + S)
        scaled, inverse = normalized(x[here, :].astype(F32))
        xhat1[here, :] = scaled.astype(BF16)
        r1[here, :] = inverse
        normed = (scaled * vector(vec, ATTN_GAIN) + vector(vec, ATTN_SHIFT)).astype(BF16)
        for part, bias in ((0, Q_BIAS), (1, None), (2, V_BIAS)):
            mixed = nn(normed, w_qkv[0, :, part * width : (part + 1) * width])
            if bias is not None:
                mixed = mixed + vector(vec, bias)
            qkv[here, part * width : (part + 1) * width] = mixed.astype(BF16)
    attend(seg, qkv, prob, ctx_t, width)
    for top in range(0, rows, S):
        here = slice(top, top + S)
        after = (
            x[here, :].astype(F32) + tn(ctx_t[:, here], w_proj[0]) + vector(vec, PROJ_BIAS)
        )
        scaled, inverse = normalized(after)
        xhat2[here, :] = scaled.astype(BF16)
        r2[here, :] = inverse
        normed = (scaled * vector(vec, MLP_GAIN) + vector(vec, MLP_SHIFT)).astype(BF16)
        output = after + vector(vec, FC2_BIAS)
        for left in range(0, hidden, CHUNK):
            cols = slice(left, left + CHUNK)
            bias = jnp.concatenate(
                [vec[0, FC1_BIAS + i : FC1_BIAS + i + 1, :] for i in range(hidden // width)], axis=1
            )[:, cols]
            pre = nn(normed, w_fc1[0, :, cols]) + bias
            phi_sum = 0.5 + 0.5 * lax.erf(pre * (0.5**0.5))
            density = jnp.exp2(pre * pre * (-0.5 * LOG2E)) * (1.0 / (2.0 * jnp.pi) ** 0.5)
            active = (pre * phi_sum).astype(BF16)
            act[here, cols] = active
            dgelu[here, cols] = (phi_sum + pre * density).astype(BF16)
            output = output + nn(active, w_fc2[0, cols, :])
        y[here, :] = output.astype(BF16)


def adder(sum_vec, width):
    def add(row, values):
        for i in range(values.shape[1] // width):
            at = (row + i) * 8
            sum_vec[at : at + 8, :] += column_sums(values[:, i * width : (i + 1) * width])

    return add


def backward_mlp(dout, weights, kept, sums, write):
    vec, _, w_proj, w_fc1, w_fc2 = weights
    ctx_t, xhat2, r2, act, dgelu = kept
    _, sum_proj, sum_fc1, sum_fc2, sum_vec = sums
    rows, width = dout.shape
    hidden = w_fc1.shape[2]
    add = adder(sum_vec, width)
    top_grad = dout[...]
    top_wide = top_grad.astype(F32)
    add(FC2_BIAS, top_wide)
    top_t = top_grad.T
    scaled = xhat2[...].astype(F32)
    normed_t = (scaled * vector(vec, MLP_GAIN) + vector(vec, MLP_SHIFT)).astype(BF16).T
    grad_normed = jnp.zeros((rows, width), F32)
    column_parts = []
    for left in range(0, hidden, CHUNK):
        cols = slice(left, left + CHUNK)
        grad_pre = nt(top_grad, w_fc2[0, cols, :]) * dgelu[:, cols].astype(F32)
        column_parts.append(column_sums(grad_pre))
        grad_pre = grad_pre.astype(BF16)
        grad_normed = grad_normed + nt(grad_pre, w_fc1[0, :, cols])
        sum_fc1[:, cols] += nn(normed_t, grad_pre)
        sum_fc2[:, cols] += nn(top_t, act[:, cols])
    columns = jnp.concatenate(column_parts, axis=1)
    for i in range(hidden // width):
        at = (FC1_BIAS + i) * 8
        sum_vec[at : at + 8, :] += columns[:, i * width : (i + 1) * width]
    add(MLP_GAIN, grad_normed * scaled)
    add(MLP_SHIFT, grad_normed)
    grad_after = top_wide + norm_back(scaled, r2[...], vector(vec, MLP_GAIN), grad_normed)
    add(PROJ_BIAS, grad_after)
    grad_branch = grad_after.astype(BF16)
    sum_proj[...] += nn(ctx_t[...], grad_branch)
    write(grad_after, nt(grad_branch, w_proj[0]).astype(BF16))


def backward_attn(grad_after, grad_context, seg, weights, kept, sums, grad_qkv, write):
    vec, w_qkv, _, _, _ = weights
    xhat1, r1, qkv, prob = kept
    sum_qkv, sum_vec = sums[0], sums[4]
    rows, width = grad_after.shape
    add = adder(sum_vec, width)
    attend_back(seg, qkv, prob, grad_context, grad_qkv, width)
    scaled = xhat1[...].astype(F32)
    normed_t = (scaled * vector(vec, ATTN_GAIN) + vector(vec, ATTN_SHIFT)).astype(BF16).T
    grad_normed = jnp.zeros((rows, width), F32)
    for part, row in ((0, Q_BIAS), (1, None), (2, V_BIAS)):
        cols = slice(part * width, (part + 1) * width)
        piece = grad_qkv[:, cols]
        if row is not None:
            add(row, piece.astype(F32))
        sum_qkv[:, cols] += nn(normed_t, piece)
        grad_normed = grad_normed + nt(piece, w_qkv[0, :, cols])
    add(ATTN_GAIN, grad_normed * scaled)
    add(ATTN_SHIFT, grad_normed)
    write(grad_after[...] + norm_back(scaled, r1[...], vector(vec, ATTN_GAIN), grad_normed))


def half_rows(share):
    return up16(share // 2)


def write_blocks(sums, members, blocks, out):
    sum_qkv, sum_proj, sum_fc1, sum_fc2, _ = sums
    width = sum_proj.shape[0]
    share = width // members
    size = half_rows(share)
    parts = sum_fc1.shape[1] // width

    def store(rows, member, block):
        at = (member * len(blocks) + blocks.index(block)) * size
        out[0, at : at + size, :] = rows[:size]
        out[1, at : at + size, :] = rows[share - size :]

    for block in blocks:
        if block < parts:
            whole = sum_fc1[:, block * width : (block + 1) * width]
        elif block < 2 * parts:
            chunk = block - parts
            whole = sum_fc2[:, chunk * width : (chunk + 1) * width].astype(BF16).T
            for place in range(members):
                row = chunk * members + place
                store(whole[place * share : (place + 1) * share], row // parts, parts + row % parts)
            continue
        elif block == 2 * parts:
            whole = sum_proj[...]
        else:
            part = block - 2 * parts - 1
            whole = sum_qkv[:, part * width : (part + 1) * width]
        whole = whole.astype(BF16)
        for member in range(members):
            store(whole[member * share : (member + 1) * share], member, block)


def vector_sums(sum_vec):
    return jnp.sum(sum_vec[...].reshape(VECTORS, 8, sum_vec.shape[1]), axis=1).astype(BF16)


def clear(refs):
    for ref in refs:
        ref[...] = jnp.zeros_like(ref)


def kept_shapes(steps, width, hidden):
    return (
        ((steps * STEP, width), BF16, (STEP, width), 0),
        ((steps * STEP, 1), F32, (STEP, 1), 0),
        ((steps * STEP, 3 * width), BF16, (STEP, 3 * width), 0),
        ((steps * PROB_ROWS * (width // PAIR), S), BF16, (PROB_ROWS * (width // PAIR), S), 0),
        ((width, steps * STEP), BF16, (width, STEP), 1),
        ((steps * STEP, width), BF16, (STEP, width), 0),
        ((steps * STEP, 1), F32, (STEP, 1), 0),
        ((steps * STEP, hidden), BF16, (STEP, hidden), 0),
        ((steps * STEP, hidden), BF16, (STEP, hidden), 0),
    )


def spec(block, axis, first=None):
    if axis == 0:
        if first is None:
            return pl.BlockSpec(block, lambda i, s: (i, 0))
        return pl.BlockSpec(block, lambda i, s: (s[0] * first + i, 0))
    if first is None:
        return pl.BlockSpec(block, lambda i, s: (0, i))
    return pl.BlockSpec(block, lambda i, s: (0, s[0] * first + i))


def weight_specs(weights, layer):
    return [
        pl.BlockSpec((1,) + w.shape[1:], lambda i, s: (layer, 0, 0), pipeline_mode=pl.Buffered(1))
        for w in weights
    ]


def sum_scratch(width, hidden):
    return [
        pltpu.VMEM((width, 3 * width), F32),
        pltpu.VMEM((width, width), F32),
        pltpu.VMEM((width, hidden), F32),
        pltpu.VMEM((width, hidden), F32),
        pltpu.VMEM((8 * VECTORS, width), F32),
    ]


def kernel_call(body, steps, in_specs, out_specs, out_shape, scratch, name, flops):
    return pl.pallas_call(
        body,
        grid_spec=pltpu.PrefetchScalarGridSpec(
            num_scalar_prefetch=1,
            grid=(steps,),
            in_specs=in_specs,
            out_specs=out_specs,
            scratch_shapes=scratch,
        ),
        out_shape=out_shape,
        compiler_params=pltpu.CompilerParams(vmem_limit_bytes=60 * MIB),
        cost_estimate=pl.CostEstimate(flops=flops, bytes_accessed=30 * MIB, transcendentals=0),
        name=name,
    )


def first_forward(section, x, seg, weights, steps):
    width, hidden = x.shape[1], weights[3].shape[2]
    shapes = kept_shapes(steps, width, hidden)

    def body(s, x, seg, vec, w_qkv, w_proj, w_fc1, w_fc2, y, *kept):
        forward(x, seg, (vec, w_qkv, w_proj, w_fc1, w_fc2), kept, y)

    return kernel_call(
        body,
        steps,
        [spec((STEP, width), 0, steps), spec((1, STEP), 1, steps)] + weight_specs(weights, 0),
        [spec((STEP, width), 0)] + [spec(block, axis) for _, _, block, axis in shapes],
        [jax.ShapeDtypeStruct((steps * STEP, width), BF16)]
        + [jax.ShapeDtypeStruct(shape, dtype) for shape, dtype, _, _ in shapes],
        [],
        "forward_first",
        steps * STEP * 4000000,
    )(section, x, seg, *weights)


def second_layer(section, x, seg, cotangent, weights, steps, members):
    width, hidden = x.shape[1], weights[3].shape[2]
    shapes = kept_shapes(steps, width, hidden)
    blocks = range(2 * (hidden // width) + 4)
    grads = (2, members * len(blocks) * half_rows(width // members), width)

    def body(s, x, seg, cot, vec, w_qkv, w_proj, w_fc1, w_fc2, y_own, y_send, g, g_out, g_vec, *scratch):
        sums, kept, (grad_after, grad_context, grad_qkv, y) = scratch[:5], scratch[5:-4], scratch[-4:]
        weights = (vec, w_qkv, w_proj, w_fc1, w_fc2)
        step = pl.program_id(0)

        @pl.when(step == 0)
        def _():
            clear(sums)

        forward(x, seg, weights, kept, y)
        first = s[0] == 0
        y_own[...] = jnp.where(first, x[...], y[...])
        y_send[...] = jnp.where(first, y[...], x[...])

        def after_mlp(after, context):
            grad_after[...] = after
            grad_context[...] = context

        def after_attn(values):
            g[...] = values.astype(BF16)

        backward_mlp(cot, weights, kept[4:], sums, after_mlp)
        backward_attn(grad_after, grad_context, seg, weights, kept[:4], sums, grad_qkv, after_attn)

        @pl.when(step == steps - 1)
        def _():
            write_blocks(sums, members, blocks, g_out)
            g_vec[...] = vector_sums(sums[4])

    rows = jax.ShapeDtypeStruct((steps * STEP, width), BF16)
    return kernel_call(
        body,
        steps,
        [spec((STEP, width), 0), spec((1, STEP), 1, steps), spec((STEP, width), 0, steps)]
        + weight_specs(weights, 1),
        [spec((STEP, width), 0)] * 3
        + [
            pl.BlockSpec(grads, lambda i, s: (0, 0, 0), pipeline_mode=pl.Buffered(1)),
            pl.BlockSpec((VECTORS, width), lambda i, s: (0, 0), pipeline_mode=pl.Buffered(1)),
        ],
        [rows] * 3
        + [jax.ShapeDtypeStruct(grads, BF16), jax.ShapeDtypeStruct((VECTORS, width), BF16)],
        sum_scratch(width, hidden)
        + [pltpu.VMEM(block, dtype) for _, dtype, block, _ in shapes]
        + [
            pltpu.VMEM((STEP, width), F32),
            pltpu.VMEM((STEP, width), BF16),
            pltpu.VMEM((STEP, 3 * width), BF16),
            pltpu.VMEM((STEP, width), BF16),
        ],
        "second_layer",
        steps * STEP * 12000000,
    )(section, x, seg, cotangent, *weights)


def place():
    return lax.axis_index("section"), lax.axis_index("group"), lax.axis_index("member")


def remote(src, dst, send, recv, device):
    return pltpu.make_async_remote_copy(
        src_ref=src, dst_ref=dst, send_sem=send, recv_sem=recv, device_id=device, device_id_type=MESH
    )


def greet(groups, members):
    section, group, member = place()
    peers = [
        (lax.rem(section + ds, 2), group, lax.rem(member + dm, members))
        for ds in range(2)
        for dm in range(members)
        if ds or dm
    ] + [
        (lax.rem(section + ds, 2), lax.rem(group + dg, groups), member)
        for ds in range(2)
        for dg in range(1, groups)
    ]
    barrier = pltpu.get_barrier_semaphore()
    for peer in peers:
        pl.semaphore_signal(barrier, inc=1, device_id=peer, device_id_type=MESH)
    pl.semaphore_wait(barrier, len(peers))


def rows_at(index, count):
    return pl.ds(pl.multiple_of(index * count, 16), count)


class Reduction:
    def __init__(self, target, groups, members, count, width):
        self.target, self.groups, self.members, self.count, self.width = target, groups, members, count, width
        self.part = up16(-(-count // groups))

    def scratch(self):
        whole = (self.members * self.count, self.width)
        sems = [1, 1, self.members, self.members, self.groups, self.groups, 2 * self.groups, 2 * self.groups]
        return [
            pltpu.VMEM(whole, BF16),
            pltpu.VMEM(whole, BF16),
            pltpu.VMEM((self.members - 1, self.count, self.width), BF16),
            pltpu.VMEM((self.groups * self.part, self.width), BF16),
            pltpu.VMEM((self.groups - 1, self.part, self.width), BF16),
            pltpu.VMEM((self.part, self.width), BF16),
        ] + [pltpu.SemaphoreType.DMA((n,)) for n in sems] + [pltpu.SemaphoreType.DMA]

    def result(self):
        return (2, self.groups, self.part, self.width)

    def bind(self, refs, source, result):
        self.mine, self.got, self.from_members, self.total, self.from_groups, self.piece = refs[:6]
        self.sems = refs[6:14]
        self.local = refs[14]
        self.source, self.result_ref = source, result
        return self

    def section_copy(self):
        section, group, member = place()
        return remote(
            self.source.at[1 - section], self.got, self.sems[0].at[0], self.sems[1].at[0], (1 - section, group, member)
        )

    def own_copy(self):
        return pltpu.make_async_copy(self.source.at[lax.axis_index("section")], self.mine, self.local)

    def member_copy(self, offset):
        section, group, member = place()
        to = lax.rem(member + offset, self.members)
        return remote(
            self.mine.at[rows_at(to, self.count)],
            self.from_members.at[offset - 1],
            self.sems[2].at[offset],
            self.sems[3].at[offset],
            (section, group, to),
        )

    def group_copy(self, offset):
        section, group, member = place()
        to = lax.rem(group + offset, self.groups)
        return remote(
            self.total.at[rows_at(to, self.part)],
            self.from_groups.at[offset - 1],
            self.sems[4].at[offset],
            self.sems[5].at[offset],
            (section, to, member),
        )

    def gather_copy(self, offset, across):
        section, group, member = place()
        slot = across * self.groups + offset
        return remote(
            self.piece,
            self.result_ref.at[section, group],
            self.sems[6].at[slot],
            self.sems[7].at[slot],
            (self.target, lax.rem(group + offset, self.groups), member),
        )

    def gathered(self, offset, across):
        section, group, member = place()
        slot = across * self.groups + offset
        origin = lax.rem(group + self.groups - offset, self.groups)
        half = 1 - section if across else section
        return remote(
            self.piece,
            self.result_ref.at[half, origin],
            self.sems[6].at[slot],
            self.sems[7].at[slot],
            (self.target, origin, member),
        )

    def start_section(self):
        self.section_copy().start()
        self.own_copy().start()

    def start_members(self):
        self.own_copy().wait()
        self.section_copy().wait()
        self.mine[...] = (self.mine[...].astype(F32) + self.got[...].astype(F32)).astype(BF16)
        for offset in range(1, self.members):
            self.member_copy(offset).start()

    def start_groups(self):
        for offset in range(1, self.members):
            self.member_copy(offset).wait()
        total = self.mine[rows_at(lax.axis_index("member"), self.count), :].astype(F32)
        for offset in range(1, self.members):
            total = total + self.from_members[offset - 1].astype(F32)
        self.total[: self.count, :] = total.astype(BF16)
        spare = self.groups * self.part - self.count
        if spare:
            self.total[self.count :, :] = jnp.zeros((spare, self.width), BF16)
        for offset in range(1, self.groups):
            self.group_copy(offset).start()

    def start_gather(self):
        section, group, member = place()
        for offset in range(1, self.groups):
            self.group_copy(offset).wait()
        total = self.total[rows_at(group, self.part), :].astype(F32)
        for offset in range(1, self.groups):
            total = total + self.from_groups[offset - 1].astype(F32)
        self.piece[...] = total.astype(BF16)

        @pl.when(section == self.target)
        def _():
            for offset in range(1, self.groups):
                self.gather_copy(offset, 0).start()
            keep = pltpu.make_async_copy(self.piece, self.result_ref.at[section, group], self.local)
            keep.start()
            keep.wait()

        @pl.when(section != self.target)
        def _():
            for offset in range(self.groups):
                self.gather_copy(offset, 1).start()

    def finish(self):
        section, group, member = place()

        @pl.when(section == self.target)
        def _():
            for offset in range(1, self.groups):
                self.gather_copy(offset, 0).wait_send()
                self.gathered(offset, 0).wait_recv()
            for offset in range(self.groups):
                self.gathered(offset, 1).wait_recv()

        @pl.when(section != self.target)
        def _():
            for offset in range(self.groups):
                self.gather_copy(offset, 1).wait_send()


class VectorSum:
    def __init__(self, groups, members, width):
        self.groups, self.members, self.width = groups, members, width

    def scratch(self):
        return [
            pltpu.VMEM((2 * self.members, VECTORS, self.width), BF16),
            pltpu.VMEM((self.groups, VECTORS, self.width), BF16),
            pltpu.VMEM((VECTORS, self.width), BF16),
            pltpu.VMEM((VECTORS, self.width), BF16),
        ] + [pltpu.SemaphoreType.DMA((n,)) for n in (2 * self.members,) * 2 + (self.groups,) * 2]

    def bind(self, refs):
        self.near, self.far, self.own, self.middle = refs[:4]
        self.sems = refs[4:]
        return self

    def near_copy(self, offset):
        section, group, member = place()
        ds, dm = divmod(offset, self.members)
        to = lax.rem(section + ds, 2), group, lax.rem(member + dm, self.members)
        return remote(
            self.own, self.near.at[section * self.members + member], self.sems[0].at[offset], self.sems[1].at[offset], to
        )

    def near_got(self, offset):
        section, group, member = place()
        ds, dm = divmod(offset, self.members)
        origin = lax.rem(section + ds, 2), lax.rem(member + self.members - dm, self.members)
        return remote(
            self.own,
            self.near.at[origin[0] * self.members + origin[1]],
            self.sems[0].at[offset],
            self.sems[1].at[offset],
            (origin[0], group, origin[1]),
        )

    def far_copy(self, offset):
        section, group, member = place()
        to = section, lax.rem(group + offset, self.groups), member
        return remote(self.middle, self.far.at[group], self.sems[2].at[offset], self.sems[3].at[offset], to)

    def far_got(self, offset):
        section, group, member = place()
        origin = lax.rem(group + self.groups - offset, self.groups)
        return remote(
            self.middle, self.far.at[origin], self.sems[2].at[offset], self.sems[3].at[offset], (section, origin, member)
        )

    def start(self, values):
        section, group, member = place()
        self.own[...] = values
        self.near[section * self.members + member] = values
        for offset in range(1, 2 * self.members):
            self.near_copy(offset).start()

    def start_far(self):
        for offset in range(1, 2 * self.members):
            self.near_copy(offset).wait_send()
            self.near_got(offset).wait_recv()
        total = jnp.zeros((VECTORS, self.width), F32)
        for index in range(2 * self.members):
            total = total + self.near[index].astype(F32)
        self.middle[...] = total.astype(BF16)
        self.far[lax.axis_index("group")] = total.astype(BF16)
        for offset in range(1, self.groups):
            self.far_copy(offset).start()

    def finish(self):
        for offset in range(1, self.groups):
            self.far_copy(offset).wait_send()
            self.far_got(offset).wait_recv()
        total = jnp.zeros((VECTORS, self.width), F32)
        for index in range(self.groups):
            total = total + self.far[index].astype(F32)
        return total


def first_backward(seg, dout, y_send, grads1, vec1, kept, weights, steps, groups, members):
    width, hidden = dout.shape[1], weights[3].shape[2]
    shapes = kept_shapes(steps, width, hidden)
    parts = hidden // width
    size = half_rows(width // members)
    mlp_blocks = range(2 * parts + 1)
    attn_blocks = range(2 * parts + 1, 2 * parts + 4)
    plans = [
        Reduction(1, groups, members, (2 * parts + 4) * size, width),
        Reduction(0, groups, members, len(mlp_blocks) * size, width),
        Reduction(0, groups, members, len(attn_blocks) * size, width),
    ]
    vectors = [VectorSum(groups, members, width) for _ in range(2)]
    counts = [len(plan.scratch()) for plan in plans] + [len(v.scratch()) for v in vectors]

    def body(seg, dout, vec, w_qkv, w_proj, w_fc1, w_fc2, *refs):
        kept, refs = refs[:9], refs[9:]
        (y_send, grads1, vec1), refs = refs[:3], refs[3:]
        (g_own, y_got, g_got, *finals), refs = refs[:8], refs[8:]
        sums, refs = refs[:5], refs[5:]
        (grad_after, grad_context, grad_qkv, g_send, grads_mlp, grads_attn), refs = refs[:6], refs[6:]
        (row_send, row_recv), refs = refs[:2], refs[2:]
        bound = []
        for item, count in zip(plans + vectors, counts):
            bound.append(refs[:count])
            refs = refs[count:]
        upper = plans[0].bind(bound[0], grads1, finals[0])
        lower_mlp = plans[1].bind(bound[1], grads_mlp, finals[1])
        lower_attn = plans[2].bind(bound[2], grads_attn, finals[2])
        upper_vec, lower_vec = [v.bind(b) for v, b in zip(vectors, bound[3:])]
        weights = (vec, w_qkv, w_proj, w_fc1, w_fc2)
        xhat1, r1, qkv, prob, *mlp_kept = kept
        step = pl.program_id(0)
        section, group, member = place()
        partner = (1 - section, group, member)

        def y_copy():
            return remote(y_send, y_got, row_send.at[steps], row_recv.at[steps], partner)

        def g_copy(index):
            return remote(
                g_send.at[index],
                g_got.at[rows_at(index, STEP)],
                row_send.at[index],
                row_recv.at[index],
                partner,
            )

        @pl.when(step == 0)
        def _():
            greet(groups, members)
            clear(sums)
            upper.start_section()
            y_copy().start()

        @pl.when(step == 1)
        def _():
            upper.start_members()
            upper_vec.start(vec1[...])

        @pl.when(step == steps)
        def _():
            upper.start_groups()
            upper_vec.start_far()

        @pl.when(step == steps + 1)
        def _():
            lower_mlp.start_members()

        @pl.when(step == steps + 2)
        def _():
            upper.start_gather()
            finals[3][...] = upper_vec.finish()

        @pl.when(step < steps)
        def _():
            g_send[step] = dout[...]
            rows = rows_at(step, STEP)

            def after_mlp(after, context):
                grad_after[rows, :] = after
                grad_context[rows, :] = context

            backward_mlp(dout, weights, mlp_kept, sums, after_mlp)

        @pl.when(step == steps - 1)
        def _():
            write_blocks(sums, members, mlp_blocks, grads_mlp)
            lower_mlp.start_section()

        @pl.when(step >= steps)
        def _():
            index = step - steps
            rows = rows_at(index, STEP)

            def after_attn(values):
                low = values.astype(BF16)
                kept_rows = g_send[index]
                g_own[...] = jnp.where(section == 0, low, kept_rows)
                g_send[index] = jnp.where(section == 0, kept_rows, low)
                g_copy(index).start()

            backward_attn(
                grad_after.at[rows], grad_context.at[rows], seg, weights, kept[:4], sums, grad_qkv, after_attn
            )

        @pl.when(step == 2 * steps - 1)
        def _():
            write_blocks(sums, members, attn_blocks, grads_attn)
            lower_attn.start_section()
            lower_vec.start(vector_sums(sums[4]))
            lower_mlp.start_groups()
            lower_attn.start_members()
            lower_vec.start_far()
            lower_mlp.start_gather()
            lower_attn.start_groups()
            upper.finish()
            y_copy().wait()
            for index in range(steps):
                g_copy(index).wait()
            finals[4][...] = lower_vec.finish()
            lower_attn.start_gather()
            lower_mlp.finish()
            lower_attn.finish()

    def early(block, axis):
        if axis == 0:
            return pl.BlockSpec(block, lambda i: (jnp.minimum(i, steps - 1), 0))
        return pl.BlockSpec(block, lambda i: (0, jnp.minimum(i, steps - 1)))

    def late(block, axis):
        if axis == 0:
            return pl.BlockSpec(block, lambda i: (jnp.maximum(i - steps, 0), 0))
        return pl.BlockSpec(block, lambda i: (0, jnp.maximum(i - steps, 0)))

    anywhere = pl.BlockSpec(memory_space=pl.ANY)
    low_rows = jax.ShapeDtypeStruct((steps * STEP, width), BF16)
    vec_out = jax.ShapeDtypeStruct((VECTORS, width), F32)
    vec_spec = pl.BlockSpec((VECTORS, width), lambda i: (0, 0))
    scratch = sum_scratch(width, hidden) + [
        pltpu.VMEM((steps * STEP, width), F32),
        pltpu.VMEM((steps * STEP, width), BF16),
        pltpu.VMEM((STEP, 3 * width), BF16),
        pltpu.VMEM((steps, STEP, width), BF16),
        pltpu.VMEM((2, members * plans[1].count, width), BF16),
        pltpu.VMEM((2, members * plans[2].count, width), BF16),
        pltpu.SemaphoreType.DMA((steps + 1,)),
        pltpu.SemaphoreType.DMA((steps + 1,)),
    ]
    for item in plans + vectors:
        scratch = scratch + item.scratch()
    return pl.pallas_call(
        body,
        grid=(2 * steps,),
        in_specs=[pl.BlockSpec((1, STEP), lambda i: (0, jnp.maximum(i - steps, 0))), early((STEP, width), 0)]
        + [
            pl.BlockSpec((1,) + w.shape[1:], lambda i: (0, 0, 0), pipeline_mode=pl.Buffered(1)) for w in weights
        ]
        + [late(block, axis) for _, _, block, axis in shapes[:4]]
        + [early(block, axis) for _, _, block, axis in shapes[4:]]
        + [anywhere, anywhere, vec_spec],
        out_specs=[late((STEP, width), 0)] + [anywhere] * 5 + [vec_spec] * 2,
        out_shape=[low_rows] * 3
        + [jax.ShapeDtypeStruct(plan.result(), BF16) for plan in plans]
        + [vec_out] * 2,
        scratch_shapes=scratch,
        compiler_params=pltpu.CompilerParams(
            vmem_limit_bytes=60 * MIB, collective_id=1, has_side_effects=True
        ),
        cost_estimate=pl.CostEstimate(
            flops=steps * STEP * 8000000, bytes_accessed=30 * MIB, transcendentals=0
        ),
        name="backward_first",
    )(seg, dout, *weights, *kept, y_send, grads1, vec1)


def finish(section, member, y_own, y_got, g_own, g_got, finals, width, hidden, steps, members):
    parts = hidden // width
    share = width // members
    size = half_rows(share)
    upper, lower_mlp, lower_attn, upper_vec, lower_vec = finals
    upper, lower_mlp, lower_attn = [f.reshape(2, -1, width) for f in (upper, lower_mlp, lower_attn)]
    lows = 2 * parts + 1

    def body(s, y_own, y_got, g_own, g_got, upper, lower_mlp, lower_attn, upper_vec, lower_vec, *outs):
        acts, grads, a_gain, a_shift, d_qkv, d_qv, d_proj, b_proj, m_gain, m_shift, d_fc1, b_fc1, d_fc2, b_fc2 = outs
        step = pl.program_id(0)
        first = s[0] == 0
        mine = step // steps == s[0]
        acts[0] = jnp.where(mine, y_own[...], y_got[...])
        grads[0] = jnp.where(mine, g_own[...], g_got[...]).astype(F32)

        @pl.when(step == 0)
        def _():
            for block in range(2 * parts + 4):
                for half in range(2):
                    top = half * (share - size)
                    at = block * size
                    low = (
                        lower_mlp[half, at : at + size, :]
                        if block < lows
                        else lower_attn[half, at - lows * size : at - lows * size + size, :]
                    )
                    rows = jnp.where(first, low.astype(F32), upper[half, at : at + size, :].astype(F32))
                    if block < parts:
                        d_fc1[0, top : top + size, block * width : (block + 1) * width] = rows
                    elif block < 2 * parts:
                        base = (block - parts) * share + top
                        d_fc2[0, base : base + size, :] = rows
                    elif block == 2 * parts:
                        d_proj[0, top : top + size, :] = rows
                    else:
                        left = (block - lows) * width
                        d_qkv[0, top : top + size, left : left + width] = rows
            vectors = jnp.where(first, lower_vec[...], upper_vec[...])

            def put(out, row, count=1):
                flat = jnp.concatenate([vectors[row + i : row + i + 1, :] for i in range(count)], axis=1)
                length = count * width // members
                value = flat[:, :length]
                for m in range(1, members):
                    value = jnp.where(s[1] == m, flat[:, m * length : (m + 1) * length], value)
                out[...] = value

            put(a_gain, ATTN_GAIN)
            put(a_shift, ATTN_SHIFT)
            put(d_qv, Q_BIAS, 2)
            put(b_proj, PROJ_BIAS)
            put(m_gain, MLP_GAIN)
            put(m_shift, MLP_SHIFT)
            put(b_fc1, FC1_BIAS, parts)
            put(b_fc2, FC2_BIAS)

    def whole(shape):
        return pl.BlockSpec(shape, lambda i, s, n=len(shape): (0,) * n)

    own = pl.BlockSpec((STEP, width), lambda i, s: (jnp.clip(i - s[0] * steps, 0, steps - 1), 0))
    got = pl.BlockSpec((STEP, width), lambda i, s: (jnp.clip(i - (1 - s[0]) * steps, 0, steps - 1), 0))
    total = 2 * steps * STEP
    smalls = [
        (1, share), (1, share), (1, share, 3 * width), (1, 2 * share), (1, share, width), (1, share), (1, share),
        (1, share), (1, share, hidden), (1, hidden // members), (1, hidden // members, width), (1, share),
    ]
    rows_spec = pl.BlockSpec((1, STEP, width), lambda i, s: (0, i, 0))
    inputs = [upper, lower_mlp, lower_attn, upper_vec, lower_vec]
    return pl.pallas_call(
        body,
        grid_spec=pltpu.PrefetchScalarGridSpec(
            num_scalar_prefetch=1,
            grid=(2 * steps,),
            in_specs=[own, got, own, got] + [whole(x.shape) for x in inputs],
            out_specs=[rows_spec, rows_spec] + [whole(shape) for shape in smalls],
        ),
        out_shape=[
            jax.ShapeDtypeStruct((1, total, width), BF16),
            jax.ShapeDtypeStruct((1, total, width), F32),
        ]
        + [jax.ShapeDtypeStruct(shape, F32) for shape in smalls],
        compiler_params=pltpu.CompilerParams(vmem_limit_bytes=40 * MIB),
        cost_estimate=pl.CostEstimate(flops=0, bytes_accessed=16 * MIB, transcendentals=0),
        name="finish",
    )(jnp.stack([section, member]).astype(jnp.int32), y_own, y_got, g_own, g_got, *inputs)


def gather_weights(own):
    count = len(own)

    def body(*refs):
        mine, both, held = refs[:count], refs[count : 2 * count], refs[2 * count : 3 * count]
        send, recv, load, store = refs[3 * count :]
        section, group, member = place()
        partner = (1 - section, group, member)
        loads = [pltpu.make_async_copy(src.at[0], dst, load.at[i]) for i, (src, dst) in enumerate(zip(mine, held))]
        for copy in loads:
            copy.start()
        barrier = pltpu.get_barrier_semaphore()
        pl.semaphore_signal(barrier, inc=1, device_id=partner, device_id_type=MESH)
        pl.semaphore_wait(barrier, 1)
        copies = [
            remote(src.at[0], dst.at[section], send.at[i], recv.at[i], partner)
            for i, (src, dst) in enumerate(zip(mine, both))
        ]
        for copy in copies:
            copy.start()
        stores = [
            pltpu.make_async_copy(src, dst.at[section], store.at[i]) for i, (src, dst) in enumerate(zip(held, both))
        ]
        for copy, later in zip(loads, stores):
            copy.wait()
            later.start()
        for copy in copies + stores:
            copy.wait()

    anywhere = pl.BlockSpec(memory_space=pl.ANY)
    return pl.pallas_call(
        body,
        in_specs=[anywhere] * count,
        out_specs=[anywhere] * count,
        out_shape=[jax.ShapeDtypeStruct((2,) + w.shape[1:], w.dtype) for w in own],
        scratch_shapes=[pltpu.VMEM(w.shape[1:], w.dtype) for w in own] + [pltpu.SemaphoreType.DMA((count,))] * 4,
        compiler_params=pltpu.CompilerParams(collective_id=0, has_side_effects=True),
        name="gather_weights",
    )(*own)


def pack_vectors(vectors, width):
    flat = jnp.concatenate([v.reshape(-1, width) for v in vectors], axis=0)
    return jnp.pad(flat, ((0, VECTORS - flat.shape[0]), (0, 0)))[None]


def per_device(
    tokens,
    segment,
    cotangent,
    attn_gain,
    attn_shift,
    qkv_weight,
    qv_bias,
    proj_weight,
    proj_bias,
    mlp_gain,
    mlp_shift,
    fc1_weight,
    fc1_bias,
    fc2_weight,
    fc2_bias,
):
    section, member = lax.axis_index("section"), lax.axis_index("member")
    groups, members = lax.axis_size("group"), lax.axis_size("member")
    rows, width = tokens.shape
    hidden = fc1_weight.shape[2]
    steps = rows // 2 // STEP
    vec = pack_vectors(
        (attn_gain, attn_shift, qv_bias, proj_bias, mlp_gain, mlp_shift, fc2_bias, fc1_bias), width
    )
    weights = gather_weights([vec, qkv_weight, proj_weight, fc1_weight, fc2_weight])
    at = section.reshape(1).astype(jnp.int32)
    seg = segment.reshape(1, rows)
    y0, *kept = first_forward(at, tokens, seg, weights, steps)
    y_own, y_send, g1, grads1, vec1 = second_layer(at, y0, seg, cotangent, weights, steps, members)
    seg_half = lax.dynamic_slice(seg, (0, section * (rows // 2)), (1, rows // 2))
    g_own, y_got, g_got, *finals = first_backward(
        seg_half, g1, y_send, grads1, vec1, kept, weights, steps, groups, members
    )
    return tuple(finish(section, member, y_own, y_got, g_own, g_got, finals, width, hidden, steps, members))


def solution(mesh):
    row = P("section", None)
    mat = P("section", None, None)
    tokens = P(("group", "member"), None)
    split = P("section", "member")
    split_mat = P("section", "member", None)
    stacked = P("section", ("group", "member"), None)
    return jax.shard_map(
        per_device,
        mesh=mesh,
        in_specs=(
            tokens, P(("group", "member")), tokens,
            row, row, mat, row, mat, row, row, row, mat, row, mat, row,
        ),
        out_specs=(
            stacked, stacked,
            split, split, split_mat, split, split_mat, split, split, split, split_mat, split, split_mat, split,
        ),
        check_vma=False,
    )
```

```python
import jax
import jax.numpy as jnp
from jax import lax
from jax.experimental import pallas as pl
from jax.experimental.pallas import tpu as pltpu
from jax.sharding import PartitionSpec as P

HD = 64
S = 256
HALF = S // 2
GLOBAL_LEN = 197
LOCAL_LEN = 37
PAIR = 2 * HD
STEP = 2 * S
EPS = 1e-06
SCALE = HD ** (-0.5)
LOG2E = 1.4426950408889634
CHUNK = 768
FORWARD_CHUNK = 256
DEPTH = 4
F32 = jnp.float32
BF16 = jnp.bfloat16
MIB = 1 << 20
MESH = pl.DeviceIdType.MESH

ATTN_GAIN, ATTN_SHIFT, Q_BIAS, V_BIAS, PROJ_BIAS, MLP_GAIN, MLP_SHIFT, FC2_BIAS, FC1_BIAS = range(9)
VECTORS = 16


def up16(value):
    return -(-value // 16) * 16


def key_windows(local):
    if not local:
        return ((0, up16(GLOBAL_LEN)),) * 2
    first_end = ((HALF - 1) // LOCAL_LEN + 1) * LOCAL_LEN
    second_start = HALF // LOCAL_LEN * LOCAL_LEN // 16 * 16
    return ((0, up16(first_end)), (second_start, up16(S // LOCAL_LEN * LOCAL_LEN)))


WINDOWS = tuple((local, key_windows(local)) for local in (False, True))
PROB_ROWS = sum(hi - lo for _, windows in WINDOWS for lo, hi in windows)


def prob_offset(pair, sequence, block):
    spans = [hi - lo for _, windows in WINDOWS for lo, hi in windows]
    return pair * PROB_ROWS + sum(spans[: 2 * sequence + block])


def nn(left, right):
    return jnp.dot(left, right, preferred_element_type=F32)


def nt(left, right):
    return lax.dot_general(left, right, (((1,), (1,)), ((), ())), preferred_element_type=F32)


def tn(left, right):
    return lax.dot_general(left, right, (((0,), (0,)), ((), ())), preferred_element_type=F32)


def column_sums(values):
    return jnp.sum(values.reshape(values.shape[0] // 8, 8, values.shape[1]), axis=0)


def normalized(values):
    centered = values - jnp.mean(values, axis=1, keepdims=True)
    inverse = lax.rsqrt(jnp.mean(centered * centered, axis=1, keepdims=True) + EPS)
    return centered * inverse, inverse


def norm_back(scaled, inverse, gain, grad):
    grad_scaled = grad * gain
    first = jnp.mean(grad_scaled, axis=1, keepdims=True)
    second = jnp.mean(grad_scaled * scaled, axis=1, keepdims=True)
    return inverse * (grad_scaled - first - scaled * second)


def crop_of(index):
    total = jnp.zeros_like(index)
    for crop in range(1, S // LOCAL_LEN + 1):
        total = total + (index >= crop * LOCAL_LEN).astype(jnp.int32)
    return total


def mask_bias(local, block, lo, hi):
    if not local:
        rows = lax.broadcasted_iota(jnp.int32, (hi - lo, HALF), 0) + lo
        return jnp.where(rows < GLOBAL_LEN, 0.0, -1e30)
    keys = crop_of(lax.broadcasted_iota(jnp.int32, (hi - lo, HALF), 0) + lo)
    queries = crop_of(lax.broadcasted_iota(jnp.int32, (hi - lo, HALF), 1) + block * HALF)
    return jnp.where(keys == queries, 0.0, -1e30)


def split_pair(rows):
    lane = lax.broadcasted_iota(jnp.int32, (1, PAIR), 1)
    first = (lane < HD).astype(rows.dtype)
    second = (lane >= HD).astype(rows.dtype)
    return jnp.concatenate([rows * first, rows * second], axis=0)


def padded(rows, lo, hi):
    parts = [rows]
    if lo:
        parts = [jnp.zeros((lo, rows.shape[1]), rows.dtype)] + parts
    if hi < S:
        parts = parts + [jnp.zeros((S - hi, rows.shape[1]), rows.dtype)]
    return jnp.concatenate(parts, axis=0) if len(parts) > 1 else rows


def diagonal(values):
    return jnp.concatenate([values[:HD, :HALF], values[HD:, HALF:]], axis=0)


def units_of(width):
    return [(sequence, pair, block) for sequence in range(2) for pair in range(width // PAIR) for block in range(2)]


def pipelined(units, depth, stages):
    held = [{} for _ in stages]
    for now in range(len(units) + depth * (len(stages) - 1)):
        for i, stage in enumerate(stages):
            at = now - i * depth
            if 0 <= at < len(units):
                before = [held[i - 1].pop(at)] if i else []
                held[i][at] = stage(units[at], *before)


class Once(dict):
    def get_or(self, key, make):
        if key not in self:
            self[key] = make()
        return self[key]


def place_of(unit):
    sequence, pair, block = unit
    lo, hi = WINDOWS[sequence][1][block]
    return sequence * S, pair * PAIR, block * HALF, lo, hi


def attend(seg, qkv, prob, ctx_t, width):
    once = Once()

    def valid_of(unit):
        base, _, at, _, _ = place_of(unit)
        return seg[0:1, base + at : base + at + HALF] >= 0

    def values_of(unit):
        base, left, _, _, _ = place_of(unit)
        cols = slice(2 * width + left, 2 * width + left + PAIR)
        return once.get_or(unit[:2], lambda: qkv[base : base + S, cols].T)

    def bias_of(unit):
        sequence, _, block = unit
        _, _, _, lo, hi = place_of(unit)

        def make():
            bias = mask_bias(WINDOWS[sequence][0], block, lo, hi)
            return jnp.concatenate([bias, bias], axis=1)

        return once.get_or(("bias", sequence, block), make)

    def raw_scores(unit):
        base, left, at, lo, hi = place_of(unit)
        values_of(unit)
        keys = qkv[base + lo : base + hi, width + left : width + left + PAIR]
        return nt(keys, split_pair(qkv[base + at : base + at + HALF, left : left + PAIR]))

    def softmax(unit, raw):
        sequence, pair, block = unit
        _, _, _, lo, hi = place_of(unit)
        scores = raw * (SCALE * LOG2E)
        cut = 0 if WINDOWS[sequence][0] else GLOBAL_LEN // 16 * 16 - lo
        tail = scores[cut:] + bias_of(unit)[cut:]
        scores = jnp.concatenate([scores[:cut], tail], axis=0) if cut else tail
        exponent = jnp.exp2(scores - jnp.max(scores, axis=0, keepdims=True))
        total = jnp.sum(exponent, axis=0, keepdims=True)
        valid = valid_of(unit)
        inverse = jnp.where(jnp.concatenate([valid, valid], axis=1), 1.0 / total, 0.0)
        probs = (exponent * inverse).astype(BF16)
        offset = prob_offset(pair, sequence, block)
        prob[offset : offset + hi - lo, :] = probs
        return probs

    def context(unit, probs):
        base, left, at, lo, hi = place_of(unit)
        values_t = values_of(unit)
        mixed = diagonal(nn(values_t, padded(probs, lo, hi)))
        own = values_t[:, at : at + HALF].astype(F32)
        ctx_t[left : left + PAIR, base + at : base + at + HALF] = jnp.where(
            valid_of(unit), mixed, own
        ).astype(BF16)

    pipelined(units_of(width), DEPTH, [raw_scores, softmax, context])


def attend_back(seg, qkv, prob, grad_context, grad_qkv, width):
    once = Once()

    def padding_of(unit):
        base = unit[0] * S

        def make():
            valid = (seg[0:1, base : base + S] >= 0).astype(jnp.int32)
            count = jnp.sum(valid, axis=1, keepdims=True)
            return lax.broadcasted_iota(jnp.int32, (S, PAIR), 0) >= count

        return once.get_or(("padding", unit[0]), make)

    def keys_of(unit):
        base, left, _, _, _ = place_of(unit)
        cols = slice(width + left, width + left + PAIR)
        return once.get_or(("keys", unit[:2]), lambda: qkv[base : base + S, cols].T)

    def grads_of(unit):
        base, left, at, _, _ = place_of(unit)
        rows = slice(base + at, base + at + HALF)
        return once.get_or(("grads", unit), lambda: split_pair(grad_context[rows, left : left + PAIR]))

    def grad_probs(unit):
        base, left, _, lo, hi = place_of(unit)
        keys_of(unit)
        return nt(qkv[base + lo : base + hi, 2 * width + left : 2 * width + left + PAIR], grads_of(unit))

    def grad_scores(unit, grads):
        sequence, pair, block = unit
        _, _, _, lo, hi = place_of(unit)
        offset = prob_offset(pair, sequence, block)
        probs_low = prob[offset : offset + hi - lo, :]
        probs = probs_low.astype(F32)
        product = probs * grads
        inner = jnp.sum(product, axis=0, keepdims=True)
        return (product - probs * inner).astype(BF16), probs_low

    def grad_rows(unit, given):
        grad_raw, probs_low = given
        base, left, at, lo, hi = place_of(unit)
        queries = split_pair(qkv[base + at : base + at + HALF, left : left + PAIR])
        grad_values = padded(nn(probs_low, grads_of(unit)), lo, hi)
        grad_keys = padded(nn(grad_raw, queries), lo, hi)
        grad_queries = diagonal(nn(keys_of(unit), padded(grad_raw, lo, hi))) * SCALE
        grad_qkv[base + at : base + at + HALF, left : left + PAIR] = grad_queries.astype(BF16).T
        if unit[2] == 0:
            once["first", unit[:2]] = grad_values, grad_keys
            return
        other_values, other_keys = once["first", unit[:2]]
        own = jnp.where(padding_of(unit), grad_context[base : base + S, left : left + PAIR].astype(F32), 0.0)
        grad_qkv[base : base + S, width + left : width + left + PAIR] = (
            (other_keys + grad_keys) * SCALE
        ).astype(BF16)
        grad_qkv[base : base + S, 2 * width + left : 2 * width + left + PAIR] = (
            other_values + grad_values + own
        ).astype(BF16)

    pipelined(units_of(width), DEPTH, [grad_probs, grad_scores, grad_rows])


def vector(vec, row, count=1):
    parts = [vec[0, row + i : row + i + 1, :] for i in range(count)]
    return parts[0] if count == 1 else jnp.concatenate(parts, axis=1)


def forward(x, seg, weights, kept, y, after_attention=None):
    vec, w_qkv, w_proj, w_fc1, w_fc2 = weights
    xhat1, r1, qkv, prob, ctx_t, xhat2, r2, act, dgelu = kept
    _, width = x.shape
    hidden = w_fc1.shape[2]
    scaled, inverse = normalized(x[...].astype(F32))
    xhat1[...] = scaled.astype(BF16)
    r1[...] = inverse
    normed = (scaled * vector(vec, ATTN_GAIN) + vector(vec, ATTN_SHIFT)).astype(BF16)
    for part, bias in ((0, Q_BIAS), (1, None), (2, V_BIAS)):
        mixed = nn(normed, w_qkv[0, :, part * width : (part + 1) * width])
        if bias is not None:
            mixed = mixed + vector(vec, bias)
        qkv[:, part * width : (part + 1) * width] = mixed.astype(BF16)
    attend(seg, qkv, prob, ctx_t, width)
    if after_attention is not None:
        after_attention()
    after = x[...].astype(F32) + tn(ctx_t[...], w_proj[0]) + vector(vec, PROJ_BIAS)
    scaled, inverse = normalized(after)
    xhat2[...] = scaled.astype(BF16)
    r2[...] = inverse
    normed = (scaled * vector(vec, MLP_GAIN) + vector(vec, MLP_SHIFT)).astype(BF16)
    output = after + vector(vec, FC2_BIAS)
    bias = vector(vec, FC1_BIAS, hidden // width)
    tops = list(range(0, hidden, FORWARD_CHUNK))

    def product(left):
        return nn(normed, w_fc1[0, :, left : left + FORWARD_CHUNK])

    coming = product(tops[0])
    for i, left in enumerate(tops):
        cols = slice(left, left + FORWARD_CHUNK)
        pre = coming + bias[:, cols]
        if i + 1 < len(tops):
            coming = product(tops[i + 1])
        below = 0.5 + 0.5 * lax.erf(pre * (0.5**0.5))
        density = jnp.exp2(pre * pre * (-0.5 * LOG2E)) * (1.0 / (2.0 * jnp.pi) ** 0.5)
        active = (pre * below).astype(BF16)
        act[:, cols] = active
        dgelu[:, cols] = (below + pre * density).astype(BF16)
        output = output + nn(active, w_fc2[0, cols, :])
    y[...] = output.astype(BF16)


def adder(sum_vec, width):
    def add(row, values):
        for i in range(values.shape[1] // width):
            at = (row + i) * 8
            sum_vec[at : at + 8, :] += column_sums(values[:, i * width : (i + 1) * width])

    return add


def backward_fc2(dout, act, sums):
    sum_fc2, sum_vec = sums[3:]
    top_grad = dout[...]
    adder(sum_vec, dout.shape[1])(FC2_BIAS, top_grad.astype(F32))
    sum_fc2[...] += nn(top_grad.T, act[...])


def backward_mlp(dout, weights, kept, sums, write, with_fc2=True):
    vec, _, w_proj, w_fc1, w_fc2 = weights
    ctx_t, xhat2, r2, act, dgelu = kept
    _, sum_proj, sum_fc1, _, sum_vec = sums
    rows, width = dout.shape
    hidden = w_fc1.shape[2]
    add = adder(sum_vec, width)
    top_grad = dout[...]
    top_wide = top_grad.astype(F32)
    if with_fc2:
        backward_fc2(dout, act, sums)
    scaled = xhat2[...].astype(F32)
    normed_t = (scaled * vector(vec, MLP_GAIN) + vector(vec, MLP_SHIFT)).astype(BF16).T
    grad_normed = jnp.zeros((rows, width), F32)
    column_parts = []
    for left in range(0, hidden, CHUNK):
        cols = slice(left, left + CHUNK)
        grad_pre = nt(top_grad, w_fc2[0, cols, :]) * dgelu[:, cols].astype(F32)
        column_parts.append(column_sums(grad_pre))
        grad_pre = grad_pre.astype(BF16)
        grad_normed = grad_normed + nt(grad_pre, w_fc1[0, :, cols])
        sum_fc1[:, cols] += nn(normed_t, grad_pre)
    columns = jnp.concatenate(column_parts, axis=1)
    for i in range(hidden // width):
        at = (FC1_BIAS + i) * 8
        sum_vec[at : at + 8, :] += columns[:, i * width : (i + 1) * width]
    add(MLP_GAIN, grad_normed * scaled)
    add(MLP_SHIFT, grad_normed)
    grad_after = top_wide + norm_back(scaled, r2[...], vector(vec, MLP_GAIN), grad_normed)
    add(PROJ_BIAS, grad_after)
    grad_branch = grad_after.astype(BF16)
    sum_proj[...] += nn(ctx_t[...], grad_branch)
    write(grad_after, nt(grad_branch, w_proj[0]).astype(BF16))


def backward_attn(grad_after, grad_context, seg, weights, kept, sums, grad_qkv, write, halfway=None):
    vec, w_qkv, _, _, _ = weights
    xhat1, r1, qkv, prob = kept
    sum_qkv, sum_vec = sums[0], sums[4]
    rows, width = grad_after.shape
    add = adder(sum_vec, width)
    attend_back(seg, qkv, prob, grad_context, grad_qkv, width)
    if halfway is not None:
        halfway()
    scaled = xhat1[...].astype(F32)
    normed_t = (scaled * vector(vec, ATTN_GAIN) + vector(vec, ATTN_SHIFT)).astype(BF16).T
    grad_normed = jnp.zeros((rows, width), F32)
    for part, row in ((0, Q_BIAS), (1, None), (2, V_BIAS)):
        cols = slice(part * width, (part + 1) * width)
        piece = grad_qkv[:, cols]
        if row is not None:
            add(row, piece.astype(F32))
        sum_qkv[:, cols] += nn(normed_t, piece)
        grad_normed = grad_normed + nt(piece, w_qkv[0, :, cols])
    add(ATTN_GAIN, grad_normed * scaled)
    add(ATTN_SHIFT, grad_normed)
    write(grad_after[...] + norm_back(scaled, r1[...], vector(vec, ATTN_GAIN), grad_normed))


def half_rows(share):
    return up16(share // 2)


def write_blocks(sums, members, blocks, out):
    sum_qkv, sum_proj, sum_fc1, sum_fc2, _ = sums
    width = sum_proj.shape[0]
    share = width // members
    size = half_rows(share)
    parts = sum_fc1.shape[1] // width

    def store(rows, member, block):
        at = (member * len(blocks) + blocks.index(block)) * size
        out[0, at : at + size, :] = rows[:size]
        out[1, at : at + size, :] = rows[share - size :]

    for block in blocks:
        if block < parts:
            whole = sum_fc1[:, block * width : (block + 1) * width]
        elif block < 2 * parts:
            chunk = block - parts
            whole = sum_fc2[:, chunk * width : (chunk + 1) * width].astype(BF16).T
            for place in range(members):
                row = chunk * members + place
                store(whole[place * share : (place + 1) * share], row // parts, parts + row % parts)
            continue
        elif block == 2 * parts:
            whole = sum_proj[...]
        else:
            part = block - 2 * parts - 1
            whole = sum_qkv[:, part * width : (part + 1) * width]
        whole = whole.astype(BF16)
        for member in range(members):
            store(whole[member * share : (member + 1) * share], member, block)


def vector_sums(sum_vec):
    return jnp.sum(sum_vec[...].reshape(VECTORS, 8, sum_vec.shape[1]), axis=1).astype(BF16)


def clear(refs):
    for ref in refs:
        ref[...] = jnp.zeros_like(ref)


def kept_shapes(steps, width, hidden):
    return (
        ((steps * STEP, width), BF16, (STEP, width), 0),
        ((steps * STEP, 1), F32, (STEP, 1), 0),
        ((steps * STEP, 3 * width), BF16, (STEP, 3 * width), 0),
        ((steps * PROB_ROWS * (width // PAIR), S), BF16, (PROB_ROWS * (width // PAIR), S), 0),
        ((width, steps * STEP), BF16, (width, STEP), 1),
        ((steps * STEP, width), BF16, (STEP, width), 0),
        ((steps * STEP, 1), F32, (STEP, 1), 0),
        ((steps * STEP, hidden), BF16, (STEP, hidden), 0),
        ((steps * STEP, hidden), BF16, (STEP, hidden), 0),
    )


def sum_scratch(width, hidden):
    return [
        pltpu.VMEM((width, 3 * width), F32),
        pltpu.VMEM((width, width), F32),
        pltpu.VMEM((width, hidden), F32),
        pltpu.VMEM((width, hidden), F32),
        pltpu.VMEM((8 * VECTORS, width), F32),
    ]


def place():
    return lax.axis_index("section"), lax.axis_index("group"), lax.axis_index("member")


def remote(src, dst, send, recv, device):
    return pltpu.make_async_remote_copy(
        src_ref=src, dst_ref=dst, send_sem=send, recv_sem=recv, device_id=device, device_id_type=MESH
    )


def greet(peers):
    barrier = pltpu.get_barrier_semaphore()
    for peer in peers:
        pl.semaphore_signal(barrier, inc=1, device_id=peer, device_id_type=MESH)
    pl.semaphore_wait(barrier, len(peers))


def near_peers(members, sections):
    section, group, member = place()
    return [
        (lax.rem(section + ds, 2), group, lax.rem(member + dm, members))
        for ds in range(2)
        for dm in range(members)
        if (ds or dm) and (sections or not (ds and dm))
    ]


def far_peers(groups):
    section, group, member = place()
    return [
        (lax.rem(section + ds, 2), lax.rem(group + dg, groups), member)
        for ds in range(2)
        for dg in range(1, groups)
    ]


def rows_at(index, count):
    return pl.ds(pl.multiple_of(index * count, 16), count)


class Near:
    def __init__(self, members, count, width):
        self.members, self.count, self.width = members, count, width

    def source_shape(self):
        return (2, self.members * self.count, self.width)

    def scratch(self):
        return [
            pltpu.VMEM((self.members * self.count, self.width), BF16),
            pltpu.VMEM((self.members - 1, self.count, self.width), BF16),
        ] + [pltpu.SemaphoreType.DMA((n,)) for n in (1, 1, self.members, self.members)]

    def bind(self, refs, source):
        self.got, self.from_members, *self.sems = refs
        self.source = source
        return self

    def section_copy(self):
        section, group, member = place()
        return remote(
            self.source.at[1 - section], self.got, self.sems[0].at[0], self.sems[1].at[0], (1 - section, group, member)
        )

    def member_copy(self, offset):
        section, group, member = place()
        to = lax.rem(member + offset, self.members)
        return remote(
            self.got.at[rows_at(to, self.count)],
            self.from_members.at[offset - 1],
            self.sems[2].at[offset],
            self.sems[3].at[offset],
            (section, group, to),
        )

    def start_section(self):
        self.section_copy().start()

    def start_members(self):
        self.section_copy().wait()
        own = self.source[lax.axis_index("section")].astype(F32)
        self.got[...] = (self.got[...].astype(F32) + own).astype(BF16)
        for offset in range(1, self.members):
            self.member_copy(offset).start()

    def finish(self, out):
        for offset in range(1, self.members):
            self.member_copy(offset).wait()
        total = self.got[rows_at(lax.axis_index("member"), self.count), :].astype(F32)
        for offset in range(1, self.members):
            total = total + self.from_members[offset - 1].astype(F32)
        out[: self.count, :] = total.astype(BF16)
        spare = out.shape[0] - self.count
        if spare:
            out[self.count :, :] = jnp.zeros((spare, self.width), BF16)


class Far:
    def __init__(self, target, groups, count, width):
        self.target, self.groups, self.width = target, groups, width
        self.part = up16(-(-count // groups))

    def total_shape(self):
        return (self.groups * self.part, self.width)

    def result_shape(self):
        return (2, self.groups, self.part, self.width)

    def scratch(self):
        return [
            pltpu.VMEM((self.groups - 1, self.part, self.width), BF16),
            pltpu.VMEM((self.part, self.width), BF16),
            pltpu.SemaphoreType.DMA,
        ] + [pltpu.SemaphoreType.DMA((n,)) for n in (self.groups,) * 2 + (2 * self.groups,) * 2]

    def bind(self, refs, total, result):
        self.from_groups, self.piece, self.local, *self.sems = refs
        self.total, self.result_ref = total, result
        return self

    def group_copy(self, offset):
        section, group, member = place()
        to = lax.rem(group + offset, self.groups)
        return remote(
            self.total.at[rows_at(to, self.part)],
            self.from_groups.at[offset - 1],
            self.sems[0].at[offset],
            self.sems[1].at[offset],
            (section, to, member),
        )

    def gather_copy(self, offset, across):
        section, group, member = place()
        slot = across * self.groups + offset
        return remote(
            self.piece,
            self.result_ref.at[section, group],
            self.sems[2].at[slot],
            self.sems[3].at[slot],
            (self.target, lax.rem(group + offset, self.groups), member),
        )

    def gathered(self, offset, across):
        section, group, member = place()
        slot = across * self.groups + offset
        origin = lax.rem(group + self.groups - offset, self.groups)
        half = 1 - section if across else section
        return remote(
            self.piece,
            self.result_ref.at[half, origin],
            self.sems[2].at[slot],
            self.sems[3].at[slot],
            (self.target, origin, member),
        )

    def start_groups(self):
        for offset in range(1, self.groups):
            self.group_copy(offset).start()

    def start_gather(self):
        section, group, member = place()
        for offset in range(1, self.groups):
            self.group_copy(offset).wait()
        total = self.total[rows_at(group, self.part), :].astype(F32)
        for offset in range(1, self.groups):
            total = total + self.from_groups[offset - 1].astype(F32)
        self.piece[...] = total.astype(BF16)

        @pl.when(section == self.target)
        def _():
            for offset in range(1, self.groups):
                self.gather_copy(offset, 0).start()
            keep = pltpu.make_async_copy(self.piece, self.result_ref.at[section, group], self.local)
            keep.start()
            keep.wait()

        @pl.when(section != self.target)
        def _():
            for offset in range(self.groups):
                self.gather_copy(offset, 1).start()

    def finish(self):
        section, group, member = place()

        @pl.when(section == self.target)
        def _():
            for offset in range(1, self.groups):
                self.gather_copy(offset, 0).wait_send()
                self.gathered(offset, 0).wait_recv()
            for offset in range(self.groups):
                self.gathered(offset, 1).wait_recv()

        @pl.when(section != self.target)
        def _():
            for offset in range(self.groups):
                self.gather_copy(offset, 1).wait_send()


class VectorSum:
    def __init__(self, groups, members, width):
        self.groups, self.members, self.width = groups, members, width

    def scratch(self):
        return [
            pltpu.VMEM((2 * self.members, VECTORS, self.width), BF16),
            pltpu.VMEM((self.groups, VECTORS, self.width), BF16),
            pltpu.VMEM((VECTORS, self.width), BF16),
            pltpu.VMEM((VECTORS, self.width), BF16),
        ] + [pltpu.SemaphoreType.DMA((n,)) for n in (2 * self.members,) * 2 + (self.groups,) * 2]

    def bind(self, refs):
        self.near, self.far, self.own, self.middle = refs[:4]
        self.sems = refs[4:]
        return self

    def near_copy(self, offset):
        section, group, member = place()
        ds, dm = divmod(offset, self.members)
        to = lax.rem(section + ds, 2), group, lax.rem(member + dm, self.members)
        return remote(
            self.own, self.near.at[section * self.members + member], self.sems[0].at[offset], self.sems[1].at[offset], to
        )

    def near_got(self, offset):
        section, group, member = place()
        ds, dm = divmod(offset, self.members)
        origin = lax.rem(section + ds, 2), lax.rem(member + self.members - dm, self.members)
        return remote(
            self.own,
            self.near.at[origin[0] * self.members + origin[1]],
            self.sems[0].at[offset],
            self.sems[1].at[offset],
            (origin[0], group, origin[1]),
        )

    def far_copy(self, offset):
        section, group, member = place()
        to = section, lax.rem(group + offset, self.groups), member
        return remote(self.middle, self.far.at[group], self.sems[2].at[offset], self.sems[3].at[offset], to)

    def far_got(self, offset):
        section, group, member = place()
        origin = lax.rem(group + self.groups - offset, self.groups)
        return remote(
            self.middle, self.far.at[origin], self.sems[2].at[offset], self.sems[3].at[offset], (section, origin, member)
        )

    def start(self, values):
        section, group, member = place()
        self.own[...] = values
        self.near[section * self.members + member] = values
        for offset in range(1, 2 * self.members):
            self.near_copy(offset).start()

    def start_far(self):
        for offset in range(1, 2 * self.members):
            self.near_copy(offset).wait_send()
            self.near_got(offset).wait_recv()
        total = jnp.zeros((VECTORS, self.width), F32)
        for index in range(2 * self.members):
            total = total + self.near[index].astype(F32)
        self.middle[...] = total.astype(BF16)
        self.far[lax.axis_index("group")] = total.astype(BF16)
        for offset in range(1, self.groups):
            self.far_copy(offset).start()

    def finish(self):
        for offset in range(1, self.groups):
            self.far_copy(offset).wait_send()
            self.far_got(offset).wait_recv()
        total = jnp.zeros((VECTORS, self.width), F32)
        for index in range(self.groups):
            total = total + self.far[index].astype(F32)
        return total


def take(refs, *counts):
    out, at = [], 0
    for count in counts:
        out.append(list(refs[at : at + count]))
        at += count
    assert at == len(refs)
    return out


def params(collective):
    return pltpu.CompilerParams(vmem_limit_bytes=62 * MIB, collective_id=collective, has_side_effects=True)


def cost(flops, moved):
    return pl.CostEstimate(flops=flops, bytes_accessed=moved * MIB, transcendentals=0)


def block_at(shape, axis, index):
    return pl.BlockSpec(shape, lambda i: tuple(index(i) if d == axis else 0 for d in range(len(shape))))


def fixed(shape):
    return pl.BlockSpec(shape, lambda i: (0,) * len(shape), pipeline_mode=pl.Buffered(1))


ANYWHERE = pl.BlockSpec(memory_space=pl.ANY)


def first_forward(tokens, seg, vectors, own, steps):
    width, hidden = tokens.shape[1], own[2].shape[2]
    shapes = kept_shapes(steps, width, hidden)
    held = [((2, VECTORS, width), F32)] + [((2,) + w.shape[1:], w.dtype) for w in own]
    count = len(own)

    def body(x, seg, *refs):
        vectors_in, own, (y,), kept, weights, held, sems = take(
            refs, len(vectors), count, 1, len(shapes), count + 1, count + 1, 5
        )
        load, send, recv, out, _ = sems
        step = pl.program_id(0)
        section, group, member = place()
        partner = (1 - section, group, member)
        order = list(range(count + 1))

        def own_load(i):
            return pltpu.make_async_copy(own[i - 1].at[0], held[i].at[section], load.at[i])

        def push(i, whose):
            source = own[i - 1].at[0] if i else held[0].at[whose]
            return remote(source, held[i].at[whose], send.at[i], recv.at[i], partner)

        def layer_zero(which):
            @pl.when(section == 0)
            def _():
                for i in which:
                    if i:
                        own_load(i).wait()

            @pl.when(section == 1)
            def _():
                for i in which:
                    push(i, 1 - section).wait_recv()

        def store(i):
            return pltpu.make_async_copy(held[i], weights[i], out.at[i])

        @pl.when(step == 0)
        def _():
            for i in order[1:]:
                own_load(i).start()
            row = 0
            for vector_in in vectors_in:
                for part in range(vector_in.shape[1] // width):
                    held[0][section, row : row + 1, :] = vector_in[:, part * width : (part + 1) * width]
                    row += 1
            held[0][section, row:, :] = jnp.zeros((VECTORS - row, width), F32)
            greet([partner])
            for i in order:
                push(i, section).start()
            layer_zero(order[:2])

        @pl.when(step == 1)
        def _():
            @pl.when(section == 0)
            def _():
                for i in order:
                    push(i, 1 - section).wait_recv()

            @pl.when(section == 1)
            def _():
                for i in order[1:]:
                    own_load(i).wait()

            for i in order:
                store(i).start()

        def after_attention():
            @pl.when(step == 0)
            def _():
                layer_zero(order[2:])

        forward(x, seg, held, kept, y, after_attention)

        @pl.when(step == steps - 1)
        def _():
            for i in order:
                store(i).wait()
                push(i, section).wait_send()

    def mine(i):
        return lax.axis_index("section") * steps + i

    return pl.pallas_call(
        body,
        grid=(steps,),
        in_specs=[block_at((STEP, width), 0, mine), block_at((1, STEP), 1, mine)]
        + [fixed(v.shape) for v in vectors]
        + [ANYWHERE] * count,
        out_specs=[block_at((STEP, width), 0, lambda i: i)]
        + [block_at(block, axis, lambda i: i) for _, _, block, axis in shapes]
        + [ANYWHERE] * (count + 1),
        out_shape=[jax.ShapeDtypeStruct((steps * STEP, width), BF16)]
        + [jax.ShapeDtypeStruct(shape, dtype) for shape, dtype, _, _ in shapes]
        + [jax.ShapeDtypeStruct(shape, dtype) for shape, dtype in held],
        scratch_shapes=[pltpu.VMEM(shape, dtype) for shape, dtype in held]
        + [pltpu.SemaphoreType.DMA((count + 1,))] * 5,
        compiler_params=params(0),
        cost_estimate=cost(steps * STEP * 4000000, 40),
        name="forward_first",
    )(tokens, seg, *vectors, *own)


def block_lists(parts):
    fc1, fc2, proj = list(range(parts)), list(range(parts, 2 * parts)), 2 * parts
    qkv = [proj + 1, proj + 2, proj + 3]
    upper = (fc2 + fc1[: parts // 2], fc1[parts // 2 :] + [proj] + qkv)
    lower = (fc2, fc1 + [proj], qkv)
    return upper, lower


def second_layer(x, seg, cotangent, weights, steps, groups, members):
    width, hidden = x.shape[1], weights[3].shape[2]
    shapes = kept_shapes(steps, width, hidden)
    size = half_rows(width // members)
    early, late = block_lists(hidden // width)[0]
    near = Near(members, len(early) * size, width)
    far = Far(1, groups, len(early) * size, width)
    late_shape = Near(members, len(late) * size, width).source_shape()

    def body(x, seg, cot, vec, w_qkv, w_proj, w_fc1, w_fc2, *refs):
        outs, sums, attn_kept, mlp_kept, rest, sems, near_refs = take(
            refs, 6, 5, 4, 5, 6, 2, len(near.scratch())
        )
        y_own, y_got, g, late_out, total_out, vec_out = outs
        grad_after, grad_context, grad_qkv, y, y_send, early_out = rest
        send, recv = sems
        near.bind(near_refs, early_out)
        weights = (vec, w_qkv, w_proj, w_fc1, w_fc2)
        step = pl.program_id(0)
        section, group, member = place()

        def y_copy(index):
            return remote(
                y_send.at[index], y_got.at[rows_at(index, STEP)], send.at[index], recv.at[index], (1 - section, group, member)
            )

        @pl.when(step == 0)
        def _():
            clear(sums)
            greet(near_peers(members, False))

        @pl.when(step < steps)
        def _():
            forward(x, seg, weights, [ref.at[step] for ref in attn_kept] + mlp_kept, y)
            y_own[...] = jnp.where(section == 0, x[...], y[...])
            y_send[step] = jnp.where(section == 0, y[...], x[...])
            y_copy(step).start()

            def write(after, context):
                grad_after[step] = after
                grad_context[step] = context

            backward_mlp(cot, weights, mlp_kept, sums, write)

        @pl.when(step == steps - 1)
        def _():
            write_blocks(sums, members, early, early_out)
            near.start_section()

        @pl.when(step >= steps)
        def _():
            index = step - steps

            def write(values):
                g[...] = values.astype(BF16)

            def halfway():
                @pl.when(step == steps)
                def _():
                    near.start_members()

            backward_attn(
                grad_after.at[index], grad_context.at[index], seg, weights,
                [ref.at[index] for ref in attn_kept], sums, grad_qkv, write, halfway,
            )

        @pl.when(step == 2 * steps - 1)
        def _():
            write_blocks(sums, members, late, late_out)
            vec_out[...] = vector_sums(sums[4])
            for index in range(steps):
                y_copy(index).wait()
            near.finish(total_out)

    def mine(index):
        return lambda i: lax.axis_index("section") * steps + index(i)

    def first(i):
        return jnp.minimum(i, steps - 1)

    def then(i):
        return jnp.maximum(i - steps, 0)

    rows = jax.ShapeDtypeStruct((steps * STEP, width), BF16)
    fixed_outs = [late_shape, far.total_shape(), (VECTORS, width)]
    return pl.pallas_call(
        body,
        grid=(2 * steps,),
        in_specs=[
            block_at((STEP, width), 0, first),
            block_at((1, STEP), 1, mine(lambda i: lax.rem(i, steps))),
            block_at((STEP, width), 0, mine(first)),
        ]
        + [pl.BlockSpec((1,) + w.shape[1:], lambda i: (1, 0, 0), pipeline_mode=pl.Buffered(1)) for w in weights],
        out_specs=[block_at((STEP, width), 0, first), ANYWHERE, block_at((STEP, width), 0, then)]
        + [fixed(shape) for shape in fixed_outs],
        out_shape=[rows] * 3 + [jax.ShapeDtypeStruct(shape, BF16) for shape in fixed_outs],
        scratch_shapes=sum_scratch(width, hidden)
        + [pltpu.VMEM((steps,) + block, dtype) for _, dtype, block, _ in shapes[:4]]
        + [pltpu.VMEM(block, dtype) for _, dtype, block, _ in shapes[4:]]
        + [
            pltpu.VMEM((steps, STEP, width), F32),
            pltpu.VMEM((steps, STEP, width), BF16),
            pltpu.VMEM((STEP, 3 * width), BF16),
            pltpu.VMEM((STEP, width), BF16),
            pltpu.VMEM((steps, STEP, width), BF16),
            pltpu.VMEM(near.source_shape(), BF16),
        ]
        + [pltpu.SemaphoreType.DMA((steps,))] * 2
        + near.scratch(),
        compiler_params=params(1),
        cost_estimate=cost(steps * STEP * 12000000, 20),
        name="second_layer",
    )(x, seg, cotangent, *weights)


def first_backward(seg, dout, late1, total1, vec1, kept, weights, steps, groups, members):
    width, hidden = dout.shape[1], weights[3].shape[2]
    shapes = kept_shapes(steps, width, hidden)
    size = half_rows(width // members)
    (upper_early, upper_late), lower = block_lists(hidden // width)
    fars = [
        Far(target, groups, len(blocks) * size, width)
        for target, blocks in [(1, upper_early), (1, upper_late)] + [(0, blocks) for blocks in lower]
    ]
    nears = [Near(members, len(blocks) * size, width) for blocks in (upper_late,) + lower]
    vector_plans = [VectorSum(groups, members, width) for _ in range(2)]
    plans = fars + nears + vector_plans

    def body(seg, dout, vec, w_qkv, w_proj, w_fc1, w_fc2, *refs):
        kept, (late1, total1, vec1), (g_own, g_got), results, vec_outs, sums, rest, sources, totals, sems, *bound = take(
            refs, 9, 3, 2, 5, 2, 5, 4, 3, 4, 2, *[len(plan.scratch()) for plan in plans]
        )
        grad_after, grad_context, grad_qkv, g_send = rest
        send, recv = sems
        for plan, plan_refs, total, result in zip(fars, bound[:5], [total1] + list(totals), results):
            plan.bind(plan_refs, total, result)
        for plan, plan_refs, source in zip(nears, bound[5:9], [late1] + list(sources)):
            plan.bind(plan_refs, source)
        for plan, plan_refs in zip(vector_plans, bound[9:]):
            plan.bind(plan_refs)
        far_a, far_b, far_fc2, far_fc1, far_qkv = fars
        near_b, near_fc2, near_fc1, near_qkv = nears
        total_b, total_fc2, total_fc1, total_qkv = totals
        upper_vec, lower_vec = vector_plans
        weights = (vec, w_qkv, w_proj, w_fc1, w_fc2)
        xhat1, r1, qkv, prob, ctx_t, xhat2, r2, act, dgelu = kept
        step = pl.program_id(0)
        section, group, member = place()

        def g_copy(index):
            return remote(
                g_send.at[index], g_got.at[rows_at(index, STEP)], send.at[index], recv.at[index], (1 - section, group, member)
            )

        @pl.when(step == 0)
        def _():
            greet(near_peers(members, True) + far_peers(groups))
            near_b.start_section()
            far_a.start_groups()
            upper_vec.start(vec1[...])
            clear(sums)

        @pl.when(step == steps)
        def _():
            near_b.start_members()

        @pl.when(step == steps + 1)
        def _():
            near_fc2.start_members()
            far_a.start_gather()
            upper_vec.start_far()

        @pl.when(step == 2 * steps)
        def _():
            near_b.finish(total_b)
            far_b.start_groups()
            vec_outs[0][...] = upper_vec.finish()

        @pl.when(step == 2 * steps + 1)
        def _():
            near_fc1.start_members()

        @pl.when(step == 2 * steps + 2)
        def _():
            near_fc2.finish(total_fc2)
            far_fc2.start_groups()
            far_b.start_gather()

        @pl.when(step == 2 * steps + 3)
        def _():
            far_fc2.start_gather()

        @pl.when(step < steps)
        def _():
            g_send[step] = dout[...]
            backward_fc2(dout, act, sums)

        @pl.when(step == steps - 1)
        def _():
            write_blocks(sums, members, lower[0], near_fc2.source)
            near_fc2.start_section()

        @pl.when(jnp.logical_and(step >= steps, step < 2 * steps))
        def _():
            index = step - steps

            def write(after, context):
                grad_after[index] = after
                grad_context[index] = context

            backward_mlp(g_send.at[index], weights, (ctx_t, xhat2, r2, None, dgelu), sums, write, False)

        @pl.when(step == 2 * steps - 1)
        def _():
            write_blocks(sums, members, lower[1], near_fc1.source)
            near_fc1.start_section()

        @pl.when(step >= 2 * steps)
        def _():
            index = step - 2 * steps

            def write(values):
                low = values.astype(BF16)
                upper_rows = g_send[index]
                g_own[...] = jnp.where(section == 0, low, upper_rows)
                g_send[index] = jnp.where(section == 0, upper_rows, low)
                g_copy(index).start()

            backward_attn(
                grad_after.at[index], grad_context.at[index], seg, weights, (xhat1, r1, qkv, prob), sums, grad_qkv, write
            )

        @pl.when(step == 3 * steps - 1)
        def _():
            write_blocks(sums, members, lower[2], near_qkv.source)
            near_qkv.start_section()
            lower_vec.start(vector_sums(sums[4]))
            near_fc1.finish(total_fc1)
            far_fc1.start_groups()
            near_qkv.start_members()
            lower_vec.start_far()
            far_fc1.start_gather()
            for index in range(steps):
                g_copy(index).wait()
            far_a.finish()
            far_b.finish()
            far_fc2.finish()
            vec_outs[1][...] = lower_vec.finish()
            near_qkv.finish(total_qkv)
            far_qkv.start_groups()
            far_qkv.start_gather()
            far_fc1.finish()
            far_qkv.finish()

    def phase(number):
        return lambda i: jnp.clip(i - number * steps, 0, steps - 1)

    def kept_spec(number, entry):
        _, _, block, axis = entry
        return block_at(block, axis, phase(number))

    phases = (2, 2, 2, 2, 1, 1, 1, 0, 1)
    low_rows = jax.ShapeDtypeStruct((steps * STEP, width), BF16)
    vec_shape = (VECTORS, width)
    return pl.pallas_call(
        body,
        grid=(3 * steps,),
        in_specs=[
            block_at((1, STEP), 1, lambda i: lax.axis_index("section") * steps + phase(2)(i)),
            block_at((STEP, width), 0, phase(0)),
        ]
        + [fixed((1,) + w.shape[1:]) for w in weights]
        + [kept_spec(number, entry) for number, entry in zip(phases, shapes)]
        + [fixed(late1.shape), fixed(total1.shape), fixed(vec_shape)],
        out_specs=[block_at((STEP, width), 0, phase(2)), ANYWHERE] + [ANYWHERE] * 5 + [fixed(vec_shape)] * 2,
        out_shape=[low_rows] * 2
        + [jax.ShapeDtypeStruct(far.result_shape(), BF16) for far in fars]
        + [jax.ShapeDtypeStruct(vec_shape, F32)] * 2,
        scratch_shapes=sum_scratch(width, hidden)
        + [
            pltpu.VMEM((steps, STEP, width), F32),
            pltpu.VMEM((steps, STEP, width), BF16),
            pltpu.VMEM((STEP, 3 * width), BF16),
            pltpu.VMEM((steps, STEP, width), BF16),
        ]
        + [pltpu.VMEM(near.source_shape(), BF16) for near in nears[1:]]
        + [pltpu.VMEM(far.total_shape(), BF16) for far in fars[1:]]
        + [pltpu.SemaphoreType.DMA((steps,))] * 2
        + [item for plan in plans for item in plan.scratch()],
        compiler_params=params(2),
        cost_estimate=cost(steps * STEP * 8000000, 40),
        name="backward_first",
    )(seg, dout, *weights, *kept, late1, total1, vec1)


def finish(y_own, y_got, g_own, g_got, results, vec_sums, width, hidden, steps, members):
    parts = hidden // width
    share = width // members
    size = half_rows(share)
    upper, lower = block_lists(parts)
    lists = list(upper) + list(lower)
    results = [result.reshape(2, -1, width) for result in results]
    at = jnp.stack([lax.axis_index("section"), lax.axis_index("member")]).astype(jnp.int32)

    def body(s, y_own, y_got, g_own, g_got, *refs):
        results, (upper_vec, lower_vec), (acts, grads), outs = take(refs, 5, 2, 2, 12)
        a_gain, a_shift, d_qkv, d_qv, d_proj, b_proj, m_gain, m_shift, d_fc1, b_fc1, d_fc2, b_fc2 = outs
        step = pl.program_id(0)
        first = s[0] == 0
        mine = step // steps == s[0]
        acts[0] = jnp.where(mine, y_own[...], y_got[...])
        grads[0] = jnp.where(mine, g_own[...], g_got[...]).astype(F32)

        def rows_of(which, block, half):
            for blocks, result in list(zip(lists, results))[which]:
                if block in blocks:
                    top = blocks.index(block) * size
                    return result[half, top : top + size, :].astype(F32)
            raise KeyError(block)

        @pl.when(step == 0)
        def _():
            for block in range(2 * parts + 4):
                for half in range(2):
                    top = half * (share - size)
                    rows = jnp.where(first, rows_of(slice(2, 5), block, half), rows_of(slice(0, 2), block, half))
                    if block < parts:
                        d_fc1[0, top : top + size, block * width : (block + 1) * width] = rows
                    elif block < 2 * parts:
                        base = (block - parts) * share + top
                        d_fc2[0, base : base + size, :] = rows
                    elif block == 2 * parts:
                        d_proj[0, top : top + size, :] = rows
                    else:
                        left = (block - 2 * parts - 1) * width
                        d_qkv[0, top : top + size, left : left + width] = rows
            vectors = jnp.where(first, lower_vec[...], upper_vec[...])

            def put(out, row, count=1):
                flat = jnp.concatenate([vectors[row + i : row + i + 1, :] for i in range(count)], axis=1)
                length = count * width // members
                value = flat[:, :length]
                for m in range(1, members):
                    value = jnp.where(s[1] == m, flat[:, m * length : (m + 1) * length], value)
                out[...] = value

            put(a_gain, ATTN_GAIN)
            put(a_shift, ATTN_SHIFT)
            put(d_qv, Q_BIAS, 2)
            put(b_proj, PROJ_BIAS)
            put(m_gain, MLP_GAIN)
            put(m_shift, MLP_SHIFT)
            put(b_fc1, FC1_BIAS, parts)
            put(b_fc2, FC2_BIAS)

    def whole(shape):
        return pl.BlockSpec(shape, lambda i, s, n=len(shape): (0,) * n)

    own = pl.BlockSpec((STEP, width), lambda i, s: (jnp.clip(i - s[0] * steps, 0, steps - 1), 0))
    got = pl.BlockSpec((STEP, width), lambda i, s: (jnp.clip(i - (1 - s[0]) * steps, 0, steps - 1), 0))
    total = 2 * steps * STEP
    smalls = [
        (1, share), (1, share), (1, share, 3 * width), (1, 2 * share), (1, share, width), (1, share), (1, share),
        (1, share), (1, share, hidden), (1, hidden // members), (1, hidden // members, width), (1, share),
    ]
    rows_spec = pl.BlockSpec((1, STEP, width), lambda i, s: (0, i, 0))
    inputs = results + list(vec_sums)
    return pl.pallas_call(
        body,
        grid_spec=pltpu.PrefetchScalarGridSpec(
            num_scalar_prefetch=1,
            grid=(2 * steps,),
            in_specs=[own, got, own, got] + [whole(x.shape) for x in inputs],
            out_specs=[rows_spec, rows_spec] + [whole(shape) for shape in smalls],
        ),
        out_shape=[
            jax.ShapeDtypeStruct((1, total, width), BF16),
            jax.ShapeDtypeStruct((1, total, width), F32),
        ]
        + [jax.ShapeDtypeStruct(shape, F32) for shape in smalls],
        compiler_params=pltpu.CompilerParams(vmem_limit_bytes=62 * MIB),
        cost_estimate=cost(0, 16),
        name="finish",
    )(at, y_own, y_got, g_own, g_got, *inputs)


def per_device(
    tokens,
    segment,
    cotangent,
    attn_gain,
    attn_shift,
    qkv_weight,
    qv_bias,
    proj_weight,
    proj_bias,
    mlp_gain,
    mlp_shift,
    fc1_weight,
    fc1_bias,
    fc2_weight,
    fc2_bias,
):
    groups, members = lax.axis_size("group"), lax.axis_size("member")
    rows, width = tokens.shape
    hidden = fc1_weight.shape[2]
    steps = rows // 2 // STEP
    seg = segment.reshape(1, rows)
    vectors = (attn_gain, attn_shift, qv_bias, proj_bias, mlp_gain, mlp_shift, fc2_bias, fc1_bias)
    y0, *rest = first_forward(
        tokens, seg, vectors, [qkv_weight, proj_weight, fc1_weight, fc2_weight], steps
    )
    kept, weights = rest[:9], rest[9:]
    y_own, y_got, g1, late1, total1, vec1 = second_layer(y0, seg, cotangent, weights, steps, groups, members)
    g_own, g_got, *grads = first_backward(seg, g1, late1, total1, vec1, kept, weights, steps, groups, members)
    return tuple(finish(y_own, y_got, g_own, g_got, grads[:5], grads[5:], width, hidden, steps, members))


def solution(mesh):
    row = P("section", None)
    mat = P("section", None, None)
    tokens = P(("group", "member"), None)
    split = P("section", "member")
    split_mat = P("section", "member", None)
    stacked = P("section", ("group", "member"), None)
    return jax.shard_map(
        per_device,
        mesh=mesh,
        in_specs=(
            tokens, P(("group", "member")), tokens,
            row, row, mat, row, mat, row, row, row, mat, row, mat, row,
        ),
        out_specs=(
            stacked, stacked,
            split, split, split_mat, split, split_mat, split, split, split, split_mat, split, split_mat, split,
        ),
        check_vma=False,
    )
```

```python
import jax
import jax.numpy as jnp
from jax import lax
from jax.experimental import pallas as pl
from jax.experimental.pallas import tpu as pltpu
from jax.sharding import PartitionSpec as P

HD = 64
S = 256
HALF = S // 2
GLOBAL_LEN = 197
LOCAL_LEN = 37
PAIR = 2 * HD
STEP = 2 * S
EPS = 1e-06
SCALE = HD ** (-0.5)
LOG2E = 1.4426950408889634
CHUNK = 768
FORWARD_CHUNK = 256
DEPTH = 4
F32 = jnp.float32
BF16 = jnp.bfloat16
MIB = 1 << 20
MESH = pl.DeviceIdType.MESH

ATTN_GAIN, ATTN_SHIFT, Q_BIAS, V_BIAS, PROJ_BIAS, MLP_GAIN, MLP_SHIFT, FC2_BIAS, FC1_BIAS = range(9)
VECTORS = 16


def up16(value):
    return -(-value // 16) * 16


def key_windows(local):
    if not local:
        return ((0, up16(GLOBAL_LEN)),) * 2
    first_end = ((HALF - 1) // LOCAL_LEN + 1) * LOCAL_LEN
    second_start = HALF // LOCAL_LEN * LOCAL_LEN // 16 * 16
    return ((0, up16(first_end)), (second_start, up16(S // LOCAL_LEN * LOCAL_LEN)))


WINDOWS = tuple((local, key_windows(local)) for local in (False, True))
PROB_ROWS = sum(hi - lo for _, windows in WINDOWS for lo, hi in windows)


def prob_offset(pair, sequence, block):
    spans = [hi - lo for _, windows in WINDOWS for lo, hi in windows]
    return pair * PROB_ROWS + sum(spans[: 2 * sequence + block])


def nn(left, right):
    return jnp.dot(left, right, preferred_element_type=F32)


def nt(left, right):
    return lax.dot_general(left, right, (((1,), (1,)), ((), ())), preferred_element_type=F32)


def tn(left, right):
    return lax.dot_general(left, right, (((0,), (0,)), ((), ())), preferred_element_type=F32)


def column_sums(values):
    return jnp.sum(values.reshape(values.shape[0] // 8, 8, values.shape[1]), axis=0)


def normalized(values):
    centered = values - jnp.mean(values, axis=1, keepdims=True)
    inverse = lax.rsqrt(jnp.mean(centered * centered, axis=1, keepdims=True) + EPS)
    return centered * inverse, inverse


def norm_back(scaled, inverse, gain, grad):
    grad_scaled = grad * gain
    first = jnp.mean(grad_scaled, axis=1, keepdims=True)
    second = jnp.mean(grad_scaled * scaled, axis=1, keepdims=True)
    return inverse * (grad_scaled - first - scaled * second)


def crop_of(index):
    total = jnp.zeros_like(index)
    for crop in range(1, S // LOCAL_LEN + 1):
        total = total + (index >= crop * LOCAL_LEN).astype(jnp.int32)
    return total


def mask_bias(local, block, lo, hi):
    if not local:
        rows = lax.broadcasted_iota(jnp.int32, (hi - lo, HALF), 0) + lo
        return jnp.where(rows < GLOBAL_LEN, 0.0, -1e30)
    keys = crop_of(lax.broadcasted_iota(jnp.int32, (hi - lo, HALF), 0) + lo)
    queries = crop_of(lax.broadcasted_iota(jnp.int32, (hi - lo, HALF), 1) + block * HALF)
    return jnp.where(keys == queries, 0.0, -1e30)


def split_pair(rows):
    lane = lax.broadcasted_iota(jnp.int32, (1, PAIR), 1)
    first = (lane < HD).astype(rows.dtype)
    second = (lane >= HD).astype(rows.dtype)
    return jnp.concatenate([rows * first, rows * second], axis=0)


def padded(rows, lo, hi):
    parts = [rows]
    if lo:
        parts = [jnp.zeros((lo, rows.shape[1]), rows.dtype)] + parts
    if hi < S:
        parts = parts + [jnp.zeros((S - hi, rows.shape[1]), rows.dtype)]
    return jnp.concatenate(parts, axis=0) if len(parts) > 1 else rows


def diagonal(values):
    return jnp.concatenate([values[:HD, :HALF], values[HD:, HALF:]], axis=0)


def units_of(width):
    return [(sequence, pair, block) for sequence in range(2) for pair in range(width // PAIR) for block in range(2)]


def pipelined(units, depth, stages):
    held = [{} for _ in stages]
    for now in range(len(units) + depth * (len(stages) - 1)):
        for i, stage in enumerate(stages):
            at = now - i * depth
            if 0 <= at < len(units):
                before = [held[i - 1].pop(at)] if i else []
                held[i][at] = stage(units[at], *before)


class Once(dict):
    def get_or(self, key, make):
        if key not in self:
            self[key] = make()
        return self[key]


def place_of(unit):
    sequence, pair, block = unit
    lo, hi = WINDOWS[sequence][1][block]
    return sequence * S, pair * PAIR, block * HALF, lo, hi


def attend(seg, qkv, prob, ctx_t, width):
    once = Once()

    def valid_of(unit):
        base, _, at, _, _ = place_of(unit)
        return seg[0:1, base + at : base + at + HALF] >= 0

    def values_of(unit):
        base, left, _, _, _ = place_of(unit)
        cols = slice(2 * width + left, 2 * width + left + PAIR)
        return once.get_or(unit[:2], lambda: qkv[base : base + S, cols].T)

    def bias_of(unit):
        sequence, _, block = unit
        _, _, _, lo, hi = place_of(unit)

        def make():
            bias = mask_bias(WINDOWS[sequence][0], block, lo, hi)
            return jnp.concatenate([bias, bias], axis=1)

        return once.get_or(("bias", sequence, block), make)

    def raw_scores(unit):
        base, left, at, lo, hi = place_of(unit)
        values_of(unit)
        keys = qkv[base + lo : base + hi, width + left : width + left + PAIR]
        return nt(keys, split_pair(qkv[base + at : base + at + HALF, left : left + PAIR]))

    def softmax(unit, raw):
        sequence, pair, block = unit
        _, _, _, lo, hi = place_of(unit)
        scores = raw * (SCALE * LOG2E)
        cut = 0 if WINDOWS[sequence][0] else GLOBAL_LEN // 16 * 16 - lo
        tail = scores[cut:] + bias_of(unit)[cut:]
        scores = jnp.concatenate([scores[:cut], tail], axis=0) if cut else tail
        exponent = jnp.exp2(scores - jnp.max(scores, axis=0, keepdims=True))
        total = jnp.sum(exponent, axis=0, keepdims=True)
        valid = valid_of(unit)
        inverse = jnp.where(jnp.concatenate([valid, valid], axis=1), 1.0 / total, 0.0)
        probs = (exponent * inverse).astype(BF16)
        offset = prob_offset(pair, sequence, block)
        prob[offset : offset + hi - lo, :] = probs
        return probs

    def context(unit, probs):
        base, left, at, lo, hi = place_of(unit)
        values_t = values_of(unit)
        mixed = diagonal(nn(values_t, padded(probs, lo, hi)))
        own = values_t[:, at : at + HALF].astype(F32)
        ctx_t[left : left + PAIR, base + at : base + at + HALF] = jnp.where(
            valid_of(unit), mixed, own
        ).astype(BF16)

    pipelined(units_of(width), DEPTH, [raw_scores, softmax, context])


def span(start, size):
    return pl.ds(start if isinstance(start, int) else pl.multiple_of(start, PAIR), size)


def attend_back(seg, qkv, prob, grad_context, grad_qkv, pairs, sequences, place_in):
    once = Once()
    width = qkv.shape[1] // 3
    per_step = PROB_ROWS * (width // PAIR)

    def rows_of(unit):
        sequence, slot, block = unit
        lo, hi = WINDOWS[sequence % 2][1][block]
        return sequence * S, block * HALF, lo, hi

    def pair_of(unit):
        return pairs[unit[1]]

    def columns(unit, part):
        return span(part * width + pair_of(unit) * PAIR, PAIR)

    def padding_of(unit):
        base = unit[0] * S

        def make():
            valid = (seg[0:1, base : base + S] >= 0).astype(jnp.int32)
            count = jnp.sum(valid, axis=1, keepdims=True)
            return lax.broadcasted_iota(jnp.int32, (S, PAIR), 0) >= count

        return once.get_or(("padding", unit[0]), make)

    def keys_of(unit):
        base = unit[0] * S
        return once.get_or(("keys", unit[:2]), lambda: qkv[base : base + S, columns(unit, 1)].T)

    def grads_of(unit):
        base, at, _, _ = rows_of(unit)
        rows = slice(base + at, base + at + HALF)
        return once.get_or(("grads", unit), lambda: split_pair(grad_context[rows, columns(unit, 0)]))

    def grad_probs(unit):
        base, _, lo, hi = rows_of(unit)
        keys_of(unit)
        return nt(qkv[base + lo : base + hi, columns(unit, 2)], grads_of(unit))

    def grad_scores(unit, grads):
        sequence, _, block = unit
        _, _, lo, hi = rows_of(unit)
        start = sequence // 2 * per_step + prob_offset(0, sequence % 2, block)
        pair = pair_of(unit)
        start = start + pair * PROB_ROWS if isinstance(pair, int) else pl.multiple_of(start + pair * PROB_ROWS, 16)
        probs_low = prob[pl.ds(start, hi - lo), :]
        probs = probs_low.astype(F32)
        product = probs * grads
        inner = jnp.sum(product, axis=0, keepdims=True)
        return (product - probs * inner).astype(BF16), probs_low

    def grad_rows(unit, given):
        grad_raw, probs_low = given
        base, at, lo, hi = rows_of(unit)
        pair = pair_of(unit)
        queries = split_pair(qkv[base + at : base + at + HALF, columns(unit, 0)])
        grad_values = padded(nn(probs_low, grads_of(unit)), lo, hi)
        grad_keys = padded(nn(grad_raw, queries), lo, hi)
        grad_queries = diagonal(nn(keys_of(unit), padded(grad_raw, lo, hi))) * SCALE
        grad_qkv[base + at : base + at + HALF, span(place_in(0, pair), PAIR)] = grad_queries.astype(BF16).T
        if unit[2] == 0:
            once["first", unit[:2]] = grad_values, grad_keys
            return
        other_values, other_keys = once["first", unit[:2]]
        own = jnp.where(padding_of(unit), grad_context[base : base + S, columns(unit, 0)].astype(F32), 0.0)
        grad_qkv[base : base + S, span(place_in(1, pair), PAIR)] = ((other_keys + grad_keys) * SCALE).astype(BF16)
        grad_qkv[base : base + S, span(place_in(2, pair), PAIR)] = (other_values + grad_values + own).astype(BF16)

    units = [(q, slot, block) for q in range(sequences) for slot in range(len(pairs)) for block in range(2)]
    pipelined(units, DEPTH, [grad_probs, grad_scores, grad_rows])


def vector(vec, row, count=1):
    parts = [vec[0, row + i : row + i + 1, :] for i in range(count)]
    return parts[0] if count == 1 else jnp.concatenate(parts, axis=1)


def forward(x, seg, weights, kept, y, before_weights=None, after_attention=None):
    vec, w_qkv, w_proj, w_fc1, w_fc2 = weights
    xhat1, r1, qkv, prob, ctx_t, xhat2, r2, act, dgelu = kept
    _, width = x.shape
    hidden = w_fc1.shape[2]
    scaled, inverse = normalized(x[...].astype(F32))
    xhat1[...] = scaled.astype(BF16)
    r1[...] = inverse
    if before_weights is not None:
        before_weights()
    normed = (scaled * vector(vec, ATTN_GAIN) + vector(vec, ATTN_SHIFT)).astype(BF16)
    for part, bias in ((0, Q_BIAS), (1, None), (2, V_BIAS)):
        mixed = nn(normed, w_qkv[0, :, part * width : (part + 1) * width])
        if bias is not None:
            mixed = mixed + vector(vec, bias)
        qkv[:, part * width : (part + 1) * width] = mixed.astype(BF16)
    attend(seg, qkv, prob, ctx_t, width)
    if after_attention is not None:
        after_attention()
    after = x[...].astype(F32) + tn(ctx_t[...], w_proj[0]) + vector(vec, PROJ_BIAS)
    scaled, inverse = normalized(after)
    xhat2[...] = scaled.astype(BF16)
    r2[...] = inverse
    normed = (scaled * vector(vec, MLP_GAIN) + vector(vec, MLP_SHIFT)).astype(BF16)
    output = after + vector(vec, FC2_BIAS)
    bias = vector(vec, FC1_BIAS, hidden // width)
    tops = list(range(0, hidden, FORWARD_CHUNK))

    def product(left):
        return nn(normed, w_fc1[0, :, left : left + FORWARD_CHUNK])

    coming = product(tops[0])
    for i, left in enumerate(tops):
        cols = slice(left, left + FORWARD_CHUNK)
        pre = coming + bias[:, cols]
        if i + 1 < len(tops):
            coming = product(tops[i + 1])
        below = 0.5 + 0.5 * lax.erf(pre * (0.5**0.5))
        density = jnp.exp2(pre * pre * (-0.5 * LOG2E)) * (1.0 / (2.0 * jnp.pi) ** 0.5)
        active = (pre * below).astype(BF16)
        act[:, cols] = active
        dgelu[:, cols] = (below + pre * density).astype(BF16)
        output = output + nn(active, w_fc2[0, cols, :])
    y[...] = output.astype(BF16)


def adder(sum_vec, width):
    def add(row, values):
        for i in range(values.shape[1] // width):
            at = (row + i) * 8
            sum_vec[at : at + 8, :] += column_sums(values[:, i * width : (i + 1) * width])

    return add


def backward_fc2(dout, act, sums):
    sum_fc2, sum_vec = sums[3:]
    top_grad = dout[...]
    adder(sum_vec, dout.shape[1])(FC2_BIAS, top_grad.astype(F32))
    sum_fc2[...] += nn(top_grad.T, act[...])


def backward_mlp(dout, weights, kept, sums, write, with_fc2=True):
    vec, _, w_proj, w_fc1, w_fc2 = weights
    ctx_t, xhat2, r2, act, dgelu = kept
    _, sum_proj, sum_fc1, _, sum_vec = sums
    rows, width = dout.shape
    hidden = w_fc1.shape[2]
    add = adder(sum_vec, width)
    top_grad = dout[...]
    top_wide = top_grad.astype(F32)
    if with_fc2:
        backward_fc2(dout, act, sums)
    scaled = xhat2[...].astype(F32)
    normed_t = (scaled * vector(vec, MLP_GAIN) + vector(vec, MLP_SHIFT)).astype(BF16).T
    grad_normed = jnp.zeros((rows, width), F32)
    column_parts = []
    for left in range(0, hidden, CHUNK):
        cols = slice(left, left + CHUNK)
        grad_pre = nt(top_grad, w_fc2[0, cols, :]) * dgelu[:, cols].astype(F32)
        column_parts.append(column_sums(grad_pre))
        grad_pre = grad_pre.astype(BF16)
        grad_normed = grad_normed + nt(grad_pre, w_fc1[0, :, cols])
        sum_fc1[:, cols] += nn(normed_t, grad_pre)
    columns = jnp.concatenate(column_parts, axis=1)
    for i in range(hidden // width):
        at = (FC1_BIAS + i) * 8
        sum_vec[at : at + 8, :] += columns[:, i * width : (i + 1) * width]
    add(MLP_GAIN, grad_normed * scaled)
    add(MLP_SHIFT, grad_normed)
    grad_after = top_wide + norm_back(scaled, r2[...], vector(vec, MLP_GAIN), grad_normed)
    add(PROJ_BIAS, grad_after)
    grad_branch = grad_after.astype(BF16)
    sum_proj[...] += nn(ctx_t[...], grad_branch)
    write(grad_after, nt(grad_branch, w_proj[0]).astype(BF16))


def backward_attn(grad_after, grad_context, seg, weights, kept, sums, grad_qkv, write, halfway=None):
    vec, w_qkv, _, _, _ = weights
    xhat1, r1, qkv, prob = kept
    sum_qkv, sum_vec = sums[0], sums[4]
    rows, width = grad_after.shape
    add = adder(sum_vec, width)
    attend_back(
        seg, qkv, prob, grad_context, grad_qkv, list(range(width // PAIR)), rows // S,
        lambda part, pair: part * width + pair * PAIR,
    )
    if halfway is not None:
        halfway()
    scaled = xhat1[...].astype(F32)
    normed_t = (scaled * vector(vec, ATTN_GAIN) + vector(vec, ATTN_SHIFT)).astype(BF16).T
    grad_normed = jnp.zeros((rows, width), F32)
    for part, row in ((0, Q_BIAS), (1, None), (2, V_BIAS)):
        cols = slice(part * width, (part + 1) * width)
        piece = grad_qkv[:, cols]
        if row is not None:
            add(row, piece.astype(F32))
        sum_qkv[:, cols] += nn(normed_t, piece)
        grad_normed = grad_normed + nt(piece, w_qkv[0, :, cols])
    add(ATTN_GAIN, grad_normed * scaled)
    add(ATTN_SHIFT, grad_normed)
    write(grad_after[...] + norm_back(scaled, r1[...], vector(vec, ATTN_GAIN), grad_normed))


def half_rows(share):
    return up16(share // 2)


def write_blocks(sums, members, blocks, out):
    sum_qkv, sum_proj, sum_fc1, sum_fc2, _ = sums
    width = sum_proj.shape[0]
    share = width // members
    size = half_rows(share)
    parts = sum_fc1.shape[1] // width

    def store(rows, member, block):
        at = (member * len(blocks) + blocks.index(block)) * size
        out[0, at : at + size, :] = rows[:size]
        out[1, at : at + size, :] = rows[share - size :]

    for block in blocks:
        if block < parts:
            whole = sum_fc1[:, block * width : (block + 1) * width]
        elif block < 2 * parts:
            chunk = block - parts
            whole = sum_fc2[:, chunk * width : (chunk + 1) * width].astype(BF16).T
            for place in range(members):
                row = chunk * members + place
                store(whole[place * share : (place + 1) * share], row // parts, parts + row % parts)
            continue
        elif block == 2 * parts:
            whole = sum_proj[...]
        else:
            part = block - 2 * parts - 1
            whole = sum_qkv[:, part * width : (part + 1) * width]
        whole = whole.astype(BF16)
        for member in range(members):
            store(whole[member * share : (member + 1) * share], member, block)


def write_block(whole, members, store):
    share = whole.shape[0] // members
    size = half_rows(share)
    for member in range(members):
        rows = whole[member * share : (member + 1) * share]
        store(0, member * size, rows[:size])
        store(1, member * size, rows[share - size :])


def vector_sums(sum_vec):
    return jnp.sum(sum_vec[...].reshape(VECTORS, 8, sum_vec.shape[1]), axis=1).astype(BF16)


def clear(refs):
    for ref in refs:
        ref[...] = jnp.zeros_like(ref)


def kept_shapes(steps, width, hidden):
    return (
        ((steps * STEP, width), BF16, (STEP, width), 0),
        ((steps * STEP, 1), F32, (STEP, 1), 0),
        ((steps * STEP, 3 * width), BF16, (STEP, 3 * width), 0),
        ((steps * PROB_ROWS * (width // PAIR), S), BF16, (PROB_ROWS * (width // PAIR), S), 0),
        ((width, steps * STEP), BF16, (width, STEP), 1),
        ((steps * STEP, width), BF16, (STEP, width), 0),
        ((steps * STEP, 1), F32, (STEP, 1), 0),
        ((steps * STEP, hidden), BF16, (STEP, hidden), 0),
        ((steps * STEP, hidden), BF16, (STEP, hidden), 0),
    )


def sum_scratch(width, hidden):
    return [
        pltpu.VMEM((width, 3 * width), F32),
        pltpu.VMEM((width, width), F32),
        pltpu.VMEM((width, hidden), F32),
        pltpu.VMEM((width, hidden), F32),
        pltpu.VMEM((8 * VECTORS, width), F32),
    ]


def place():
    return lax.axis_index("section"), lax.axis_index("group"), lax.axis_index("member")


def remote(src, dst, send, recv, device):
    return pltpu.make_async_remote_copy(
        src_ref=src, dst_ref=dst, send_sem=send, recv_sem=recv, device_id=device, device_id_type=MESH
    )


def greet(peers):
    barrier = pltpu.get_barrier_semaphore()
    for peer in peers:
        pl.semaphore_signal(barrier, inc=1, device_id=peer, device_id_type=MESH)
    pl.semaphore_wait(barrier, len(peers))


def near_peers(members, sections):
    section, group, member = place()
    return [
        (lax.rem(section + ds, 2), group, lax.rem(member + dm, members))
        for ds in range(2)
        for dm in range(members)
        if (ds or dm) and (sections or not (ds and dm))
    ]


def far_peers(groups):
    section, group, member = place()
    return [
        (lax.rem(section + ds, 2), lax.rem(group + dg, groups), member)
        for ds in range(2)
        for dg in range(1, groups)
    ]


def rows_at(index, count):
    return pl.ds(pl.multiple_of(index * count, 16), count)


class Near:
    def __init__(self, members, count, width):
        self.members, self.count, self.width = members, count, width

    def source_shape(self):
        return (2, self.members * self.count, self.width)

    def scratch(self):
        return [
            pltpu.VMEM((self.members * self.count, self.width), BF16),
            pltpu.VMEM((self.members - 1, self.count, self.width), BF16),
        ] + [pltpu.SemaphoreType.DMA((n,)) for n in (1, 1, self.members, self.members)]

    def bind(self, refs, source):
        self.got, self.from_members, *self.sems = refs
        self.source = source
        return self

    def section_copy(self):
        section, group, member = place()
        return remote(
            self.source.at[1 - section], self.got, self.sems[0].at[0], self.sems[1].at[0], (1 - section, group, member)
        )

    def member_copy(self, offset):
        section, group, member = place()
        to = lax.rem(member + offset, self.members)
        return remote(
            self.got.at[rows_at(to, self.count)],
            self.from_members.at[offset - 1],
            self.sems[2].at[offset],
            self.sems[3].at[offset],
            (section, group, to),
        )

    def start_section(self):
        self.section_copy().start()

    def start_members(self):
        self.section_copy().wait()
        own = self.source[lax.axis_index("section")].astype(F32)
        self.got[...] = (self.got[...].astype(F32) + own).astype(BF16)
        for offset in range(1, self.members):
            self.member_copy(offset).start()

    def finish(self, out):
        for offset in range(1, self.members):
            self.member_copy(offset).wait()
        total = self.got[rows_at(lax.axis_index("member"), self.count), :].astype(F32)
        for offset in range(1, self.members):
            total = total + self.from_members[offset - 1].astype(F32)
        out[: self.count, :] = total.astype(BF16)
        spare = out.shape[0] - self.count
        if spare:
            out[self.count :, :] = jnp.zeros((spare, self.width), BF16)


class Far:
    def __init__(self, target, groups, count, width):
        self.target, self.groups, self.width = target, groups, width
        self.part = up16(-(-count // groups))

    def total_shape(self):
        return (self.groups * self.part, self.width)

    def result_shape(self):
        return (2, self.groups, self.part, self.width)

    def scratch(self):
        return [
            pltpu.VMEM((self.groups - 1, self.part, self.width), BF16),
            pltpu.VMEM((self.part, self.width), BF16),
            pltpu.SemaphoreType.DMA,
        ] + [pltpu.SemaphoreType.DMA((n,)) for n in (self.groups,) * 2 + (2 * self.groups,) * 2]

    def bind(self, refs, total, result):
        self.from_groups, self.piece, self.local, *self.sems = refs
        self.total, self.result_ref = total, result
        return self

    def group_copy(self, offset):
        section, group, member = place()
        to = lax.rem(group + offset, self.groups)
        return remote(
            self.total.at[rows_at(to, self.part)],
            self.from_groups.at[offset - 1],
            self.sems[0].at[offset],
            self.sems[1].at[offset],
            (section, to, member),
        )

    def gather_copy(self, offset, across):
        section, group, member = place()
        slot = across * self.groups + offset
        return remote(
            self.piece,
            self.result_ref.at[section, group],
            self.sems[2].at[slot],
            self.sems[3].at[slot],
            (self.target, lax.rem(group + offset, self.groups), member),
        )

    def gathered(self, offset, across):
        section, group, member = place()
        slot = across * self.groups + offset
        origin = lax.rem(group + self.groups - offset, self.groups)
        half = 1 - section if across else section
        return remote(
            self.piece,
            self.result_ref.at[half, origin],
            self.sems[2].at[slot],
            self.sems[3].at[slot],
            (self.target, origin, member),
        )

    def start_groups(self):
        for offset in range(1, self.groups):
            self.group_copy(offset).start()

    def start_gather(self):
        section, group, member = place()
        for offset in range(1, self.groups):
            self.group_copy(offset).wait()
        total = self.total[rows_at(group, self.part), :].astype(F32)
        for offset in range(1, self.groups):
            total = total + self.from_groups[offset - 1].astype(F32)
        self.piece[...] = total.astype(BF16)

        @pl.when(section == self.target)
        def _():
            for offset in range(1, self.groups):
                self.gather_copy(offset, 0).start()
            keep = pltpu.make_async_copy(self.piece, self.result_ref.at[section, group], self.local)
            keep.start()
            keep.wait()

        @pl.when(section != self.target)
        def _():
            for offset in range(self.groups):
                self.gather_copy(offset, 1).start()

    def finish(self):
        section, group, member = place()

        @pl.when(section == self.target)
        def _():
            for offset in range(1, self.groups):
                self.gather_copy(offset, 0).wait_send()
                self.gathered(offset, 0).wait_recv()
            for offset in range(self.groups):
                self.gathered(offset, 1).wait_recv()

        @pl.when(section != self.target)
        def _():
            for offset in range(self.groups):
                self.gather_copy(offset, 1).wait_send()


class VectorSum:
    def __init__(self, groups, members, width):
        self.groups, self.members, self.width = groups, members, width

    def scratch(self):
        return [
            pltpu.VMEM((2 * self.members, VECTORS, self.width), BF16),
            pltpu.VMEM((self.groups, VECTORS, self.width), BF16),
            pltpu.VMEM((VECTORS, self.width), BF16),
            pltpu.VMEM((VECTORS, self.width), BF16),
        ] + [pltpu.SemaphoreType.DMA((n,)) for n in (2 * self.members,) * 2 + (self.groups,) * 2]

    def bind(self, refs):
        self.near, self.far, self.own, self.middle = refs[:4]
        self.sems = refs[4:]
        return self

    def near_copy(self, offset):
        section, group, member = place()
        ds, dm = divmod(offset, self.members)
        to = lax.rem(section + ds, 2), group, lax.rem(member + dm, self.members)
        return remote(
            self.own, self.near.at[section * self.members + member], self.sems[0].at[offset], self.sems[1].at[offset], to
        )

    def near_got(self, offset):
        section, group, member = place()
        ds, dm = divmod(offset, self.members)
        origin = lax.rem(section + ds, 2), lax.rem(member + self.members - dm, self.members)
        return remote(
            self.own,
            self.near.at[origin[0] * self.members + origin[1]],
            self.sems[0].at[offset],
            self.sems[1].at[offset],
            (origin[0], group, origin[1]),
        )

    def far_copy(self, offset):
        section, group, member = place()
        to = section, lax.rem(group + offset, self.groups), member
        return remote(self.middle, self.far.at[group], self.sems[2].at[offset], self.sems[3].at[offset], to)

    def far_got(self, offset):
        section, group, member = place()
        origin = lax.rem(group + self.groups - offset, self.groups)
        return remote(
            self.middle, self.far.at[origin], self.sems[2].at[offset], self.sems[3].at[offset], (section, origin, member)
        )

    def start(self, values):
        section, group, member = place()
        self.own[...] = values
        self.near[section * self.members + member] = values
        for offset in range(1, 2 * self.members):
            self.near_copy(offset).start()

    def start_far(self):
        for offset in range(1, 2 * self.members):
            self.near_copy(offset).wait_send()
            self.near_got(offset).wait_recv()
        total = jnp.zeros((VECTORS, self.width), F32)
        for index in range(2 * self.members):
            total = total + self.near[index].astype(F32)
        self.middle[...] = total.astype(BF16)
        self.far[lax.axis_index("group")] = total.astype(BF16)
        for offset in range(1, self.groups):
            self.far_copy(offset).start()

    def finish(self):
        for offset in range(1, self.groups):
            self.far_copy(offset).wait_send()
            self.far_got(offset).wait_recv()
        total = jnp.zeros((VECTORS, self.width), F32)
        for index in range(self.groups):
            total = total + self.far[index].astype(F32)
        return total


def take(refs, *counts):
    out, at = [], 0
    for count in counts:
        out.append(list(refs[at : at + count]))
        at += count
    assert at == len(refs)
    return out


def params(collective):
    return pltpu.CompilerParams(vmem_limit_bytes=62 * MIB, collective_id=collective, has_side_effects=True)


def cost(flops, moved):
    return pl.CostEstimate(flops=flops, bytes_accessed=moved * MIB, transcendentals=0)


def block_at(shape, axis, index):
    return pl.BlockSpec(shape, lambda i: tuple(index(i) if d == axis else 0 for d in range(len(shape))))


def fixed(shape):
    return pl.BlockSpec(shape, lambda i: (0,) * len(shape), pipeline_mode=pl.Buffered(1))


ANYWHERE = pl.BlockSpec(memory_space=pl.ANY)


def first_forward(tokens, seg, vectors, own, steps):
    width, hidden = tokens.shape[1], own[2].shape[2]
    shapes = kept_shapes(steps, width, hidden)
    held = [((2, VECTORS, width), F32)] + [((2,) + w.shape[1:], w.dtype) for w in own]
    count = len(own)

    def body(x, seg, *refs):
        vectors_in, own, (y,), kept, weights, held, sems = take(
            refs, len(vectors), count, 1, len(shapes), count + 1, count + 1, 5
        )
        load, send, recv, out, _ = sems
        step = pl.program_id(0)
        section, group, member = place()
        partner = (1 - section, group, member)
        order = list(range(count + 1))

        def own_load(i):
            return pltpu.make_async_copy(own[i - 1].at[0], held[i].at[section], load.at[i])

        def push(i, whose):
            source = own[i - 1].at[0] if i else held[0].at[whose]
            return remote(source, held[i].at[whose], send.at[i], recv.at[i], partner)

        def layer_zero(which):
            @pl.when(section == 0)
            def _():
                for i in which:
                    if i:
                        own_load(i).wait()

            @pl.when(section == 1)
            def _():
                for i in which:
                    push(i, 1 - section).wait_recv()

        def store(i):
            return pltpu.make_async_copy(held[i], weights[i], out.at[i])

        @pl.when(step == 0)
        def _():
            for i in order[1:]:
                own_load(i).start()
            row = 0
            for vector_in in vectors_in:
                for part in range(vector_in.shape[1] // width):
                    held[0][section, row : row + 1, :] = vector_in[:, part * width : (part + 1) * width]
                    row += 1
            held[0][section, row:, :] = jnp.zeros((VECTORS - row, width), F32)
            greet([partner])
            for i in order:
                push(i, section).start()

        @pl.when(step == 1)
        def _():
            @pl.when(section == 0)
            def _():
                for i in order:
                    push(i, 1 - section).wait_recv()

            @pl.when(section == 1)
            def _():
                for i in order[1:]:
                    own_load(i).wait()

            for i in order:
                store(i).start()

        def before_weights():
            @pl.when(step == 0)
            def _():
                layer_zero(order[:2])

        def after_attention():
            @pl.when(step == 0)
            def _():
                layer_zero(order[2:])

        forward(x, seg, held, kept, y, before_weights, after_attention)

        @pl.when(step == steps - 1)
        def _():
            for i in order:
                store(i).wait()
                push(i, section).wait_send()

    def mine(i):
        return lax.axis_index("section") * steps + i

    return pl.pallas_call(
        body,
        grid=(steps,),
        in_specs=[block_at((STEP, width), 0, mine), block_at((1, STEP), 1, mine)]
        + [fixed(v.shape) for v in vectors]
        + [ANYWHERE] * count,
        out_specs=[block_at((STEP, width), 0, lambda i: i)]
        + [block_at(block, axis, lambda i: i) for _, _, block, axis in shapes]
        + [ANYWHERE] * (count + 1),
        out_shape=[jax.ShapeDtypeStruct((steps * STEP, width), BF16)]
        + [jax.ShapeDtypeStruct(shape, dtype) for shape, dtype, _, _ in shapes]
        + [jax.ShapeDtypeStruct(shape, dtype) for shape, dtype in held],
        scratch_shapes=[pltpu.VMEM(shape, dtype) for shape, dtype in held]
        + [pltpu.SemaphoreType.DMA((count + 1,))] * 5,
        compiler_params=params(0),
        cost_estimate=cost(steps * STEP * 4000000, 40),
        name="forward_first",
    )(tokens, seg, *vectors, *own)


def block_lists(parts):
    fc1, fc2, proj = list(range(parts)), list(range(parts, 2 * parts)), 2 * parts
    qkv = [proj + 1, proj + 2, proj + 3]
    upper = (fc2 + fc1[: parts // 2], fc1[parts // 2 :] + [proj] + qkv)
    lower = (fc2, fc1 + [proj])
    return upper, lower


def second_layer(x, seg, cotangent, weights, steps, groups, members):
    width, hidden = x.shape[1], weights[3].shape[2]
    shapes = kept_shapes(steps, width, hidden)
    size = half_rows(width // members)
    early, late = block_lists(hidden // width)[0]
    near = Near(members, len(early) * size, width)
    far = Far(1, groups, len(early) * size, width)
    late_shape = Near(members, len(late) * size, width).source_shape()

    def body(x, seg, cot, vec, w_qkv, w_proj, w_fc1, w_fc2, *refs):
        outs, sums, attn_kept, mlp_kept, rest, sems, later, near_refs = take(
            refs, 6, 5, 4, 5, 6, 3, 3, len(near.scratch())
        )
        y_own, y_got, g, late_out, total_out, vec_out = outs
        grad_after, grad_context, grad_qkv, y, y_send, early_out = rest
        send, recv, load = sems
        near.bind(near_refs, early_out)
        loads = [
            pltpu.make_async_copy(w.at[pl.ds(1, 1)], held, load.at[i])
            for i, (w, held) in enumerate(zip((w_proj, w_fc1, w_fc2), later))
        ]
        weights = (vec, w_qkv, *later)
        step = pl.program_id(0)
        section, group, member = place()

        def y_copy(index):
            return remote(
                y_send.at[index], y_got.at[rows_at(index, STEP)], send.at[index], recv.at[index], (1 - section, group, member)
            )

        @pl.when(step == 0)
        def _():
            for copy in loads:
                copy.start()
            clear(sums)
            greet(near_peers(members, False))

        @pl.when(step < steps)
        def _():
            def after_attention():
                @pl.when(step == 0)
                def _():
                    for copy in loads:
                        copy.wait()

            forward(x, seg, weights, [ref.at[step] for ref in attn_kept] + mlp_kept, y, None, after_attention)
            y_own[...] = jnp.where(section == 0, x[...], y[...])
            y_send[step] = jnp.where(section == 0, y[...], x[...])
            y_copy(step).start()

            def write(after, context):
                grad_after[step] = after
                grad_context[step] = context

            backward_mlp(cot, weights, mlp_kept, sums, write)

        @pl.when(step == steps - 1)
        def _():
            write_blocks(sums, members, early, early_out)
            near.start_section()

        @pl.when(step >= steps)
        def _():
            index = step - steps

            def write(values):
                g[...] = values.astype(BF16)

            def halfway():
                @pl.when(step == steps)
                def _():
                    near.start_members()

            backward_attn(
                grad_after.at[index], grad_context.at[index], seg, weights,
                [ref.at[index] for ref in attn_kept], sums, grad_qkv, write, halfway,
            )

        @pl.when(step == 2 * steps - 1)
        def _():
            write_blocks(sums, members, late, late_out)
            vec_out[...] = vector_sums(sums[4])
            for index in range(steps):
                y_copy(index).wait()
            near.finish(total_out)

    def mine(index):
        return lambda i: lax.axis_index("section") * steps + index(i)

    def first(i):
        return jnp.minimum(i, steps - 1)

    def then(i):
        return jnp.maximum(i - steps, 0)

    rows = jax.ShapeDtypeStruct((steps * STEP, width), BF16)
    fixed_outs = [late_shape, far.total_shape(), (VECTORS, width)]
    return pl.pallas_call(
        body,
        grid=(2 * steps,),
        in_specs=[
            block_at((STEP, width), 0, first),
            block_at((1, STEP), 1, mine(lambda i: lax.rem(i, steps))),
            block_at((STEP, width), 0, mine(first)),
        ]
        + [
            pl.BlockSpec((1,) + w.shape[1:], lambda i: (1, 0, 0), pipeline_mode=pl.Buffered(1))
            for w in weights[:2]
        ]
        + [ANYWHERE] * 3,
        out_specs=[block_at((STEP, width), 0, first), ANYWHERE, block_at((STEP, width), 0, then)]
        + [fixed(shape) for shape in fixed_outs],
        out_shape=[rows] * 3 + [jax.ShapeDtypeStruct(shape, BF16) for shape in fixed_outs],
        scratch_shapes=sum_scratch(width, hidden)
        + [pltpu.VMEM((steps,) + block, dtype) for _, dtype, block, _ in shapes[:4]]
        + [pltpu.VMEM(block, dtype) for _, dtype, block, _ in shapes[4:]]
        + [
            pltpu.VMEM((steps, STEP, width), F32),
            pltpu.VMEM((steps, STEP, width), BF16),
            pltpu.VMEM((STEP, 3 * width), BF16),
            pltpu.VMEM((STEP, width), BF16),
            pltpu.VMEM((steps, STEP, width), BF16),
            pltpu.VMEM(near.source_shape(), BF16),
        ]
        + [pltpu.SemaphoreType.DMA((steps,))] * 2
        + [pltpu.SemaphoreType.DMA((3,))]
        + [pltpu.VMEM((1,) + w.shape[1:], w.dtype) for w in weights[2:]]
        + near.scratch(),
        compiler_params=params(1),
        cost_estimate=cost(steps * STEP * 12000000, 20),
        name="second_layer",
    )(x, seg, cotangent, *weights)


def first_backward(seg, dout, late1, total1, vec1, kept, weights, steps, groups, members):
    width, hidden = dout.shape[1], weights[3].shape[2]
    shapes = kept_shapes(steps, width, hidden)
    size = half_rows(width // members)
    pairs = width // PAIR
    rows = steps * STEP
    (upper_early, upper_late), lower = block_lists(hidden // width)
    counts = [len(blocks) * size for blocks in (upper_early, upper_late) + lower] + [size] * pairs
    fars = [Far(1 if i < 2 else 0, groups, count, width) for i, count in enumerate(counts)]
    nears = [Near(members, count, width) for count in counts[1:]]
    vector_plans = [VectorSum(groups, members, width) for _ in range(2)]
    plans = fars + nears + vector_plans
    starts = [0, steps, 2 * steps, 2 * steps + pairs, 3 * steps + pairs]
    last = starts[4] - 1

    def body(seg, dout, act, ctx_t, xhat2, r2, dgelu, vec, late1, total1, vec1, *refs):
        attn_in, weights_in, (g_own, g_got), results, vec_outs, *refs = take(
            refs, 4, 4, 2, len(fars), 2, len(refs) - 12 - len(fars)
        )
        sums, rest, attn_kept, held, sources, totals, sems, *bound = take(
            refs[0], 4, 8, 4, 4, 3, len(fars) - 1, 4, *[len(plan.scratch()) for plan in plans]
        )
        grad_after, grad_context, grad_qkv, g_send, scaled_t, paired, gain_part, shift_part = rest
        send, recv, load, load_attn = sems
        take_fars, take_nears = bound[: len(fars)], bound[len(fars) : len(fars) + len(nears)]
        for plan, plan_refs, total, result in zip(fars, take_fars, [total1] + totals, results):
            plan.bind(plan_refs, total, result)
        pair_sources = [sources[2].at[pair] for pair in range(pairs)]
        for plan, plan_refs, source in zip(nears, take_nears, [late1] + sources[:2] + pair_sources):
            plan.bind(plan_refs, source)
        for plan, plan_refs in zip(vector_plans, bound[len(fars) + len(nears) :]):
            plan.bind(plan_refs)
        far_a, far_b, far_fc2, far_fc1, *far_pairs = fars
        near_b, near_fc2, near_fc1, *near_pairs = nears
        total_b, total_fc2, total_fc1, *total_pairs = totals
        upper_vec, lower_vec = vector_plans
        sum_proj, sum_fc1, sum_fc2, sum_vec = sums
        all_sums = (None, sum_proj, sum_fc1, sum_fc2, sum_vec)
        w_qkv, w_proj, w_fc1, w_fc2 = held
        weights = (vec, w_qkv, w_proj, w_fc1, w_fc2)
        xhat1, r1, qkv, prob = attn_kept
        step = pl.program_id(0)
        section, group, member = place()
        loads = [pltpu.make_async_copy(a.at[pl.ds(0, 1)], b, load.at[i]) for i, (a, b) in enumerate(zip(weights_in, held))]
        loads_attn = [pltpu.make_async_copy(a, b, load_attn.at[i]) for i, (a, b) in enumerate(zip(attn_in, attn_kept))]

        def g_copy(index):
            return remote(
                g_send.at[index], g_got.at[rows_at(index, STEP)], send.at[index], recv.at[index], (1 - section, group, member)
            )

        def at(number, offset=0):
            return pl.when(step == starts[number] + offset)

        def phase(number):
            return pl.when(jnp.logical_and(step >= starts[number], step < starts[number + 1]))

        @at(0)
        def _():
            for copy in loads + loads_attn:
                copy.start()
            clear(sums)
            greet(near_peers(members, True) + far_peers(groups))
            near_b.start_section()
            far_a.start_groups()
            upper_vec.start(vec1[...])

        @at(0, steps // 2)
        def _():
            near_b.start_members()

        @phase(0)
        def _():
            g_send[step] = dout[...]
            backward_fc2(dout, act, all_sums)

        @at(1, -1)
        def _():
            write_blocks(all_sums, members, lower[0], near_fc2.source)
            near_fc2.start_section()

        @at(1)
        def _():
            for copy in loads:
                copy.wait()

        @at(1, 1)
        def _():
            near_fc2.start_members()
            far_a.start_gather()
            upper_vec.start_far()

        @at(2, -1)
        def _():
            near_b.finish(total_b)
            far_b.start_groups()
            vec_outs[0][...] = upper_vec.finish()

        @phase(1)
        def _():
            index = step - starts[1]

            def write(after, context):
                grad_after[index] = after
                grad_context[rows_at(index, STEP), :] = context

            backward_mlp(g_send.at[index], weights, (ctx_t, xhat2, r2, None, dgelu), all_sums, write, False)

        @at(2, -1)
        def _():
            write_blocks(all_sums, members, lower[1], near_fc1.source)
            near_fc1.start_section()

        @at(2)
        def _():
            for copy in loads_attn:
                copy.wait()
            for chunk in range(steps):
                here = slice(chunk * STEP, (chunk + 1) * STEP)
                scaled_t[:width, here] = xhat1[here, :].T
            scaled_t[width:, :] = jnp.ones((16, rows), BF16)
            for pair in range(pairs):
                for part in range(3):
                    left = (3 * pair + part) * PAIR
                    source = part * width + pair * PAIR
                    paired[:, left : left + PAIR] = w_qkv[0, :, source : source + PAIR]
            gain_part[...] = jnp.zeros_like(gain_part)
            shift_part[...] = jnp.zeros_like(shift_part)

        @at(2, 1)
        def _():
            near_fc2.finish(total_fc2)
            far_fc2.start_groups()
            far_b.start_gather()

        @at(2, 2)
        def _():
            near_pairs[0].start_members()

        @phase(2)
        def _():
            pair = step - starts[2]
            attend_back(
                seg, qkv, prob, grad_context, grad_qkv, [pair], 2 * steps,
                lambda part, pair: pair * width + part * PAIR,
            )

            @at(2)
            def _():
                near_fc1.start_members()

            here = span(pair * width, width)
            product = nn(scaled_t[...], grad_qkv[:, here])
            scaled_sum, columns = product[:width], product[width : width + 1]
            weight = paired[:, here].astype(F32)
            gained, shifted = scaled_sum * weight, columns * weight
            for part in range(3):
                cols = slice(part * PAIR, (part + 1) * PAIR)
                gain_part[...] += gained[:, cols]
                shift_part[...] += shifted[:, cols]
            sum_vec[Q_BIAS * 8 : Q_BIAS * 8 + 1, span(pair * PAIR, PAIR)] = columns[:, :PAIR]
            sum_vec[V_BIAS * 8 : V_BIAS * 8 + 1, span(pair * PAIR, PAIR)] = columns[:, 2 * PAIR :]
            gain, shift = [
                jnp.broadcast_to(vector(vec, row), (8, width)).T[:, :1] for row in (ATTN_GAIN, ATTN_SHIFT)
            ]
            whole = (scaled_sum * gain + shift * columns).astype(BF16)

            def store(half, top, rows):
                sources[2][pair, half, top : top + size, :] = rows

            write_block(whole, members, store)

        for pair in range(pairs):

            @at(2, pair)
            def _(pair=pair):
                near_pairs[pair].start_section()

        @at(3)
        def _():
            sum_vec[ATTN_GAIN * 8 : ATTN_GAIN * 8 + 1, :] = jnp.sum(gain_part[...].T, axis=0, keepdims=True)
            sum_vec[ATTN_SHIFT * 8 : ATTN_SHIFT * 8 + 1, :] = jnp.sum(shift_part[...].T, axis=0, keepdims=True)
            lower_vec.start(vector_sums(sum_vec))
            near_pairs[1].start_members()
            near_fc1.finish(total_fc1)
            far_fc1.start_groups()
            far_fc2.start_gather()

        @at(3, 1)
        def _():
            near_pairs[2].start_members()

        @at(3, 2)
        def _():
            near_pairs[0].finish(total_pairs[0])
            far_pairs[0].start_groups()
            lower_vec.start_far()

        @at(3, 3)
        def _():
            near_pairs[1].finish(total_pairs[1])
            far_pairs[1].start_groups()

        @phase(3)
        def _():
            index = step - starts[3]
            here = rows_at(index, STEP)
            grad_normed = nt(grad_qkv[here, :], paired[...])
            scaled = xhat1[here, :].astype(F32)
            grads = grad_after[index] + norm_back(scaled, r1[here, :], vector(vec, ATTN_GAIN), grad_normed)
            low = grads.astype(BF16)
            upper_rows = g_send[index]
            g_own[...] = jnp.where(section == 0, low, upper_rows)
            g_send[index] = jnp.where(section == 0, upper_rows, low)
            g_copy(index).start()

        @at(4, -1)
        def _():
            for pair in range(2, pairs):
                near_pairs[pair].finish(total_pairs[pair])
                far_pairs[pair].start_groups()
            far_fc1.start_gather()
            vec_outs[1][...] = lower_vec.finish()
            for far in far_pairs:
                far.start_gather()
            for index in range(steps):
                g_copy(index).wait()
            for far in fars:
                far.finish()

    def clipped(number):
        return lambda i: jnp.clip(i - starts[number], 0, steps - 1)

    low_rows = jax.ShapeDtypeStruct((rows, width), BF16)
    vec_shape = (VECTORS, width)
    xhat1, r1, qkv, prob, ctx_t, xhat2, r2, act, dgelu = kept
    attn_in = (xhat1, r1, qkv, prob)
    return pl.pallas_call(
        body,
        grid=(starts[4],),
        in_specs=[
            block_at((1, rows), 1, lambda i: lax.axis_index("section")),
            block_at((STEP, width), 0, clipped(0)),
            block_at((STEP, hidden), 0, clipped(0)),
            block_at((width, STEP), 1, clipped(1)),
            block_at((STEP, width), 0, clipped(1)),
            block_at((STEP, 1), 0, clipped(1)),
            block_at((STEP, hidden), 0, clipped(1)),
            fixed((1, VECTORS, width)),
            fixed(late1.shape),
            fixed(total1.shape),
            fixed(vec_shape),
        ]
        + [ANYWHERE] * 8,
        out_specs=[block_at((STEP, width), 0, clipped(3)), ANYWHERE]
        + [ANYWHERE] * len(fars)
        + [fixed(vec_shape)] * 2,
        out_shape=[low_rows] * 2
        + [jax.ShapeDtypeStruct(far.result_shape(), BF16) for far in fars]
        + [jax.ShapeDtypeStruct(vec_shape, F32)] * 2,
        scratch_shapes=sum_scratch(width, hidden)[1:]
        + [
            pltpu.VMEM((steps, STEP, width), F32),
            pltpu.VMEM((rows, width), BF16),
            pltpu.VMEM((rows, 3 * width), BF16),
            pltpu.VMEM((steps, STEP, width), BF16),
            pltpu.VMEM((width + 16, rows), BF16),
            pltpu.VMEM((width, 3 * width), BF16),
            pltpu.VMEM((width, PAIR), F32),
            pltpu.VMEM((width, PAIR), F32),
        ]
        + [pltpu.VMEM(a.shape, a.dtype) for a in attn_in]
        + [pltpu.VMEM((1,) + w.shape[1:], w.dtype) for w in weights[1:]]
        + [pltpu.VMEM(near.source_shape(), BF16) for near in nears[1:3]]
        + [pltpu.VMEM((pairs,) + nears[3].source_shape(), BF16)]
        + [pltpu.VMEM(far.total_shape(), BF16) for far in fars[1:]]
        + [pltpu.SemaphoreType.DMA((steps,))] * 2
        + [pltpu.SemaphoreType.DMA((4,))] * 2
        + [item for plan in plans for item in plan.scratch()],
        compiler_params=params(2),
        cost_estimate=cost(rows * 8000000, 40),
        name="backward_first",
    )(seg, dout, act, ctx_t, xhat2, r2, dgelu, weights[0], late1, total1, vec1, *attn_in, *weights[1:])


def finish(y_own, y_got, g_own, g_got, results, vec_sums, width, hidden, steps, members):
    parts = hidden // width
    pairs = width // PAIR
    share = width // members
    size = half_rows(share)
    upper, lower = block_lists(parts)
    results = [result.reshape(2, -1, width) for result in results]
    tall = 2 * STEP
    steps = steps // 2

    def body(y_own, y_got, g_own, g_got, *refs):
        results, (upper_vec, lower_vec), (acts, grads), outs = take(refs, len(results_in), 2, 2, 12)
        a_gain, a_shift, d_qkv, d_qv, d_proj, b_proj, m_gain, m_shift, d_fc1, b_fc1, d_fc2, b_fc2 = outs
        step = pl.program_id(0)
        section, member = lax.axis_index("section"), lax.axis_index("member")
        mine = step // steps == section
        acts[0] = jnp.where(mine, y_own[...], y_got[...])
        grads[0] = jnp.where(mine, g_own[...], g_got[...]).astype(F32)

        def rows_of(lists, results, block, half):
            for blocks, result in zip(lists, results):
                if block in blocks:
                    top = blocks.index(block) * size
                    return result[half, top : top + size, :].astype(F32)
            raise KeyError(block)

        def write(lists, results, vec_sum, paired):
            for half in range(2):
                top = half * (share - size)
                for block in range(2 * parts + 1):
                    rows = rows_of(lists, results, block, half)
                    if block < parts:
                        d_fc1[0, top : top + size, block * width : (block + 1) * width] = rows
                    elif block < 2 * parts:
                        base = (block - parts) * share + top
                        d_fc2[0, base : base + size, :] = rows
                    else:
                        d_proj[0, top : top + size, :] = rows
                for index in range(3):
                    if paired:
                        rows = results[len(lists) + index][half, :size, :].astype(F32)
                        for part in range(3):
                            left = part * width + index * PAIR
                            d_qkv[0, top : top + size, left : left + PAIR] = rows[:, part * PAIR : (part + 1) * PAIR]
                    else:
                        rows = rows_of(lists, results, 2 * parts + 1 + index, half)
                        d_qkv[0, top : top + size, index * width : (index + 1) * width] = rows

            def put(out, row, count=1):
                flat = jnp.concatenate([vec_sum[row + i : row + i + 1, :] for i in range(count)], axis=1)
                length = count * width // members
                value = flat[:, :length]
                for m in range(1, members):
                    value = jnp.where(member == m, flat[:, m * length : (m + 1) * length], value)
                out[...] = value

            put(a_gain, ATTN_GAIN)
            put(a_shift, ATTN_SHIFT)
            put(d_qv, Q_BIAS, 2)
            put(b_proj, PROJ_BIAS)
            put(m_gain, MLP_GAIN)
            put(m_shift, MLP_SHIFT)
            put(b_fc1, FC1_BIAS, parts)
            put(b_fc2, FC2_BIAS)

        @pl.when(jnp.logical_and(step == 0, section == 0))
        def _():
            write(lower, results[2:], lower_vec, True)

        @pl.when(jnp.logical_and(step == 0, section == 1))
        def _():
            write(upper, results[:2], upper_vec, False)

    def whole(shape):
        return pl.BlockSpec(shape, lambda i: (0,) * len(shape))

    def rows_from(section):
        return block_at((tall, width), 0, lambda i: jnp.clip(i - section() * steps, 0, steps - 1))

    own = rows_from(lambda: lax.axis_index("section"))
    got = rows_from(lambda: 1 - lax.axis_index("section"))
    total = 2 * steps * tall
    smalls = [
        (1, share), (1, share), (1, share, 3 * width), (1, 2 * share), (1, share, width), (1, share), (1, share),
        (1, share), (1, share, hidden), (1, hidden // members), (1, hidden // members, width), (1, share),
    ]
    rows_spec = pl.BlockSpec((1, tall, width), lambda i: (0, i, 0))
    results_in = results
    return pl.pallas_call(
        body,
        grid=(2 * steps,),
        in_specs=[own, got, own, got] + [whole(x.shape) for x in results + list(vec_sums)],
        out_specs=[rows_spec, rows_spec] + [whole(shape) for shape in smalls],
        out_shape=[
            jax.ShapeDtypeStruct((1, total, width), BF16),
            jax.ShapeDtypeStruct((1, total, width), F32),
        ]
        + [jax.ShapeDtypeStruct(shape, F32) for shape in smalls],
        compiler_params=pltpu.CompilerParams(vmem_limit_bytes=62 * MIB),
        cost_estimate=cost(0, 16),
        name="finish",
    )(y_own, y_got, g_own, g_got, *results, *vec_sums)


def per_device(
    tokens,
    segment,
    cotangent,
    attn_gain,
    attn_shift,
    qkv_weight,
    qv_bias,
    proj_weight,
    proj_bias,
    mlp_gain,
    mlp_shift,
    fc1_weight,
    fc1_bias,
    fc2_weight,
    fc2_bias,
):
    groups, members = lax.axis_size("group"), lax.axis_size("member")
    rows, width = tokens.shape
    hidden = fc1_weight.shape[2]
    steps = rows // 2 // STEP
    seg = segment.reshape(1, rows)
    vectors = (attn_gain, attn_shift, qv_bias, proj_bias, mlp_gain, mlp_shift, fc2_bias, fc1_bias)
    y0, *rest = first_forward(
        tokens, seg, vectors, [qkv_weight, proj_weight, fc1_weight, fc2_weight], steps
    )
    kept, weights = rest[:9], rest[9:]
    y_own, y_got, g1, late1, total1, vec1 = second_layer(y0, seg, cotangent, weights, steps, groups, members)
    g_own, g_got, *grads = first_backward(seg, g1, late1, total1, vec1, kept, weights, steps, groups, members)
    return tuple(finish(y_own, y_got, g_own, g_got, grads[:-2], grads[-2:], width, hidden, steps, members))


def solution(mesh):
    row = P("section", None)
    mat = P("section", None, None)
    tokens = P(("group", "member"), None)
    split = P("section", "member")
    split_mat = P("section", "member", None)
    stacked = P("section", ("group", "member"), None)
    return jax.shard_map(
        per_device,
        mesh=mesh,
        in_specs=(
            tokens, P(("group", "member")), tokens,
            row, row, mat, row, mat, row, row, row, mat, row, mat, row,
        ),
        out_specs=(
            stacked, stacked,
            split, split, split_mat, split, split_mat, split, split, split, split_mat, split, split_mat, split,
        ),
        check_vma=False,
    )
```

```python
import jax
import jax.numpy as jnp
from jax import lax
from jax.experimental import pallas as pl
from jax.experimental.pallas import tpu as pltpu
from jax.sharding import PartitionSpec as P

HD = 64
S = 256
HALF = S // 2
GLOBAL_LEN = 197
LOCAL_LEN = 37
PAIR = 2 * HD
STEP = 2 * S
EPS = 1e-06
SCALE = HD ** (-0.5)
LOG2E = 1.4426950408889634
CHUNK = 1536
FORWARD_CHUNK = 256
DEPTH = 4
INTERLEAVED = 6
F32 = jnp.float32
BF16 = jnp.bfloat16
MIB = 1 << 20
MESH = pl.DeviceIdType.MESH

ATTN_GAIN, ATTN_SHIFT, Q_BIAS, V_BIAS, PROJ_BIAS, MLP_GAIN, MLP_SHIFT, FC2_BIAS, FC1_BIAS = range(9)
VECTORS = 16


def up16(value):
    return -(-value // 16) * 16


def key_windows(local):
    if not local:
        return ((0, up16(GLOBAL_LEN)),) * 2
    first_end = ((HALF - 1) // LOCAL_LEN + 1) * LOCAL_LEN
    second_start = HALF // LOCAL_LEN * LOCAL_LEN // 16 * 16
    return ((0, up16(first_end)), (second_start, up16(S // LOCAL_LEN * LOCAL_LEN)))


WINDOWS = tuple((local, key_windows(local)) for local in (False, True))
PROB_ROWS = sum(hi - lo for _, windows in WINDOWS for lo, hi in windows)


def prob_offset(pair, sequence, block):
    spans = [hi - lo for _, windows in WINDOWS for lo, hi in windows]
    return pair * PROB_ROWS + sum(spans[: 2 * sequence + block])


def nn(left, right):
    return jnp.dot(left, right, preferred_element_type=F32)


def nt(left, right):
    return lax.dot_general(left, right, (((1,), (1,)), ((), ())), preferred_element_type=F32)


def tn(left, right):
    return lax.dot_general(left, right, (((0,), (0,)), ((), ())), preferred_element_type=F32)


def column_sums(values):
    return jnp.sum(values.reshape(values.shape[0] // 8, 8, values.shape[1]), axis=0)


def normalized(values):
    centered = values - jnp.mean(values, axis=1, keepdims=True)
    inverse = lax.rsqrt(jnp.mean(centered * centered, axis=1, keepdims=True) + EPS)
    return centered * inverse, inverse


def norm_back(scaled, inverse, gain, grad):
    grad_scaled = grad * gain
    first = jnp.mean(grad_scaled, axis=1, keepdims=True)
    second = jnp.mean(grad_scaled * scaled, axis=1, keepdims=True)
    return inverse * (grad_scaled - first - scaled * second)


def crop_of(index):
    total = jnp.zeros_like(index)
    for crop in range(1, S // LOCAL_LEN + 1):
        total = total + (index >= crop * LOCAL_LEN).astype(jnp.int32)
    return total


def mask_bias(local, block, lo, hi):
    if not local:
        rows = lax.broadcasted_iota(jnp.int32, (hi - lo, HALF), 0) + lo
        return jnp.where(rows < GLOBAL_LEN, 0.0, -1e30)
    keys = crop_of(lax.broadcasted_iota(jnp.int32, (hi - lo, HALF), 0) + lo)
    queries = crop_of(lax.broadcasted_iota(jnp.int32, (hi - lo, HALF), 1) + block * HALF)
    return jnp.where(keys == queries, 0.0, -1e30)


def split_pair(rows):
    lane = lax.broadcasted_iota(jnp.int32, (1, PAIR), 1)
    first = (lane < HD).astype(rows.dtype)
    second = (lane >= HD).astype(rows.dtype)
    return jnp.concatenate([rows * first, rows * second], axis=0)


def padded(rows, lo, hi):
    parts = [rows]
    if lo:
        parts = [jnp.zeros((lo, rows.shape[1]), rows.dtype)] + parts
    if hi < S:
        parts = parts + [jnp.zeros((S - hi, rows.shape[1]), rows.dtype)]
    return jnp.concatenate(parts, axis=0) if len(parts) > 1 else rows


def diagonal(values):
    return jnp.concatenate([values[:HD, :HALF], values[HD:, HALF:]], axis=0)


def units_of(width):
    return [(sequence, pair, block) for sequence in range(2) for pair in range(width // PAIR) for block in range(2)]


def pipelined(units, depth, stages):
    held = [{} for _ in stages]
    for now in range(len(units) + depth * (len(stages) - 1)):
        for i, stage in enumerate(stages):
            at = now - i * depth
            if 0 <= at < len(units):
                before = [held[i - 1].pop(at)] if i else []
                held[i][at] = stage(units[at], *before)
                yield


class Once(dict):
    def get_or(self, key, make):
        if key not in self:
            self[key] = make()
        return self[key]


def place_of(unit):
    sequence, pair, block = unit
    lo, hi = WINDOWS[sequence][1][block]
    return sequence * S, pair * PAIR, block * HALF, lo, hi


def attend(seg, qkv, prob, ctx_t, width):
    once = Once()

    def valid_of(unit):
        base, _, at, _, _ = place_of(unit)
        return seg[0:1, base + at : base + at + HALF] >= 0

    def values_of(unit):
        base, left, _, _, _ = place_of(unit)
        cols = slice(2 * width + left, 2 * width + left + PAIR)
        return once.get_or(unit[:2], lambda: qkv[base : base + S, cols].T)

    def bias_of(unit):
        sequence, _, block = unit
        _, _, _, lo, hi = place_of(unit)

        def make():
            bias = mask_bias(WINDOWS[sequence][0], block, lo, hi)
            return jnp.concatenate([bias, bias], axis=1)

        return once.get_or(("bias", sequence, block), make)

    def raw_scores(unit):
        base, left, at, lo, hi = place_of(unit)
        values_of(unit)
        keys = qkv[base + lo : base + hi, width + left : width + left + PAIR]
        return nt(keys, split_pair(qkv[base + at : base + at + HALF, left : left + PAIR]))

    def softmax(unit, raw):
        sequence, pair, block = unit
        _, _, _, lo, hi = place_of(unit)
        scores = raw * (SCALE * LOG2E)
        cut = 0 if WINDOWS[sequence][0] else GLOBAL_LEN // 16 * 16 - lo
        tail = scores[cut:] + bias_of(unit)[cut:]
        scores = jnp.concatenate([scores[:cut], tail], axis=0) if cut else tail
        exponent = jnp.exp2(scores - jnp.max(scores, axis=0, keepdims=True))
        total = jnp.sum(exponent, axis=0, keepdims=True)
        valid = valid_of(unit)
        inverse = jnp.where(jnp.concatenate([valid, valid], axis=1), 1.0 / total, 0.0)
        probs = (exponent * inverse).astype(BF16)
        offset = prob_offset(pair, sequence, block)
        prob[offset : offset + hi - lo, :] = probs
        return probs

    def context(unit, probs):
        base, left, at, lo, hi = place_of(unit)
        values_t = values_of(unit)
        mixed = diagonal(nn(values_t, padded(probs, lo, hi)))
        own = values_t[:, at : at + HALF].astype(F32)
        ctx_t[left : left + PAIR, base + at : base + at + HALF] = jnp.where(
            valid_of(unit), mixed, own
        ).astype(BF16)

    yield from pipelined(units_of(width), DEPTH, [raw_scores, softmax, context])


def span(start, size):
    return pl.ds(start if isinstance(start, int) else pl.multiple_of(start, PAIR), size)


def attend_back(seg, qkv, prob, grad_context, grad_qkv, pairs, sequences, place_in):
    once = Once()
    width = qkv.shape[1] // 3
    per_step = PROB_ROWS * (width // PAIR)

    def rows_of(unit):
        sequence, slot, block = unit
        lo, hi = WINDOWS[sequence % 2][1][block]
        return sequence * S, block * HALF, lo, hi

    def pair_of(unit):
        return pairs[unit[1]]

    def columns(unit, part):
        return span(part * width + pair_of(unit) * PAIR, PAIR)

    def padding_of(unit):
        base = unit[0] * S

        def make():
            valid = (seg[0:1, base : base + S] >= 0).astype(jnp.int32)
            count = jnp.sum(valid, axis=1, keepdims=True)
            return lax.broadcasted_iota(jnp.int32, (S, PAIR), 0) >= count

        return once.get_or(("padding", unit[0]), make)

    def keys_of(unit):
        base = unit[0] * S
        return once.get_or(("keys", unit[:2]), lambda: qkv[base : base + S, columns(unit, 1)].T)

    def grads_of(unit):
        base, at, _, _ = rows_of(unit)
        rows = slice(base + at, base + at + HALF)
        return once.get_or(("grads", unit), lambda: split_pair(grad_context[rows, columns(unit, 0)]))

    def grad_probs(unit):
        base, _, lo, hi = rows_of(unit)
        keys_of(unit)
        return nt(qkv[base + lo : base + hi, columns(unit, 2)], grads_of(unit))

    def grad_scores(unit, grads):
        sequence, _, block = unit
        _, _, lo, hi = rows_of(unit)
        start = sequence // 2 * per_step + prob_offset(0, sequence % 2, block)
        pair = pair_of(unit)
        start = start + pair * PROB_ROWS if isinstance(pair, int) else pl.multiple_of(start + pair * PROB_ROWS, 16)
        probs_low = prob[pl.ds(start, hi - lo), :]
        probs = probs_low.astype(F32)
        product = probs * grads
        inner = jnp.sum(product, axis=0, keepdims=True)
        return (product - probs * inner).astype(BF16), probs_low

    def grad_rows(unit, given):
        grad_raw, probs_low = given
        base, at, lo, hi = rows_of(unit)
        pair = pair_of(unit)
        queries = split_pair(qkv[base + at : base + at + HALF, columns(unit, 0)])
        grad_values = padded(nn(probs_low, grads_of(unit)), lo, hi)
        grad_keys = padded(nn(grad_raw, queries), lo, hi)
        grad_queries = diagonal(nn(keys_of(unit), padded(grad_raw, lo, hi))) * SCALE
        grad_qkv[base + at : base + at + HALF, span(place_in(0, pair), PAIR)] = grad_queries.astype(BF16).T
        if unit[2] == 0:
            once["first", unit[:2]] = grad_values, grad_keys
            return
        other_values, other_keys = once["first", unit[:2]]
        own = jnp.where(padding_of(unit), grad_context[base : base + S, columns(unit, 0)].astype(F32), 0.0)
        grad_qkv[base : base + S, span(place_in(1, pair), PAIR)] = ((other_keys + grad_keys) * SCALE).astype(BF16)
        grad_qkv[base : base + S, span(place_in(2, pair), PAIR)] = (other_values + grad_values + own).astype(BF16)

    units = [(q, slot, block) for q in range(sequences) for slot in range(len(pairs)) for block in range(2)]
    for _ in pipelined(units, DEPTH, [grad_probs, grad_scores, grad_rows]):
        pass


def vector(vec, row, count=1):
    parts = [vec[0, row + i : row + i + 1, :] for i in range(count)]
    return parts[0] if count == 1 else jnp.concatenate(parts, axis=1)


def forward_qkv(x, weights, kept, before_weights=None):
    vec, w_qkv, _, _, _ = weights
    xhat1, r1, qkv, _ = kept
    width = x.shape[1]
    scaled, inverse = normalized(x[...].astype(F32))
    xhat1[...] = scaled.astype(BF16)
    r1[...] = inverse
    if before_weights is not None:
        before_weights()
    normed = (scaled * vector(vec, ATTN_GAIN) + vector(vec, ATTN_SHIFT)).astype(BF16)
    for part, bias in ((0, Q_BIAS), (1, None), (2, V_BIAS)):
        mixed = nn(normed, w_qkv[0, :, part * width : (part + 1) * width])
        if bias is not None:
            mixed = mixed + vector(vec, bias)
        qkv[:, part * width : (part + 1) * width] = mixed.astype(BF16)


def forward_mlp(x, weights, kept, y, between=None):
    vec, _, w_proj, w_fc1, w_fc2 = weights
    ctx_t, xhat2, r2, act, dgelu = kept
    width = x.shape[1]
    hidden = w_fc1.shape[2]
    after = x[...].astype(F32) + tn(ctx_t[...], w_proj[0]) + vector(vec, PROJ_BIAS)
    scaled, inverse = normalized(after)
    xhat2[...] = scaled.astype(BF16)
    r2[...] = inverse
    normed = (scaled * vector(vec, MLP_GAIN) + vector(vec, MLP_SHIFT)).astype(BF16)
    bias = vector(vec, FC1_BIAS, hidden // width)
    tops = list(range(0, hidden, FORWARD_CHUNK))

    def product(left):
        return nn(normed, w_fc1[0, :, left : left + FORWARD_CHUNK])

    coming = product(tops[0])
    for i, left in enumerate(tops):
        cols = slice(left, left + FORWARD_CHUNK)
        pre = coming + bias[:, cols]
        if i + 1 < len(tops):
            coming = product(tops[i + 1])
        below = 0.5 + 0.5 * lax.erf(pre * (0.5**0.5))
        density = jnp.exp2(pre * pre * (-0.5 * LOG2E)) * (1.0 / (2.0 * jnp.pi) ** 0.5)
        act[:, cols] = (pre * below).astype(BF16)
        dgelu[:, cols] = (below + pre * density).astype(BF16)
        if between is not None:
            between()
    y[...] = (after + vector(vec, FC2_BIAS) + nn(act[...], w_fc2[0])).astype(BF16)


def forward(x, seg, weights, kept, y, after_attention=None):
    forward_qkv(x, weights, kept[:4])
    for _ in attend(seg, kept[2], kept[3], kept[4], x.shape[1]):
        pass
    if after_attention is not None:
        after_attention()
    forward_mlp(x, weights, kept[4:], y)


def adder(sum_vec, width):
    def add(row, values):
        for i in range(values.shape[1] // width):
            at = (row + i) * 8
            sum_vec[at : at + 8, :] += column_sums(values[:, i * width : (i + 1) * width])

    return add


def backward_fc2(dout, act, sums):
    sum_fc2, sum_vec = sums[3:]
    top_grad = dout[...]
    adder(sum_vec, dout.shape[1])(FC2_BIAS, top_grad.astype(F32))
    sum_fc2[...] += nn(top_grad.T, act[...])


def backward_mlp(dout, weights, kept, sums, write, with_fc2=True):
    vec, _, w_proj, w_fc1, w_fc2 = weights
    ctx_t, xhat2, r2, act, dgelu = kept
    _, sum_proj, sum_fc1, _, sum_vec = sums
    rows, width = dout.shape
    hidden = w_fc1.shape[2]
    add = adder(sum_vec, width)
    top_grad = dout[...]
    top_wide = top_grad.astype(F32)
    if with_fc2:
        backward_fc2(dout, act, sums)
    scaled = xhat2[...].astype(F32)
    normed_t = (scaled * vector(vec, MLP_GAIN) + vector(vec, MLP_SHIFT)).astype(BF16).T
    grad_normed = jnp.zeros((rows, width), F32)
    column_parts = []
    for left in range(0, hidden, CHUNK):
        cols = slice(left, left + CHUNK)
        grad_pre = nt(top_grad, w_fc2[0, cols, :]) * dgelu[:, cols].astype(F32)
        column_parts.append(column_sums(grad_pre))
        grad_pre = grad_pre.astype(BF16)
        grad_normed = grad_normed + nt(grad_pre, w_fc1[0, :, cols])
        sum_fc1[:, cols] += nn(normed_t, grad_pre)
    columns = jnp.concatenate(column_parts, axis=1)
    for i in range(hidden // width):
        at = (FC1_BIAS + i) * 8
        sum_vec[at : at + 8, :] += columns[:, i * width : (i + 1) * width]
    add(MLP_GAIN, grad_normed * scaled)
    add(MLP_SHIFT, grad_normed)
    grad_after = top_wide + norm_back(scaled, r2[...], vector(vec, MLP_GAIN), grad_normed)
    add(PROJ_BIAS, grad_after)
    grad_branch = grad_after.astype(BF16)
    sum_proj[...] += nn(ctx_t[...], grad_branch)
    write(grad_after, nt(grad_branch, w_proj[0]).astype(BF16))


def backward_attn(grad_after, grad_context, seg, weights, kept, sums, grad_qkv, write, halfway=None):
    vec, w_qkv, _, _, _ = weights
    xhat1, r1, qkv, prob = kept
    sum_qkv, sum_vec = sums[0], sums[4]
    rows, width = grad_after.shape
    add = adder(sum_vec, width)
    attend_back(
        seg, qkv, prob, grad_context, grad_qkv, list(range(width // PAIR)), rows // S,
        lambda part, pair: part * width + pair * PAIR,
    )
    if halfway is not None:
        halfway()
    scaled = xhat1[...].astype(F32)
    normed_t = (scaled * vector(vec, ATTN_GAIN) + vector(vec, ATTN_SHIFT)).astype(BF16).T
    grad_normed = jnp.zeros((rows, width), F32)
    for part, row in ((0, Q_BIAS), (1, None), (2, V_BIAS)):
        cols = slice(part * width, (part + 1) * width)
        piece = grad_qkv[:, cols]
        if row is not None:
            add(row, piece.astype(F32))
        sum_qkv[:, cols] += nn(normed_t, piece)
        grad_normed = grad_normed + nt(piece, w_qkv[0, :, cols])
    add(ATTN_GAIN, grad_normed * scaled)
    add(ATTN_SHIFT, grad_normed)
    write(grad_after[...] + norm_back(scaled, r1[...], vector(vec, ATTN_GAIN), grad_normed))


def half_rows(share):
    return up16(share // 2)


def write_blocks(sums, members, blocks, out):
    sum_qkv, sum_proj, sum_fc1, sum_fc2, _ = sums
    width = sum_proj.shape[0]
    share = width // members
    size = half_rows(share)
    parts = sum_fc1.shape[1] // width

    def store(rows, member, block):
        at = (member * len(blocks) + blocks.index(block)) * size
        out[0, at : at + size, :] = rows[:size]
        out[1, at : at + size, :] = rows[share - size :]

    for block in blocks:
        if block < parts:
            whole = sum_fc1[:, block * width : (block + 1) * width]
        elif block < 2 * parts:
            chunk = block - parts
            whole = sum_fc2[:, chunk * width : (chunk + 1) * width].astype(BF16).T
            for place in range(members):
                row = chunk * members + place
                store(whole[place * share : (place + 1) * share], row // parts, parts + row % parts)
            continue
        elif block == 2 * parts:
            whole = sum_proj[...]
        else:
            part = block - 2 * parts - 1
            whole = sum_qkv[:, part * width : (part + 1) * width]
        whole = whole.astype(BF16)
        for member in range(members):
            store(whole[member * share : (member + 1) * share], member, block)


def write_block(whole, members, store):
    share = whole.shape[0] // members
    size = half_rows(share)
    for member in range(members):
        rows = whole[member * share : (member + 1) * share]
        store(0, member * size, rows[:size])
        store(1, member * size, rows[share - size :])


def vector_sums(sum_vec):
    return jnp.sum(sum_vec[...].reshape(VECTORS, 8, sum_vec.shape[1]), axis=1).astype(BF16)


def clear(refs):
    for ref in refs:
        ref[...] = jnp.zeros_like(ref)


def kept_shapes(steps, width, hidden):
    return (
        ((steps * STEP, width), BF16, (STEP, width), 0),
        ((steps * STEP, 1), F32, (STEP, 1), 0),
        ((steps * STEP, 3 * width), BF16, (STEP, 3 * width), 0),
        ((steps * PROB_ROWS * (width // PAIR), S), BF16, (PROB_ROWS * (width // PAIR), S), 0),
        ((width, steps * STEP), BF16, (width, STEP), 1),
        ((steps * STEP, width), BF16, (STEP, width), 0),
        ((steps * STEP, 1), F32, (STEP, 1), 0),
        ((steps * STEP, hidden), BF16, (STEP, hidden), 0),
        ((steps * STEP, hidden), BF16, (STEP, hidden), 0),
    )


def sum_scratch(width, hidden):
    return [
        pltpu.VMEM((width, 3 * width), F32),
        pltpu.VMEM((width, width), F32),
        pltpu.VMEM((width, hidden), F32),
        pltpu.VMEM((width, hidden), F32),
        pltpu.VMEM((8 * VECTORS, width), F32),
    ]


def place():
    return lax.axis_index("section"), lax.axis_index("group"), lax.axis_index("member")


def remote(src, dst, send, recv, device):
    return pltpu.make_async_remote_copy(
        src_ref=src, dst_ref=dst, send_sem=send, recv_sem=recv, device_id=device, device_id_type=MESH
    )


def greet(peers):
    barrier = pltpu.get_barrier_semaphore()
    for peer in peers:
        pl.semaphore_signal(barrier, inc=1, device_id=peer, device_id_type=MESH)
    pl.semaphore_wait(barrier, len(peers))


def near_peers(members, sections):
    section, group, member = place()
    return [
        (lax.rem(section + ds, 2), group, lax.rem(member + dm, members))
        for ds in range(2)
        for dm in range(members)
        if (ds or dm) and (sections or not (ds and dm))
    ]


def far_peers(groups):
    section, group, member = place()
    return [
        (lax.rem(section + ds, 2), lax.rem(group + dg, groups), member)
        for ds in range(2)
        for dg in range(1, groups)
    ]


def rows_at(index, count):
    return pl.ds(pl.multiple_of(index * count, 16), count)


class Near:
    def __init__(self, members, count, width):
        self.members, self.count, self.width = members, count, width

    def source_shape(self):
        return (2, self.members * self.count, self.width)

    def scratch(self):
        return [
            pltpu.VMEM((self.members * self.count, self.width), BF16),
            pltpu.VMEM((self.members - 1, self.count, self.width), BF16),
        ] + [pltpu.SemaphoreType.DMA((n,)) for n in (1, 1, self.members, self.members)]

    def bind(self, refs, source):
        self.got, self.from_members, *self.sems = refs
        self.source = source
        return self

    def section_copy(self):
        section, group, member = place()
        return remote(
            self.source.at[1 - section], self.got, self.sems[0].at[0], self.sems[1].at[0], (1 - section, group, member)
        )

    def member_copy(self, offset):
        section, group, member = place()
        to = lax.rem(member + offset, self.members)
        return remote(
            self.got.at[rows_at(to, self.count)],
            self.from_members.at[offset - 1],
            self.sems[2].at[offset],
            self.sems[3].at[offset],
            (section, group, to),
        )

    def start_section(self):
        self.section_copy().start()

    def start_members(self):
        self.section_copy().wait()
        own = self.source[lax.axis_index("section")].astype(F32)
        self.got[...] = (self.got[...].astype(F32) + own).astype(BF16)
        for offset in range(1, self.members):
            self.member_copy(offset).start()

    def finish(self, out):
        for offset in range(1, self.members):
            self.member_copy(offset).wait()
        total = self.got[rows_at(lax.axis_index("member"), self.count), :].astype(F32)
        for offset in range(1, self.members):
            total = total + self.from_members[offset - 1].astype(F32)
        out[: self.count, :] = total.astype(BF16)
        spare = out.shape[0] - self.count
        if spare:
            out[self.count :, :] = jnp.zeros((spare, self.width), BF16)


class Far:
    def __init__(self, target, groups, count, width):
        self.target, self.groups, self.width = target, groups, width
        self.part = up16(-(-count // groups))

    def total_shape(self):
        return (self.groups * self.part, self.width)

    def result_shape(self):
        return (2, self.groups, self.part, self.width)

    def scratch(self):
        return [
            pltpu.VMEM((self.groups - 1, self.part, self.width), BF16),
            pltpu.VMEM((self.part, self.width), BF16),
            pltpu.SemaphoreType.DMA,
        ] + [pltpu.SemaphoreType.DMA((n,)) for n in (self.groups,) * 4 + (1, 1)]

    def bind(self, refs, total, result):
        self.from_groups, self.piece, self.local, *self.sems = refs
        self.total, self.result_ref = total, result
        return self

    def group_copy(self, offset):
        section, group, member = place()
        to = lax.rem(group + offset, self.groups)
        return remote(
            self.total.at[rows_at(to, self.part)],
            self.from_groups.at[offset - 1],
            self.sems[0].at[offset],
            self.sems[1].at[offset],
            (section, to, member),
        )

    def gather_copy(self, offset):
        section, group, member = place()
        return remote(
            self.piece,
            self.result_ref.at[section, group],
            self.sems[2].at[offset],
            self.sems[3].at[offset],
            (section, lax.rem(group + offset, self.groups), member),
        )

    def gathered(self, offset):
        section, group, member = place()
        origin = lax.rem(group + self.groups - offset, self.groups)
        return remote(
            self.piece,
            self.result_ref.at[section, origin],
            self.sems[2].at[offset],
            self.sems[3].at[offset],
            (section, origin, member),
        )

    def keep_copy(self):
        section, group, _ = place()
        return pltpu.make_async_copy(self.piece, self.result_ref.at[section, group], self.local)

    def half_copy(self, half):
        section, group, member = place()
        return remote(
            self.result_ref.at[half],
            self.result_ref.at[half],
            self.sems[4].at[0],
            self.sems[5].at[0],
            (1 - section, group, member),
        )

    def start_groups(self):
        for offset in range(1, self.groups):
            self.group_copy(offset).start()

    def start_gather(self):
        section, group, member = place()
        for offset in range(1, self.groups):
            self.group_copy(offset).wait()
        total = self.total[rows_at(group, self.part), :].astype(F32)
        for offset in range(1, self.groups):
            total = total + self.from_groups[offset - 1].astype(F32)
        self.piece[...] = total.astype(BF16)
        for offset in range(1, self.groups):
            self.gather_copy(offset).start()
        self.keep_copy().start()

    def hand_over(self):
        section = lax.axis_index("section")
        for offset in range(1, self.groups):
            self.gather_copy(offset).wait_send()
            self.gathered(offset).wait_recv()
        self.keep_copy().wait()

        @pl.when(section != self.target)
        def _():
            self.half_copy(section).start()

    def finish(self):
        section = lax.axis_index("section")

        @pl.when(section != self.target)
        def _():
            self.half_copy(section).wait_send()

        @pl.when(section == self.target)
        def _():
            self.half_copy(1 - section).wait_recv()


class VectorSum:
    def __init__(self, groups, members, width):
        self.groups, self.members, self.width = groups, members, width

    def scratch(self):
        return [
            pltpu.VMEM((2 * self.members, VECTORS, self.width), BF16),
            pltpu.VMEM((self.groups, VECTORS, self.width), BF16),
            pltpu.VMEM((VECTORS, self.width), BF16),
            pltpu.VMEM((VECTORS, self.width), BF16),
        ] + [pltpu.SemaphoreType.DMA((n,)) for n in (2 * self.members,) * 2 + (self.groups,) * 2]

    def bind(self, refs):
        self.near, self.far, self.own, self.middle = refs[:4]
        self.sems = refs[4:]
        return self

    def near_copy(self, offset):
        section, group, member = place()
        ds, dm = divmod(offset, self.members)
        to = lax.rem(section + ds, 2), group, lax.rem(member + dm, self.members)
        return remote(
            self.own, self.near.at[section * self.members + member], self.sems[0].at[offset], self.sems[1].at[offset], to
        )

    def near_got(self, offset):
        section, group, member = place()
        ds, dm = divmod(offset, self.members)
        origin = lax.rem(section + ds, 2), lax.rem(member + self.members - dm, self.members)
        return remote(
            self.own,
            self.near.at[origin[0] * self.members + origin[1]],
            self.sems[0].at[offset],
            self.sems[1].at[offset],
            (origin[0], group, origin[1]),
        )

    def far_copy(self, offset):
        section, group, member = place()
        to = section, lax.rem(group + offset, self.groups), member
        return remote(self.middle, self.far.at[group], self.sems[2].at[offset], self.sems[3].at[offset], to)

    def far_got(self, offset):
        section, group, member = place()
        origin = lax.rem(group + self.groups - offset, self.groups)
        return remote(
            self.middle, self.far.at[origin], self.sems[2].at[offset], self.sems[3].at[offset], (section, origin, member)
        )

    def start(self, values):
        section, group, member = place()
        self.own[...] = values
        self.near[section * self.members + member] = values
        for offset in range(1, 2 * self.members):
            self.near_copy(offset).start()

    def start_far(self):
        for offset in range(1, 2 * self.members):
            self.near_copy(offset).wait_send()
            self.near_got(offset).wait_recv()
        total = jnp.zeros((VECTORS, self.width), F32)
        for index in range(2 * self.members):
            total = total + self.near[index].astype(F32)
        self.middle[...] = total.astype(BF16)
        self.far[lax.axis_index("group")] = total.astype(BF16)
        for offset in range(1, self.groups):
            self.far_copy(offset).start()

    def finish(self):
        for offset in range(1, self.groups):
            self.far_copy(offset).wait_send()
            self.far_got(offset).wait_recv()
        total = jnp.zeros((VECTORS, self.width), F32)
        for index in range(self.groups):
            total = total + self.far[index].astype(F32)
        return total


def take(refs, *counts):
    out, at = [], 0
    for count in counts:
        out.append(list(refs[at : at + count]))
        at += count
    assert at == len(refs)
    return out


def params(collective):
    return pltpu.CompilerParams(vmem_limit_bytes=62 * MIB, collective_id=collective, has_side_effects=True)


def cost(flops, moved):
    return pl.CostEstimate(flops=flops, bytes_accessed=moved * MIB, transcendentals=0)


def block_at(shape, axis, index):
    return pl.BlockSpec(shape, lambda i: tuple(index(i) if d == axis else 0 for d in range(len(shape))))


def fixed(shape):
    return pl.BlockSpec(shape, lambda i: (0,) * len(shape), pipeline_mode=pl.Buffered(1))


ANYWHERE = pl.BlockSpec(memory_space=pl.ANY)


def first_forward(tokens, seg, vectors, own, steps):
    width, hidden = tokens.shape[1], own[2].shape[2]
    shapes = kept_shapes(steps, width, hidden)
    held = [((2, VECTORS, width), F32)] + [((2,) + w.shape[1:], w.dtype) for w in own]
    count = len(own)

    def body(x, seg, *refs):
        vectors_in, own, (y,), kept, weights, held, sems, (x_held, ctx_held) = take(
            refs, len(vectors), count, 1, len(shapes), count + 1, count + 1, 5, 2
        )
        load, send, recv, out, _ = sems
        step = pl.program_id(0)
        section, group, member = place()
        partner = (1 - section, group, member)
        order = list(range(count + 1))

        def own_load(i):
            return pltpu.make_async_copy(own[i - 1].at[0], held[i].at[section], load.at[i])

        def push(i, whose):
            source = own[i - 1].at[0] if i else held[0].at[whose]
            return remote(source, held[i].at[whose], send.at[i], recv.at[i], partner)

        def layer_zero(which):
            @pl.when(section == 0)
            def _():
                for i in which:
                    if i:
                        own_load(i).wait()

            @pl.when(section == 1)
            def _():
                for i in which:
                    push(i, 1 - section).wait_recv()

        def store(i):
            return pltpu.make_async_copy(held[i], weights[i], out.at[i])

        @pl.when(step == 0)
        def _():
            for i in order[1:]:
                own_load(i).start()
            row = 0
            for vector_in in vectors_in:
                for part in range(vector_in.shape[1] // width):
                    held[0][section, row : row + 1, :] = vector_in[:, part * width : (part + 1) * width]
                    row += 1
            held[0][section, row:, :] = jnp.zeros((VECTORS - row, width), F32)
            greet([partner])
            for i in order:
                push(i, section).start()

        now, before = lax.rem(step, 2), lax.rem(step + 1, 2)
        ctx_out, *mlp_kept = kept[4:]

        def before_weights():
            @pl.when(step == 0)
            def _():
                layer_zero(order[:2])

        def start(hook=None):
            x_held[now] = x[...]
            forward_qkv(x, held, kept[:4], hook)
            return attend(seg, kept[2], kept[3], ctx_held.at[now], width)

        def end(between=None):
            ctx_out[...] = ctx_held[before]
            forward_mlp(x_held.at[before], held, [ctx_held.at[before]] + mlp_kept, y, between)

        @pl.when(step < 2)
        def _():
            for _ in start(before_weights):
                pass

        @pl.when(step == 1)
        def _():
            layer_zero(order[2:])

        @pl.when(jnp.logical_or(step == 1, step == steps))
        def _():
            end()

        @pl.when(jnp.logical_and(step > 1, step < steps))
        def _():
            parts = start()

            def between():
                for _ in range(INTERLEAVED):
                    next(parts, None)

            end(between)
            for _ in parts:
                pass

        @pl.when(step == 2)
        def _():
            @pl.when(section == 0)
            def _():
                for i in order:
                    push(i, 1 - section).wait_recv()

            @pl.when(section == 1)
            def _():
                for i in order[1:]:
                    own_load(i).wait()

            for i in order:
                store(i).start()

        @pl.when(step == steps)
        def _():
            for i in order:
                store(i).wait()
                push(i, section).wait_send()

    def first(i):
        return jnp.minimum(i, steps - 1)

    def then(i):
        return jnp.maximum(i - 1, 0)

    def mine(i):
        return lax.axis_index("section") * steps + first(i)

    return pl.pallas_call(
        body,
        grid=(steps + 1,),
        in_specs=[block_at((STEP, width), 0, mine), block_at((1, STEP), 1, mine)]
        + [fixed(v.shape) for v in vectors]
        + [ANYWHERE] * count,
        out_specs=[block_at((STEP, width), 0, then)]
        + [block_at(block, axis, first) for _, _, block, axis in shapes[:4]]
        + [block_at(block, axis, then) for _, _, block, axis in shapes[4:]]
        + [ANYWHERE] * (count + 1),
        out_shape=[jax.ShapeDtypeStruct((steps * STEP, width), BF16)]
        + [jax.ShapeDtypeStruct(shape, dtype) for shape, dtype, _, _ in shapes]
        + [jax.ShapeDtypeStruct(shape, dtype) for shape, dtype in held],
        scratch_shapes=[pltpu.VMEM(shape, dtype) for shape, dtype in held]
        + [pltpu.SemaphoreType.DMA((count + 1,))] * 5
        + [pltpu.VMEM((2, STEP, width), BF16), pltpu.VMEM((2, width, STEP), BF16)],
        compiler_params=params(0),
        cost_estimate=cost(steps * STEP * 4000000, 40),
        name="forward_first",
    )(tokens, seg, *vectors, *own)


def block_lists(parts):
    fc1, fc2, proj = list(range(parts)), list(range(parts, 2 * parts)), 2 * parts
    qkv = [proj + 1, proj + 2, proj + 3]
    upper = (fc2 + fc1[: parts // 2], fc1[parts // 2 :] + [proj] + qkv)
    lower = (fc2, fc1 + [proj])
    return upper, lower


def second_layer(x, seg, cotangent, weights, steps, groups, members):
    width, hidden = x.shape[1], weights[3].shape[2]
    shapes = kept_shapes(steps, width, hidden)
    size = half_rows(width // members)
    early, late = block_lists(hidden // width)[0]
    near = Near(members, len(early) * size, width)
    far = Far(1, groups, len(early) * size, width)
    late_shape = Near(members, len(late) * size, width).source_shape()

    def body(x, seg, cot, vec, w_qkv, w_proj, w_fc1, w_fc2, *refs):
        outs, sums, attn_kept, mlp_kept, rest, sems, later, near_refs = take(
            refs, 6, 5, 4, 5, 6, 3, 3, len(near.scratch())
        )
        y_own, y_got, g, late_out, total_out, vec_out = outs
        grad_after, grad_context, grad_qkv, y, y_send, early_out = rest
        send, recv, load = sems
        near.bind(near_refs, early_out)
        loads = [
            pltpu.make_async_copy(w.at[pl.ds(1, 1)], held, load.at[i])
            for i, (w, held) in enumerate(zip((w_proj, w_fc1, w_fc2), later))
        ]
        weights = (vec, w_qkv, *later)
        step = pl.program_id(0)
        section, group, member = place()

        def y_copy(index):
            return remote(
                y_send.at[index], y_got.at[rows_at(index, STEP)], send.at[index], recv.at[index], (1 - section, group, member)
            )

        @pl.when(step == 0)
        def _():
            for copy in loads:
                copy.start()
            clear(sums)
            greet(near_peers(members, False))

        @pl.when(step < steps)
        def _():
            def after_attention():
                @pl.when(step == 0)
                def _():
                    for copy in loads:
                        copy.wait()

            forward(x, seg, weights, [ref.at[step] for ref in attn_kept] + mlp_kept, y, after_attention)
            y_own[...] = jnp.where(section == 0, x[...], y[...])
            y_send[step] = jnp.where(section == 0, y[...], x[...])
            y_copy(step).start()

            def write(after, context):
                grad_after[step] = after
                grad_context[step] = context

            backward_mlp(cot, weights, mlp_kept, sums, write)

        @pl.when(step == steps - 1)
        def _():
            write_blocks(sums, members, early, early_out)
            near.start_section()

        @pl.when(step >= steps)
        def _():
            index = step - steps

            def write(values):
                g[...] = values.astype(BF16)

            def halfway():
                @pl.when(step == steps)
                def _():
                    near.start_members()

            backward_attn(
                grad_after.at[index], grad_context.at[index], seg, weights,
                [ref.at[index] for ref in attn_kept], sums, grad_qkv, write, halfway,
            )

        @pl.when(step == 2 * steps - 1)
        def _():
            write_blocks(sums, members, late, late_out)
            vec_out[...] = vector_sums(sums[4])
            for index in range(steps):
                y_copy(index).wait()
            near.finish(total_out)

    def mine(index):
        return lambda i: lax.axis_index("section") * steps + index(i)

    def first(i):
        return jnp.minimum(i, steps - 1)

    def then(i):
        return jnp.maximum(i - steps, 0)

    rows = jax.ShapeDtypeStruct((steps * STEP, width), BF16)
    fixed_outs = [late_shape, far.total_shape(), (VECTORS, width)]
    return pl.pallas_call(
        body,
        grid=(2 * steps,),
        in_specs=[
            block_at((STEP, width), 0, first),
            block_at((1, STEP), 1, mine(lambda i: lax.rem(i, steps))),
            block_at((STEP, width), 0, mine(first)),
        ]
        + [
            pl.BlockSpec((1,) + w.shape[1:], lambda i: (1, 0, 0), pipeline_mode=pl.Buffered(1))
            for w in weights[:2]
        ]
        + [ANYWHERE] * 3,
        out_specs=[block_at((STEP, width), 0, first), ANYWHERE, block_at((STEP, width), 0, then)]
        + [fixed(shape) for shape in fixed_outs],
        out_shape=[rows] * 3 + [jax.ShapeDtypeStruct(shape, BF16) for shape in fixed_outs],
        scratch_shapes=sum_scratch(width, hidden)
        + [pltpu.VMEM((steps,) + block, dtype) for _, dtype, block, _ in shapes[:4]]
        + [pltpu.VMEM(block, dtype) for _, dtype, block, _ in shapes[4:]]
        + [
            pltpu.VMEM((steps, STEP, width), F32),
            pltpu.VMEM((steps, STEP, width), BF16),
            pltpu.VMEM((STEP, 3 * width), BF16),
            pltpu.VMEM((STEP, width), BF16),
            pltpu.VMEM((steps, STEP, width), BF16),
            pltpu.VMEM(near.source_shape(), BF16),
        ]
        + [pltpu.SemaphoreType.DMA((steps,))] * 2
        + [pltpu.SemaphoreType.DMA((3,))]
        + [pltpu.VMEM((1,) + w.shape[1:], w.dtype) for w in weights[2:]]
        + near.scratch(),
        compiler_params=params(1),
        cost_estimate=cost(steps * STEP * 12000000, 20),
        name="second_layer",
    )(x, seg, cotangent, *weights)


def first_backward(seg, dout, late1, total1, vec1, kept, weights, steps, groups, members):
    width, hidden = dout.shape[1], weights[3].shape[2]
    shapes = kept_shapes(steps, width, hidden)
    size = half_rows(width // members)
    pairs = width // PAIR
    rows = steps * STEP
    (upper_early, upper_late), lower = block_lists(hidden // width)
    counts = [len(blocks) * size for blocks in (upper_early, upper_late) + lower] + [size] * pairs
    fars = [Far(1 if i < 2 else 0, groups, count, width) for i, count in enumerate(counts)]
    nears = [Near(members, count, width) for count in counts[1:]]
    vector_plans = [VectorSum(groups, members, width) for _ in range(2)]
    plans = fars + nears + vector_plans
    starts = [0, steps, 2 * steps, 2 * steps + pairs, 3 * steps + pairs]
    last = starts[4] - 1

    def body(seg, dout, act, ctx_t, xhat2, r2, dgelu, vec, late1, total1, vec1, *refs):
        attn_in, weights_in, (g_own, g_got), results, vec_outs, *refs = take(
            refs, 4, 4, 2, len(fars), 2, len(refs) - 12 - len(fars)
        )
        sums, rest, attn_kept, held, sources, totals, sems, *bound = take(
            refs[0], 4, 8, 4, 4, 3, len(fars) - 1, 4, *[len(plan.scratch()) for plan in plans]
        )
        grad_after, grad_context, grad_qkv, g_send, scaled_t, paired, gain_part, shift_part = rest
        send, recv, load, load_attn = sems
        take_fars, take_nears = bound[: len(fars)], bound[len(fars) : len(fars) + len(nears)]
        for plan, plan_refs, total, result in zip(fars, take_fars, [total1] + totals, results):
            plan.bind(plan_refs, total, result)
        pair_sources = [sources[2].at[pair] for pair in range(pairs)]
        for plan, plan_refs, source in zip(nears, take_nears, [late1] + sources[:2] + pair_sources):
            plan.bind(plan_refs, source)
        for plan, plan_refs in zip(vector_plans, bound[len(fars) + len(nears) :]):
            plan.bind(plan_refs)
        far_a, far_b, far_fc2, far_fc1, *far_pairs = fars
        near_b, near_fc2, near_fc1, *near_pairs = nears
        total_b, total_fc2, total_fc1, *total_pairs = totals
        upper_vec, lower_vec = vector_plans
        sum_proj, sum_fc1, sum_fc2, sum_vec = sums
        all_sums = (None, sum_proj, sum_fc1, sum_fc2, sum_vec)
        w_qkv, w_proj, w_fc1, w_fc2 = held
        weights = (vec, w_qkv, w_proj, w_fc1, w_fc2)
        xhat1, r1, qkv, prob = attn_kept
        step = pl.program_id(0)
        section, group, member = place()
        loads = [pltpu.make_async_copy(a.at[pl.ds(0, 1)], b, load.at[i]) for i, (a, b) in enumerate(zip(weights_in, held))]
        loads_attn = [pltpu.make_async_copy(a, b, load_attn.at[i]) for i, (a, b) in enumerate(zip(attn_in, attn_kept))]

        def g_copy(index):
            return remote(
                g_send.at[index], g_got.at[rows_at(index, STEP)], send.at[index], recv.at[index], (1 - section, group, member)
            )

        def at(number, offset=0):
            return pl.when(step == starts[number] + offset)

        def phase(number):
            return pl.when(jnp.logical_and(step >= starts[number], step < starts[number + 1]))

        @at(0)
        def _():
            for copy in loads + loads_attn:
                copy.start()
            clear(sums)
            greet(near_peers(members, True) + far_peers(groups))
            near_b.start_section()
            far_a.start_groups()
            upper_vec.start(vec1[...])

        @at(0, steps // 2)
        def _():
            near_b.start_members()

        @phase(0)
        def _():
            g_send[step] = dout[...]
            backward_fc2(dout, act, all_sums)

        @at(1, -1)
        def _():
            write_blocks(all_sums, members, lower[0], near_fc2.source)
            near_fc2.start_section()

        @at(1)
        def _():
            for copy in loads:
                copy.wait()

        @at(1, 1)
        def _():
            near_fc2.start_members()
            far_a.start_gather()
            upper_vec.start_far()

        @at(2, -1)
        def _():
            near_b.finish(total_b)
            far_b.start_groups()
            vec_outs[0][...] = upper_vec.finish()

        @phase(1)
        def _():
            index = step - starts[1]

            def write(after, context):
                grad_after[index] = after
                grad_context[rows_at(index, STEP), :] = context

            backward_mlp(g_send.at[index], weights, (ctx_t, xhat2, r2, None, dgelu), all_sums, write, False)

        @at(2, -1)
        def _():
            write_blocks(all_sums, members, lower[1], near_fc1.source)
            near_fc1.start_section()

        @at(2)
        def _():
            for copy in loads_attn:
                copy.wait()
            for chunk in range(steps):
                here = slice(chunk * STEP, (chunk + 1) * STEP)
                scaled_t[:width, here] = xhat1[here, :].T
            scaled_t[width:, :] = jnp.ones((16, rows), BF16)
            for pair in range(pairs):
                for part in range(3):
                    left = (3 * pair + part) * PAIR
                    source = part * width + pair * PAIR
                    paired[:, left : left + PAIR] = w_qkv[0, :, source : source + PAIR]
            gain_part[...] = jnp.zeros_like(gain_part)
            shift_part[...] = jnp.zeros_like(shift_part)

        @at(2, 1)
        def _():
            near_fc2.finish(total_fc2)
            far_fc2.start_groups()
            far_b.start_gather()

        @at(2, 2)
        def _():
            near_pairs[0].start_members()

        @phase(2)
        def _():
            pair = step - starts[2]
            attend_back(
                seg, qkv, prob, grad_context, grad_qkv, [pair], 2 * steps,
                lambda part, pair: pair * width + part * PAIR,
            )

            @at(2)
            def _():
                near_fc1.start_members()

            here = span(pair * width, width)
            product = nn(scaled_t[...], grad_qkv[:, here])
            scaled_sum, columns = product[:width], product[width : width + 1]
            weight = paired[:, here].astype(F32)
            gained, shifted = scaled_sum * weight, columns * weight
            for part in range(3):
                cols = slice(part * PAIR, (part + 1) * PAIR)
                gain_part[...] += gained[:, cols]
                shift_part[...] += shifted[:, cols]
            sum_vec[Q_BIAS * 8 : Q_BIAS * 8 + 1, span(pair * PAIR, PAIR)] = columns[:, :PAIR]
            sum_vec[V_BIAS * 8 : V_BIAS * 8 + 1, span(pair * PAIR, PAIR)] = columns[:, 2 * PAIR :]
            gain, shift = [
                jnp.broadcast_to(vector(vec, row), (8, width)).T[:, :1] for row in (ATTN_GAIN, ATTN_SHIFT)
            ]
            whole = (scaled_sum * gain + shift * columns).astype(BF16)

            def store(half, top, rows):
                sources[2][pair, half, top : top + size, :] = rows

            write_block(whole, members, store)

        for pair in range(pairs):

            @at(2, pair)
            def _(pair=pair):
                near_pairs[pair].start_section()

        @at(3)
        def _():
            sum_vec[ATTN_GAIN * 8 : ATTN_GAIN * 8 + 1, :] = jnp.sum(gain_part[...].T, axis=0, keepdims=True)
            sum_vec[ATTN_SHIFT * 8 : ATTN_SHIFT * 8 + 1, :] = jnp.sum(shift_part[...].T, axis=0, keepdims=True)
            lower_vec.start(vector_sums(sum_vec))
            near_pairs[1].start_members()
            near_fc1.finish(total_fc1)
            far_fc1.start_groups()
            far_fc2.start_gather()

        @at(3, 1)
        def _():
            near_pairs[2].start_members()
            far_a.hand_over()

        @at(3, 2)
        def _():
            near_pairs[0].finish(total_pairs[0])
            far_pairs[0].start_groups()
            lower_vec.start_far()

        @at(3, 3)
        def _():
            near_pairs[1].finish(total_pairs[1])
            far_pairs[1].start_groups()
            far_b.hand_over()

        @phase(3)
        def _():
            index = step - starts[3]
            here = rows_at(index, STEP)
            grad_normed = nt(grad_qkv[here, :], paired[...])
            scaled = xhat1[here, :].astype(F32)
            grads = grad_after[index] + norm_back(scaled, r1[here, :], vector(vec, ATTN_GAIN), grad_normed)
            low = grads.astype(BF16)
            upper_rows = g_send[index]
            g_own[...] = jnp.where(section == 0, low, upper_rows)
            g_send[index] = jnp.where(section == 0, upper_rows, low)
            g_copy(index).start()

        @at(4, -1)
        def _():
            for pair in range(2, pairs):
                near_pairs[pair].finish(total_pairs[pair])
                far_pairs[pair].start_groups()
            far_fc1.start_gather()
            vec_outs[1][...] = lower_vec.finish()
            for far in far_pairs:
                far.start_gather()
            for index in range(steps):
                g_copy(index).wait()
            for far in fars[2:]:
                far.hand_over()
            for far in fars:
                far.finish()

    def clipped(number):
        return lambda i: jnp.clip(i - starts[number], 0, steps - 1)

    low_rows = jax.ShapeDtypeStruct((rows, width), BF16)
    vec_shape = (VECTORS, width)
    xhat1, r1, qkv, prob, ctx_t, xhat2, r2, act, dgelu = kept
    attn_in = (xhat1, r1, qkv, prob)
    return pl.pallas_call(
        body,
        grid=(starts[4],),
        in_specs=[
            block_at((1, rows), 1, lambda i: lax.axis_index("section")),
            block_at((STEP, width), 0, clipped(0)),
            block_at((STEP, hidden), 0, clipped(0)),
            block_at((width, STEP), 1, clipped(1)),
            block_at((STEP, width), 0, clipped(1)),
            block_at((STEP, 1), 0, clipped(1)),
            block_at((STEP, hidden), 0, clipped(1)),
            fixed((1, VECTORS, width)),
            fixed(late1.shape),
            fixed(total1.shape),
            fixed(vec_shape),
        ]
        + [ANYWHERE] * 8,
        out_specs=[block_at((STEP, width), 0, clipped(3)), ANYWHERE]
        + [ANYWHERE] * len(fars)
        + [fixed(vec_shape)] * 2,
        out_shape=[low_rows] * 2
        + [jax.ShapeDtypeStruct(far.result_shape(), BF16) for far in fars]
        + [jax.ShapeDtypeStruct(vec_shape, F32)] * 2,
        scratch_shapes=sum_scratch(width, hidden)[1:]
        + [
            pltpu.VMEM((steps, STEP, width), F32),
            pltpu.VMEM((rows, width), BF16),
            pltpu.VMEM((rows, 3 * width), BF16),
            pltpu.VMEM((steps, STEP, width), BF16),
            pltpu.VMEM((width + 16, rows), BF16),
            pltpu.VMEM((width, 3 * width), BF16),
            pltpu.VMEM((width, PAIR), F32),
            pltpu.VMEM((width, PAIR), F32),
        ]
        + [pltpu.VMEM(a.shape, a.dtype) for a in attn_in]
        + [pltpu.VMEM((1,) + w.shape[1:], w.dtype) for w in weights[1:]]
        + [pltpu.VMEM(near.source_shape(), BF16) for near in nears[1:3]]
        + [pltpu.VMEM((pairs,) + nears[3].source_shape(), BF16)]
        + [pltpu.VMEM(far.total_shape(), BF16) for far in fars[1:]]
        + [pltpu.SemaphoreType.DMA((steps,))] * 2
        + [pltpu.SemaphoreType.DMA((4,))] * 2
        + [item for plan in plans for item in plan.scratch()],
        compiler_params=params(2),
        cost_estimate=cost(rows * 8000000, 40),
        name="backward_first",
    )(seg, dout, act, ctx_t, xhat2, r2, dgelu, weights[0], late1, total1, vec1, *attn_in, *weights[1:])


def finish(y_own, y_got, g_own, g_got, results, vec_sums, width, hidden, steps, members):
    parts = hidden // width
    pairs = width // PAIR
    share = width // members
    size = half_rows(share)
    upper, lower = block_lists(parts)
    results = [result.reshape(2, -1, width) for result in results]
    tall = 2 * STEP
    steps = steps // 2

    def body(y_own, y_got, g_own, g_got, *refs):
        results, (upper_vec, lower_vec), (acts, grads), outs = take(refs, len(results_in), 2, 2, 12)
        a_gain, a_shift, d_qkv, d_qv, d_proj, b_proj, m_gain, m_shift, d_fc1, b_fc1, d_fc2, b_fc2 = outs
        step = pl.program_id(0)
        section, member = lax.axis_index("section"), lax.axis_index("member")
        mine = step // steps == section
        acts[0] = jnp.where(mine, y_own[...], y_got[...])
        grads[0] = jnp.where(mine, g_own[...], g_got[...]).astype(F32)

        def rows_of(lists, results, block, half):
            for blocks, result in zip(lists, results):
                if block in blocks:
                    top = blocks.index(block) * size
                    return result[half, top : top + size, :].astype(F32)
            raise KeyError(block)

        def write(lists, results, vec_sum, paired):
            for half in range(2):
                top = half * (share - size)
                for block in range(2 * parts + 1):
                    rows = rows_of(lists, results, block, half)
                    if block < parts:
                        d_fc1[0, top : top + size, block * width : (block + 1) * width] = rows
                    elif block < 2 * parts:
                        base = (block - parts) * share + top
                        d_fc2[0, base : base + size, :] = rows
                    else:
                        d_proj[0, top : top + size, :] = rows
                for index in range(3):
                    if paired:
                        rows = results[len(lists) + index][half, :size, :].astype(F32)
                        for part in range(3):
                            left = part * width + index * PAIR
                            d_qkv[0, top : top + size, left : left + PAIR] = rows[:, part * PAIR : (part + 1) * PAIR]
                    else:
                        rows = rows_of(lists, results, 2 * parts + 1 + index, half)
                        d_qkv[0, top : top + size, index * width : (index + 1) * width] = rows

            def put(out, row, count=1):
                flat = jnp.concatenate([vec_sum[row + i : row + i + 1, :] for i in range(count)], axis=1)
                length = count * width // members
                value = flat[:, :length]
                for m in range(1, members):
                    value = jnp.where(member == m, flat[:, m * length : (m + 1) * length], value)
                out[...] = value

            put(a_gain, ATTN_GAIN)
            put(a_shift, ATTN_SHIFT)
            put(d_qv, Q_BIAS, 2)
            put(b_proj, PROJ_BIAS)
            put(m_gain, MLP_GAIN)
            put(m_shift, MLP_SHIFT)
            put(b_fc1, FC1_BIAS, parts)
            put(b_fc2, FC2_BIAS)

        @pl.when(jnp.logical_and(step == 0, section == 0))
        def _():
            write(lower, results[2:], lower_vec, True)

        @pl.when(jnp.logical_and(step == 0, section == 1))
        def _():
            write(upper, results[:2], upper_vec, False)

    def whole(shape):
        return pl.BlockSpec(shape, lambda i: (0,) * len(shape))

    def rows_from(section):
        return block_at((tall, width), 0, lambda i: jnp.clip(i - section() * steps, 0, steps - 1))

    own = rows_from(lambda: lax.axis_index("section"))
    got = rows_from(lambda: 1 - lax.axis_index("section"))
    total = 2 * steps * tall
    smalls = [
        (1, share), (1, share), (1, share, 3 * width), (1, 2 * share), (1, share, width), (1, share), (1, share),
        (1, share), (1, share, hidden), (1, hidden // members), (1, hidden // members, width), (1, share),
    ]
    rows_spec = pl.BlockSpec((1, tall, width), lambda i: (0, i, 0))
    results_in = results
    return pl.pallas_call(
        body,
        grid=(2 * steps,),
        in_specs=[own, got, own, got] + [whole(x.shape) for x in results + list(vec_sums)],
        out_specs=[rows_spec, rows_spec] + [whole(shape) for shape in smalls],
        out_shape=[
            jax.ShapeDtypeStruct((1, total, width), BF16),
            jax.ShapeDtypeStruct((1, total, width), F32),
        ]
        + [jax.ShapeDtypeStruct(shape, F32) for shape in smalls],
        compiler_params=pltpu.CompilerParams(vmem_limit_bytes=62 * MIB),
        cost_estimate=cost(0, 16),
        name="finish",
    )(y_own, y_got, g_own, g_got, *results, *vec_sums)


def per_device(
    tokens,
    segment,
    cotangent,
    attn_gain,
    attn_shift,
    qkv_weight,
    qv_bias,
    proj_weight,
    proj_bias,
    mlp_gain,
    mlp_shift,
    fc1_weight,
    fc1_bias,
    fc2_weight,
    fc2_bias,
):
    groups, members = lax.axis_size("group"), lax.axis_size("member")
    rows, width = tokens.shape
    hidden = fc1_weight.shape[2]
    steps = rows // 2 // STEP
    seg = segment.reshape(1, rows)
    vectors = (attn_gain, attn_shift, qv_bias, proj_bias, mlp_gain, mlp_shift, fc2_bias, fc1_bias)
    y0, *rest = first_forward(
        tokens, seg, vectors, [qkv_weight, proj_weight, fc1_weight, fc2_weight], steps
    )
    kept, weights = rest[:9], rest[9:]
    y_own, y_got, g1, late1, total1, vec1 = second_layer(y0, seg, cotangent, weights, steps, groups, members)
    g_own, g_got, *grads = first_backward(seg, g1, late1, total1, vec1, kept, weights, steps, groups, members)
    return tuple(finish(y_own, y_got, g_own, g_got, grads[:-2], grads[-2:], width, hidden, steps, members))


def solution(mesh):
    row = P("section", None)
    mat = P("section", None, None)
    tokens = P(("group", "member"), None)
    split = P("section", "member")
    split_mat = P("section", "member", None)
    stacked = P("section", ("group", "member"), None)
    return jax.shard_map(
        per_device,
        mesh=mesh,
        in_specs=(
            tokens, P(("group", "member")), tokens,
            row, row, mat, row, mat, row, row, row, mat, row, mat, row,
        ),
        out_specs=(
            stacked, stacked,
            split, split, split_mat, split, split_mat, split, split, split, split_mat, split, split_mat, split,
        ),
        check_vma=False,
    )
```
